256 devices in a mesh: member: 4 (over x), tile: 32 (over y_hi, z, core), grp: 2 (over y_lo).
Axes of the slice: x: 4, y: 4 (y_hi: 2, y_lo: 2; y = y_hi * 2 + y_lo), z: 8, core: 2. Of those that a mesh axis runs over, the one named last changes fastest.
Arguments:
- members: float32 [80, 1024, 1024], P(('member', 'grp'), 'tile'), may hold values from -6 to 6
- courant_x: float32 [1024, 1024], P('tile'), may hold values from -0.48 to 0.48
- courant_y: float32 [1024, 1024], P('tile'), may hold values from -0.48 to 0.48
- obs_cell: int32 [32, 8, 1024], P('tile', ('member', 'grp')), may hold values from 0 to 4095
- innovation: float32 [32, 8, 1024], P('tile', ('member', 'grp')), may hold values from -6 to 6
- obs_weight: float32 [32, 8, 1024], P('tile', ('member', 'grp')), may hold values from 0.5 to 3
- stencil_offsets: int32 [9, 2], replicated, may hold values from -2 to 2, as said below
- stencil_weights: float32 [9], replicated, may hold values from 0.2 to 1
Outputs:
- analysis: float32 [80, 1024, 1024], P(('member', 'grp'), 'tile')
- increment: float32 [1024, 1024], P('tile', ('member', 'grp'))
The draws below stay inside these ranges and needn't reach their ends.
Inputs may be any that keep to these rules, and one draw needn't show every extreme that they name: `stencil_offsets`: each row is a stencil entry's offsets along rows and columns; some entry reaches 2 cells along rows and some along columns. `obs_cell`: cells of a block are numbered row by row, 128 to a row.
All inputs are finite; a program needn't handle non-finite values.
Results may differ from the reference program's by a relative error of at most 0.0001.
Values sent between devices are 32-bit elements; how exact they have to be, the bound alone decides.
No kernel may reach another device: no remote copies, remote signals or barrier semaphores. Data moves between devices by JAX's collectives and lax.ppermute only.
A program may use at most 128 MiB of HBM per device.

```python
import math
import jax
import jax.numpy as jnp
from jax import lax

CX = 32
CY = 128
RADIUS = 2
STENCIL_ENTRIES = 9
FSTEPS = 3
GSTEPS = 2
ENS = 80
NX = 1024
NY = 1024
OBS_BLK = 1024
N_MEMBER = 4
N_TILE = 32
N_GRP = 2


def draw_stencil_offsets(key, part):
    first_key, second_key = jax.random.split(jax.random.fold_in(key, 17), 2)
    offsets = jax.random.randint(first_key, (STENCIL_ENTRIES, 2), -RADIUS, RADIUS + 1)
    signs = 2 * jax.random.randint(second_key, (2,), 0, 2) - 1
    offsets = offsets.at[0, 0].set(signs[0] * RADIUS)
    offsets = offsets.at[1, 1].set(signs[1] * RADIUS)
    return offsets.astype(jnp.int32)


def set_ends(values, stream_key, smallest, high):
    longest = values.shape.index(max(values.shape))
    spots = []
    for shift in (0, 1):
        where = [jax.random.randint(jax.random.fold_in(stream_key, axis), (), 0, length) for axis, length in enumerate(values.shape)]
        where[longest] = (where[longest] + shift) % values.shape[longest]
        spots.append(tuple(where))
    return values.at[spots[0]].set(smallest).at[spots[1]].set(high)


def levels(rng, dims, pieces, smallest, largest):
    factor_of, own = 1.0, jax.random.fold_in(rng, 6)
    for axis_at, blocks in pieces:
        steps = jnp.exp(jax.random.uniform(jax.random.fold_in(own, axis_at), (blocks,), jnp.float32, smallest / len(pieces), largest / len(pieces)))
        factor_of = factor_of * jnp.repeat(steps, dims[axis_at] // blocks).reshape([-1 if axis == axis_at else 1 for axis in range(len(dims))])
    return factor_of


def centred(own_key, dims, scale, reach, cuts=(), dtype=jnp.bfloat16):
    array = jax.random.normal(own_key, dims, jnp.float32) * scale
    if len(cuts) > 0:
        array = levels(own_key, dims, cuts, -0.22, 0.18) * array
    return jnp.clip(array, min=-reach, max=reach).astype(dtype)


def setup_inputs(seed: int = 0) -> dict:
    key_list = jax.random.split(jax.random.key(seed), 9)
    members = centred(key_list[0], (ENS, NX, NY), 1.0, 6.0, ((0, 8), (1, 32)), jnp.float32)
    courant_x = jnp.clip(jax.random.uniform(key_list[1], (NX, NY), jnp.float32, -0.48, 0.48) * levels(key_list[1], (NX, NY), ((0, 32),), -0.4, 0.0), -0.48, 0.48)
    courant_y = jnp.clip(jax.random.uniform(key_list[2], (NX, NY), jnp.float32, -0.48, 0.48) * levels(key_list[2], (NX, NY), ((0, 32),), -0.4, 0.0), -0.48, 0.48)
    obs_cell = set_ends(jax.random.randint(key_list[3], (N_TILE, N_MEMBER * N_GRP, OBS_BLK), 0, CX * CY), jax.random.fold_in(key_list[3], 1), 0, (CX * CY) - 1).astype(jnp.int32)
    innovation = centred(key_list[4], (N_TILE, N_MEMBER * N_GRP, OBS_BLK), 1.0, 6.0, ((0, 32), (1, 8)), jnp.float32)
    obs_weight = jnp.clip(jnp.exp(math.log(3.0) - 1.7917595 * jax.random.uniform(key_list[5], (N_TILE, N_MEMBER * N_GRP, OBS_BLK), jnp.float32) ** levels(key_list[5], (N_TILE, N_MEMBER * N_GRP, OBS_BLK), ((0, 32), (1, 8)), -0.2, 0.2)), 0.5, 3.0)
    stencil_offsets = draw_stencil_offsets(jax.random.fold_in(key_list[8], 71), 0)
    stencil_weights = jnp.clip(jnp.exp(jax.random.uniform(key_list[7], (STENCIL_ENTRIES,), jnp.float32, math.log(0.2), math.log(1.0))), 0.2, 1.0)
    return {"members": members, "courant_x": courant_x, "courant_y": courant_y, "obs_cell": obs_cell, "innovation": innovation, "obs_weight": obs_weight, "stencil_offsets": stencil_offsets, "stencil_weights": stencil_weights}


STEP_SIZE = 0.25

def upwind(padded, courant_x, courant_y):
    centre = padded[..., 1:-1, 1:-1]
    upper = padded[..., :-2, 1:-1]
    lower = padded[..., 2:, 1:-1]
    left_cell = padded[..., 1:-1, :-2]
    right_cell = padded[..., 1:-1, 2:]
    x_plus = jnp.maximum(courant_x, 0.0)
    x_minus = jnp.minimum(courant_x, 0.0)
    y_plus = jnp.maximum(courant_y, 0.0)
    y_minus = jnp.minimum(courant_y, 0.0)
    return centre - x_plus * (centre - upper) - x_minus * (lower - centre) - y_plus * (centre - left_cell) - y_minus * (right_cell - centre)

def localize(padded, offsets, weights, sign, row_count, col_count):
    summed = jnp.zeros(padded.shape[:-2] + (row_count, col_count), jnp.float32)
    for entry in range(offsets.shape[0]):
        shifted = lax.dynamic_slice_in_dim(padded, RADIUS + sign * offsets[entry, 0], row_count, padded.ndim - 2)
        shifted = lax.dynamic_slice_in_dim(shifted, RADIUS + sign * offsets[entry, 1], col_count, padded.ndim - 1)
        summed = summed + weights[entry] * shifted
    return summed / jnp.sum(weights)

def pad_margin(values):
    widths = [(0, 0)] * (values.ndim - 2) + [(RADIUS, RADIUS), (RADIUS, RADIUS)]
    return jnp.pad(values, widths)

def reference(members, courant_x, courant_y, obs_cell, innovation, obs_weight, stencil_offsets, stencil_weights):

    def advect_step(field):
        for section in range(FSTEPS):
            field = upwind(jnp.pad(field, 1), courant_x, courant_y)
        return field
    predict_members = lax.map(advect_step, members)
    member_fields = predict_members.shape[0]
    member_deviation = math.sqrt(member_fields - 1)
    ensemble_average = lax.optimization_barrier(jnp.sum(predict_members, axis=0)) / member_fields
    deviation_rows = jnp.concatenate([(predict_members - ensemble_average[None]) / member_deviation, jnp.ones_like(predict_members[:1])], axis=0)
    tile_ids = lax.broadcasted_iota(jnp.int32, obs_cell.shape, 0)
    block_ids = lax.broadcasted_iota(jnp.int32, obs_cell.shape, 1)
    row_ids = tile_ids * CX + obs_cell // CY
    col_ids = block_ids * CY + obs_cell % CY
    flat_index = (row_ids * NY + col_ids).reshape(-1).astype(jnp.int32)
    innov_flat = innovation.reshape(-1)
    weight_flat = obs_weight.reshape(-1)
    row_count, col_count = (NX, NY)

    def observe(values):
        flat = values.reshape(-1)
        misfit = weight_flat * (flat[flat_index] - innov_flat)
        return jnp.zeros_like(flat).at[flat_index].add(misfit).reshape(values.shape)

    def combine(control):
        localized = localize(pad_margin(control), stencil_offsets, stencil_weights, 1, row_count, col_count)
        return lax.optimization_barrier(jnp.sum(deviation_rows[:-1] * localized[:-1], axis=0)) + localized[-1]
    control = jnp.zeros_like(deviation_rows)
    for sweep in range(GSTEPS):
        if sweep == 0:
            current = jnp.zeros((row_count, col_count), jnp.float32)
        else:
            current = combine(control)
        residual_field = observe(current)
        product = pad_margin(deviation_rows * residual_field[None])
        descent = control + localize(product, stencil_offsets, stencil_weights, -1, row_count, col_count)
        control = control - STEP_SIZE * descent
    increment = combine(control)
    return (predict_members + increment[None], increment)
```

```python
import math

import jax
import jax.numpy as jnp
from jax import lax
from jax.experimental import pallas as pl
from jax.experimental.pallas import tpu as pltpu
from jax.sharding import PartitionSpec as P

F32 = jnp.float32
BF16 = jnp.bfloat16
RADIUS = 2
STEP_SIZE = 0.25
GROUPS = 8
LOCAL = 10
ROWS = 32
LANES = 128
COLS = 1024
REACH = 4 * RADIUS
EDGE = REACH + 3
TALL = ROWS + 2 * REACH
WIDE = LANES + 2 * REACH
SLOTS = 12
SPARE = LOCAL * WIDE - (SLOTS - 1) * LANES
HALO = 136
VMEM = 48 * 1024 * 1024


def lane_ids(rows):
    return lax.broadcasted_iota(jnp.int32, (rows, LANES), 1)


def pieces(value, count):
    found = []
    for _ in range(count):
        part = value.astype(BF16)
        found.append(part)
        value = value - part.astype(F32)
    return found


def message_kernel(members, courant_x, courant_y, cell, innov, weight, up, down, fields):
    cells = cell[0]
    weights = weight[0]
    row_hit = lax.broadcasted_iota(jnp.int32, (ROWS, 1024), 0) == lax.shift_right_logical(cells, 7)
    col_hit = lax.broadcasted_iota(jnp.int32, (LANES, 1024), 0) == lax.bitwise_and(cells, LANES - 1)
    parts = pieces(weights * innov[0], 3) + pieces(weights, 3)
    hits = row_hit.astype(F32)
    left = jnp.concatenate([(hits * part.astype(F32)).astype(BF16) for part in parts], axis=0)
    sums = lax.dot_general(
        left, col_hit.astype(F32).astype(BF16), (((1,), (1,)), ((), ())), preferred_element_type=F32
    )
    for kind in range(2):
        base = 3 * ROWS * kind
        fields[kind] = (
            sums[base : base + ROWS]
            + sums[base + ROWS : base + 2 * ROWS]
            + sums[base + 2 * ROWS : base + 3 * ROWS]
        )
    for field in range(LOCAL + 2):
        if field < LOCAL:
            source = members.at[field]
        else:
            source = courant_x if field == LOCAL else courant_y
        up[field * EDGE : (field + 1) * EDGE, :] = source[0:EDGE, :]
        down[field * EDGE : (field + 1) * EDGE, :] = source[ROWS - EDGE : ROWS, :]
    base = (LOCAL + 2) * EDGE
    for kind in range(2):
        for row in range(REACH):
            lanes = slice(row * LANES, (row + 1) * LANES)
            up[base + kind : base + kind + 1, lanes] = fields[kind, row : row + 1, :]
            down[base + kind : base + kind + 1, lanes] = fields[
                kind, ROWS - REACH + row : ROWS - REACH + row + 1, :
            ]
    up[base + 2 : HALO, :] = jnp.zeros((HALO - base - 2, COLS), F32)
    down[base + 2 : HALO, :] = jnp.zeros((HALO - base - 2, COLS), F32)


TOP = 16
HEIGHT = 64


def send_plan():
    plan = [[] for _ in range(SLOTS)]
    for member in range(LOCAL):
        start = member * WIDE
        spans = (
            (start, start + REACH, -1),
            (start + REACH, start + REACH + LANES, 0),
            (start + REACH + LANES, start + WIDE, 1),
        )
        for low, high, offset in spans:
            while low < high:
                slot = low // LANES
                stop = min(high, (slot + 1) * LANES)
                plan[slot].append((member, offset, low - slot * LANES, stop - slot * LANES))
                low = stop
    return plan


def forecast_kernel(
    members, courant_x, courant_y, above, below, fields, out, send, fields_tall, old, new, coefs, rolled
):
    lane = lane_ids(8)
    first, last = lane == 0, lane == LANES - 1
    base = (LOCAL + 2) * EDGE
    for block in range(GROUPS):
        lanes = slice(block * LANES, (block + 1) * LANES)
        for kind, own in enumerate((courant_x, courant_y)):
            at = (LOCAL + kind) * EDGE
            new[kind, block + 1, TOP : TOP + ROWS, :] = own[:, lanes]
            new[kind, block + 1, TOP - EDGE : TOP, :] = above[at : at + EDGE, lanes]
            new[kind, block + 1, TOP + ROWS : TOP + ROWS + EDGE, :] = below[at : at + EDGE, lanes]
        for member in range(LOCAL):
            at = member * EDGE
            old[member, block + 1, TOP : TOP + ROWS, :] = members[member, :, lanes]
            old[member, block + 1, TOP - EDGE : TOP, :] = above[at : at + EDGE, lanes]
            old[member, block + 1, TOP + ROWS : TOP + ROWS + EDGE, :] = below[at : at + EDGE, lanes]
    nothing = jnp.zeros((HEIGHT, LANES), F32)
    for member in range(LOCAL):
        for side in (0, GROUPS + 1):
            old[member, side] = nothing
            rolled[member, side] = nothing[:TALL]

    @pl.loop(0, GROUPS)
    def _(block):
        for part in range(HEIGHT // 8):
            rows = slice(part * 8, part * 8 + 8)
            cx = new[0, block + 1, rows, :]
            cy = new[1, block + 1, rows, :]
            x_plus, x_minus = jnp.maximum(cx, 0.0), jnp.minimum(cx, 0.0)
            y_plus, y_minus = jnp.maximum(cy, 0.0), jnp.minimum(cy, 0.0)
            coefs[0, block, rows, :] = 1.0 - x_plus + x_minus - y_plus + y_minus
            coefs[1, block, rows, :] = x_plus
            coefs[2, block, rows, :] = -x_minus
            coefs[3, block, rows, :] = y_plus
            coefs[4, block, rows, :] = -y_minus

    for member in range(LOCAL):
        for side in (0, GROUPS + 1):
            new[member, side] = nothing

    buffers = (old, new)
    for step in range(3):
        source, target = buffers[step % 2], buffers[(step + 1) % 2]
        starts = range(TOP - EDGE + 1 + step, TOP + ROWS + EDGE - 1 - step, 8)

        @pl.loop(0, GROUPS)
        def _(block):
            for low in starts:
                rows = slice(low, low + 8)
                k_mid, k_up, k_down, k_left, k_right = (
                    coefs[kind, block, rows, :] for kind in range(5)
                )
                above_rows = slice(low - 1, low + 7)
                below_rows = slice(low + 1, low + 9)
                for member in range(LOCAL):
                    mid = source[member, block + 1, rows, :]
                    before = source[member, block, rows, :]
                    after = source[member, block + 2, rows, :]
                    value = (
                        k_mid * mid
                        + k_up * source[member, block + 1, above_rows, :]
                        + k_down * source[member, block + 1, below_rows, :]
                        + k_left * pltpu.roll(jnp.where(last, before, mid), 1, 1)
                        + k_right * pltpu.roll(jnp.where(first, after, mid), LANES - 1, 1)
                    )
                    if step < 2:
                        target[member, block + 1, rows, :] = value
                    else:
                        shift = (member * WIDE + REACH) % LANES
                        rolled[member, block + 1, low - 8 : low, :] = (
                            pltpu.roll(value, shift, 1) if shift else value
                        )
                        if TOP <= low < TOP + ROWS:
                            target[member, block + 1, rows, :] = value

    final = buffers[1]
    for member in range(LOCAL):
        for block in range(GROUPS):
            out[member, :, block * LANES : (block + 1) * LANES] = final[
                member, block + 1, TOP : TOP + ROWS, :
            ]

    for kind in range(2):
        for row in range(REACH):
            lanes = slice(row * LANES, (row + 1) * LANES)
            fields_tall[kind, row : row + 1, :] = above[base + kind : base + kind + 1, lanes]
            fields_tall[kind, REACH + ROWS + row : REACH + ROWS + row + 1, :] = below[
                base + kind : base + kind + 1, lanes
            ]
        fields_tall[kind, REACH : REACH + ROWS, :] = fields[kind]

    tall_lane = lane_ids(TALL)
    ends = jnp.where(
        tall_lane < SPARE + 2 * REACH,
        pltpu.roll(fields_tall[0], SPARE + REACH, 1),
        pltpu.roll(fields_tall[1], SPARE + 3 * REACH, 1),
    )
    plan = send_plan()

    @pl.loop(0, GROUPS)
    def _(block):
        for slot in range(SLOTS):
            value = ends if slot == SLOTS - 1 else None
            for member, offset, low, high in plan[slot]:
                part = rolled[member, block + 1 + offset]
                if value is None:
                    value = part
                else:
                    value = jnp.where((tall_lane >= low) & (tall_lane < high), part, value)
            send[block, slot] = value


DEEP = 56


def member_place(member):
    return member * WIDE // LANES, member * WIDE % LANES


def folded(slots, lane):
    near, far = None, None
    for member in range(LOCAL):
        base, shift = member_place(member)
        here, there = slots(base), slots(base + 1)
        if shift:
            here = pltpu.roll(jnp.where(lane >= shift, here, there), LANES - shift, 1)
            there = pltpu.roll(there, LANES - shift, 1)
        near = here if near is None else near + here
        far = there if far is None else far + there
    return near, far


def spread_out(near, far, lane, store):
    slots = [None] * SLOTS
    for member in range(LOCAL):
        base, shift = member_place(member)
        moved = pltpu.roll(near, shift, 1) if shift else near
        tail = pltpu.roll(far, shift, 1) if shift else far
        slots[base] = moved if slots[base] is None else jnp.where(lane >= shift, moved, slots[base])
        slots[base + 1] = jnp.where(
            lane < shift, moved, jnp.where(lane < shift + 2 * REACH, tail, 0.0)
        )
    for slot in range(SLOTS):
        store(slot, slots[slot])


def shifted_copies(copies, slots, rows):
    lane = lane_ids(rows)

    @pl.loop(0, slots)
    def _(slot):
        mid = copies[RADIUS, slot, 0:rows, :]
        after = copies[RADIUS, jnp.minimum(slot + 1, SLOTS - 1), 0:rows, :]
        before = copies[RADIUS, jnp.maximum(slot - 1, 0), 0:rows, :]
        for shift in (1, 2):
            copies[RADIUS + shift, slot, 0:rows, :] = pltpu.roll(
                jnp.where(lane < shift, after, mid), LANES - shift, 1
            )
            copies[RADIUS - shift, slot, 0:rows, :] = pltpu.roll(
                jnp.where(lane >= LANES - shift, before, mid), shift, 1
            )


def analysis_kernel(
    place, offsets, weights, got, fields, increment, spread_copies,
    spread, averages, gains, inside, products, localized, total, plane,
):
    tile, block = place[0], place[1]
    lane = lane_ids(TALL)
    entries = offsets.shape[0]
    tap_row = [offsets[entry, 0] for entry in range(entries)]
    tap_col = [offsets[entry, 1] for entry in range(entries)]
    tap = [weights[entry] for entry in range(entries)]
    weight_sum = tap[0]
    for entry in range(1, entries):
        weight_sum = weight_sum + tap[entry]
    scale = 1.0 / jnp.full((1, LANES), weight_sum, F32)
    scale = scale * scale

    @pl.loop(0, SLOTS)
    def _(slot):
        value = got[0, slot]
        for source in range(1, GROUPS):
            value = value + got[source, slot]
        averages[slot] = value

    near, far = folded(lambda slot: averages[slot], lane)
    count = GROUPS * LOCAL

    def store_average(slot, value):
        averages[slot] = value

    spread_out(near / count, far / count, lane, store_average)
    deviation = 1.0 / math.sqrt(count - 1)

    @pl.loop(0, SLOTS)
    def _(slot):
        for source in range(GROUPS):
            spread[source, slot] = (got[source, slot] - averages[slot]) * deviation

    row = lax.broadcasted_iota(jnp.int32, (TALL, LANES), 0) + (tile * ROWS - REACH)
    col = lane + (block * LANES - REACH)
    row_ok = (row >= 0) & (row < ROWS * 32)
    near_ok = row_ok & (col >= 0) & (col < COLS)
    far_ok = row_ok & (col + LANES < COLS)

    def store_inside(slot, value):
        inside[slot, 0:TALL, :] = value
        inside[slot, TALL:DEEP, :] = jnp.zeros((DEEP - TALL, LANES), F32)

    spread_out(near_ok.astype(F32), far_ok.astype(F32), lane, store_inside)

    left_ends = got[jnp.maximum(block - 1, 0), SLOTS - 1]
    right_ends = got[jnp.minimum(block + 1, GROUPS - 1), SLOTS - 1]
    left_ends = jnp.where(block > 0, left_ends, 0.0)
    right_ends = jnp.where(block < GROUPS - 1, right_ends, 0.0)
    planes = []
    for kind in range(2):
        back = LANES - SPARE - 2 * REACH * kind
        own = pltpu.roll(fields[kind], REACH, 1)
        near = jnp.where(lane < REACH, pltpu.roll(left_ends, back, 1), own)
        far = jnp.where(lane < REACH, own, pltpu.roll(right_ends, back, 1))
        far = jnp.where(lane < 2 * REACH, far, 0.0)
        planes.append((near, far))

    def store_gain(slot, value):
        gains[slot] = value

    def sweep(slots, multiplier, z_low, z_rows, x_low, x_rows, finish):
        @pl.loop(0, slots)
        def _(slot):
            products[RADIUS, slot, 0:TALL, :] = multiplier(slot)

        shifted_copies(products, slots, TALL)

        @pl.loop(0, slots)
        def _(slot):
            value = None
            for entry in range(entries):
                term = tap[entry] * products[
                    RADIUS - tap_col[entry], slot, pl.ds(z_low - tap_row[entry], z_rows), :
                ]
                value = term if value is None else value + term
            rows = slice(z_low, z_low + z_rows)
            localized[RADIUS, slot, rows, :] = value * inside[slot, rows, :]

        shifted_copies(localized, slots, DEEP)

        @pl.loop(0, slots)
        def _(slot):
            value = None
            for entry in range(entries):
                term = tap[entry] * localized[
                    RADIUS + tap_col[entry], slot, pl.ds(x_low + tap_row[entry], x_rows), :
                ]
                value = term if value is None else value + term
            finish(slot, value)

    def apply(near, far, z_low, z_rows, x_low, x_rows):
        spread_out(near, far, lane, store_gain)
        ones = []

        def finish_ones(slot, value):
            plane[slot, 0:x_rows, :] = value

        sweep(2, lambda slot: gains[slot], z_low, z_rows, x_low, x_rows, finish_ones)

        @pl.loop(0, SLOTS)
        def _(slot):
            total[slot, 0:x_rows, :] = jnp.zeros((x_rows, LANES), F32)

        @pl.loop(0, GROUPS)
        def _(source):
            def finish(slot, value):
                total[slot, 0:x_rows, :] += value * spread[source, slot, x_low : x_low + x_rows, :]

            sweep(
                SLOTS, lambda slot: gains[slot] * spread[source, slot],
                z_low, z_rows, x_low, x_rows, finish,
            )

        near, far = folded(lambda slot: total[slot, 0:x_rows, :], lane_ids(x_rows))
        return (near + plane[0, 0:x_rows, :]) * scale, (far + plane[1, 0:x_rows, :]) * scale

    for slot in range(SLOTS):
        for kind in range(2 * RADIUS + 1):
            products[kind, slot, TALL:DEEP, :] = jnp.zeros((DEEP - TALL, LANES), F32)
        localized[RADIUS, slot] = jnp.zeros((DEEP, LANES), F32)

    (near_v, far_v), (near_w, far_w) = planes
    near, far = apply(near_v, far_v, 2, 48, 4, 40)
    for part, value in enumerate((near, far)):
        plane[2 + part, 0:TALL, :] = jnp.zeros((TALL, LANES), F32)
        plane[2 + part, 4:44, :] = value
    near = (STEP_SIZE * near_w) * plane[2, 0:TALL, :] - (2.0 - STEP_SIZE) * near_v
    far = (STEP_SIZE * far_w) * plane[3, 0:TALL, :] - (2.0 - STEP_SIZE) * far_v
    far = jnp.where(lane < 2 * REACH, far, 0.0)
    near, far = apply(near, far, 6, 40, 8, 32)
    short_lane = lane_ids(ROWS)
    result = pltpu.roll(jnp.where(short_lane < REACH, far, near), LANES - REACH, 1) * -STEP_SIZE
    increment[...] = result
    for target in range(GROUPS):
        spread_copies[target] = result


def recentre_kernel(fields, increments, out):
    for block in range(GROUPS):
        lanes = slice(block * LANES, (block + 1) * LANES)
        value = increments[block]
        for member in range(LOCAL):
            out[member, :, lanes] = fields[member, :, lanes] + value


def on_vmem(count):
    return [pl.BlockSpec(memory_space=pltpu.VMEM)] * count


def on_device(
    members, courant_x, courant_y, obs_cell, innovation, obs_weight, stencil_offsets, stencil_weights
):
    both = ("member", "grp")
    params = pltpu.CompilerParams(vmem_limit_bytes=VMEM)
    tiles = lax.axis_size("tile")
    up, down, fields = pl.pallas_call(
        message_kernel,
        out_shape=[
            jax.ShapeDtypeStruct((HALO, COLS), F32),
            jax.ShapeDtypeStruct((HALO, COLS), F32),
            jax.ShapeDtypeStruct((2, ROWS, LANES), F32),
        ],
        in_specs=on_vmem(6),
        out_specs=on_vmem(3),
        compiler_params=params,
        name="messages",
    )(members, courant_x, courant_y, obs_cell, innovation, obs_weight)
    above = lax.ppermute(down, "tile", [(i, i + 1) for i in range(tiles - 1)])
    below = lax.ppermute(up, "tile", [(i + 1, i) for i in range(tiles - 1)])
    forecast, send, fields_tall = pl.pallas_call(
        forecast_kernel,
        out_shape=[
            jax.ShapeDtypeStruct(members.shape, F32),
            jax.ShapeDtypeStruct((GROUPS, SLOTS, TALL, LANES), F32),
            jax.ShapeDtypeStruct((2, TALL, LANES), F32),
        ],
        in_specs=on_vmem(6),
        out_specs=on_vmem(3),
        scratch_shapes=[
            pltpu.VMEM((LOCAL, GROUPS + 2, HEIGHT, LANES), F32),
            pltpu.VMEM((LOCAL, GROUPS + 2, HEIGHT, LANES), F32),
            pltpu.VMEM((5, GROUPS, HEIGHT, LANES), F32),
            pltpu.VMEM((LOCAL, GROUPS + 2, TALL, LANES), F32),
        ],
        compiler_params=params,
        name="forecast",
    )(members, courant_x, courant_y, above, below, fields)
    got = lax.all_to_all(
        send.reshape(GROUPS, SLOTS * TALL, LANES), both, 0, 0, tiled=True
    ).reshape(GROUPS, SLOTS, TALL, LANES)
    place = jnp.stack([lax.axis_index("tile"), lax.axis_index(both)]).astype(jnp.int32)
    increment, copies = pl.pallas_call(
        analysis_kernel,
        out_shape=[
            jax.ShapeDtypeStruct((ROWS, LANES), F32),
            jax.ShapeDtypeStruct((GROUPS, ROWS, LANES), F32),
        ],
        in_specs=[pl.BlockSpec(memory_space=pltpu.SMEM)] * 3 + on_vmem(2),
        out_specs=on_vmem(2),
        scratch_shapes=[
            pltpu.VMEM((GROUPS, SLOTS, TALL, LANES), F32),
            pltpu.VMEM((SLOTS, TALL, LANES), F32),
            pltpu.VMEM((SLOTS, TALL, LANES), F32),
            pltpu.VMEM((SLOTS, DEEP, LANES), F32),
            pltpu.VMEM((2 * RADIUS + 1, SLOTS, DEEP, LANES), F32),
            pltpu.VMEM((2 * RADIUS + 1, SLOTS, DEEP, LANES), F32),
            pltpu.VMEM((SLOTS, TALL, LANES), F32),
            pltpu.VMEM((4, TALL, LANES), F32),
        ],
        compiler_params=params,
        name="analysis",
    )(place, stencil_offsets, stencil_weights, got, fields_tall)
    increments = lax.all_to_all(copies, both, 0, 0, tiled=True)
    analysis = pl.pallas_call(
        recentre_kernel,
        out_shape=jax.ShapeDtypeStruct(members.shape, F32),
        in_specs=on_vmem(2),
        out_specs=pl.BlockSpec(memory_space=pltpu.VMEM),
        compiler_params=params,
        name="recentre",
    )(forecast, increments)
    return analysis, increment


def solution(mesh):
    both = ("member", "grp")
    placed = (
        P(both, "tile", None),
        P("tile", None),
        P("tile", None),
        P("tile", both, None),
        P("tile", both, None),
        P("tile", both, None),
        P(),
        P(),
    )
    return jax.shard_map(
        on_device,
        mesh=mesh,
        in_specs=placed,
        out_specs=(P(both, "tile", None), P("tile", both)),
        check_vma=False,
    )
```

```python
import math

import jax
import jax.numpy as jnp
from jax import lax
from jax.experimental import pallas as pl
from jax.experimental.pallas import tpu as pltpu
from jax.sharding import PartitionSpec as P

F32 = jnp.float32
BF16 = jnp.bfloat16
RADIUS = 2
STEP_SIZE = 0.25
GROUPS = 8
LOCAL = 10
ROWS = 32
LANES = 128
COLS = 1024
REACH = 4 * RADIUS
EDGE = REACH + 3
TALL = ROWS + 2 * REACH
WIDE = LANES + 2 * REACH
SLOTS = 12
SPARE = LOCAL * WIDE - (SLOTS - 1) * LANES
HALO = 136
MID = 24
RIM = (TALL - MID) // 2
VMEM = 48 * 1024 * 1024


def lane_ids(rows):
    return lax.broadcasted_iota(jnp.int32, (rows, LANES), 1)


def pieces(value, count):
    found = []
    for _ in range(count):
        part = value.astype(BF16)
        found.append(part)
        value = value - part.astype(F32)
    return found


def set_coefs(courants, coefs, rows):
    @pl.loop(0, GROUPS)
    def _(block):
        for low in rows:
            span = slice(low, low + 8)
            cx = courants[0, block, span, :]
            cy = courants[1, block, span, :]
            x_plus, x_minus = jnp.maximum(cx, 0.0), jnp.minimum(cx, 0.0)
            y_plus, y_minus = jnp.maximum(cy, 0.0), jnp.minimum(cy, 0.0)
            coefs[0, block, span, :] = 1.0 - x_plus + x_minus - y_plus + y_minus
            coefs[1, block, span, :] = x_plus
            coefs[2, block, span, :] = -x_minus
            coefs[3, block, span, :] = y_plus
            coefs[4, block, span, :] = -y_minus


def clear_sides(buffers):
    for buffer in buffers:
        nothing = jnp.zeros(buffer.shape[2:], F32)
        for member in range(LOCAL):
            for side in (0, GROUPS + 1):
                buffer[member, side] = nothing


def advance(source, target, coefs, starts):
    lane = lane_ids(8)
    first, last = lane == 0, lane == LANES - 1

    @pl.loop(0, GROUPS)
    def _(block):
        for low in starts:
            rows = slice(low, low + 8)
            k_mid, k_up, k_down, k_left, k_right = (coefs[kind, block, rows, :] for kind in range(5))
            for member in range(LOCAL):
                mid = source[member, block + 1, rows, :]
                before = source[member, block, rows, :]
                after = source[member, block + 2, rows, :]
                target[member, block + 1, rows, :] = (
                    k_mid * mid
                    + k_up * source[member, block + 1, low - 1 : low + 7, :]
                    + k_down * source[member, block + 1, low + 1 : low + 9, :]
                    + k_left * pltpu.roll(jnp.where(last, before, mid), 1, 1)
                    + k_right * pltpu.roll(jnp.where(first, after, mid), LANES - 1, 1)
                )


def send_plan():
    plan = [[] for _ in range(SLOTS)]
    for member in range(LOCAL):
        start = member * WIDE
        spans = (
            (start, start + REACH, -1),
            (start + REACH, start + REACH + LANES, 0),
            (start + REACH + LANES, start + WIDE, 1),
        )
        for low, high, offset in spans:
            while low < high:
                slot = low // LANES
                stop = min(high, (slot + 1) * LANES)
                plan[slot].append((member, offset, low - slot * LANES, stop - slot * LANES))
                low = stop
    return plan


def pack(final, pieces_of_rows, fields, rolled, send):
    @pl.loop(0, GROUPS)
    def _(block):
        for member in range(LOCAL):
            shift = (member * WIDE + REACH) % LANES
            for there, here, count in pieces_of_rows:
                value = final[member, block + 1, there : there + count, :]
                rolled[member, block + 1, here : here + count, :] = (
                    pltpu.roll(value, shift, 1) if shift else value
                )

    lane = lane_ids(MID)
    ends = jnp.where(
        lane < SPARE + 2 * REACH,
        pltpu.roll(fields[0], SPARE + REACH, 1),
        pltpu.roll(fields[1], SPARE + 3 * REACH, 1),
    )
    plan = send_plan()

    @pl.loop(0, GROUPS)
    def _(block):
        for slot in range(SLOTS):
            value = ends if slot == SLOTS - 1 else None
            for member, offset, low, high in plan[slot]:
                part = rolled[member, block + 1 + offset]
                if value is None:
                    value = part
                else:
                    value = jnp.where((lane >= low) & (lane < high), part, value)
            send[block, slot] = value


TOP = 16
HEIGHT = 56


def inner_kernel(
    members, courant_x, courant_y, cell, innov, weight,
    up, down, fields, out, send,
    old, new, courants, coefs, rolled, cells, values, member_sems, sems,
):
    own = slice(TOP, TOP + ROWS)
    small = [
        pltpu.make_async_copy(cell, cells, sems.at[0]),
        pltpu.make_async_copy(innov, values.at[0], sems.at[1]),
        pltpu.make_async_copy(weight, values.at[1], sems.at[2]),
    ]
    large, wind = [], []
    for copy in small:
        copy.start()
    for block in range(GROUPS):
        lanes = slice(block * LANES, (block + 1) * LANES)
        for kind, source in enumerate((courant_x, courant_y)):
            wind.append(
                pltpu.make_async_copy(
                    source.at[:, lanes], courants.at[kind, block, own, :],
                    sems.at[3 + 2 * block + kind],
                )
            )
        large.append(
            pltpu.make_async_copy(
                members.at[:, :, lanes], old.at[:, block + 1, own, :], member_sems.at[block]
            )
        )
    for copy in wind + large:
        copy.start()
    clear_sides((old, new, rolled))
    for copy in small:
        copy.wait()

    row_hit = lax.broadcasted_iota(jnp.int32, (ROWS, 1024), 0) == lax.shift_right_logical(cells[0], 7)
    col_hit = lax.broadcasted_iota(jnp.int32, (LANES, 1024), 0) == lax.bitwise_and(
        cells[0], LANES - 1
    )
    parts = pieces(values[1, 0] * values[0, 0], 3) + pieces(values[1, 0], 3)
    hits = row_hit.astype(F32)
    left = jnp.concatenate([(hits * part.astype(F32)).astype(BF16) for part in parts], axis=0)
    sums = lax.dot_general(
        left, col_hit.astype(F32).astype(BF16), (((1,), (1,)), ((), ())), preferred_element_type=F32
    )
    for kind in range(2):
        base = 3 * ROWS * kind
        fields[kind] = (
            sums[base : base + ROWS]
            + sums[base + ROWS : base + 2 * ROWS]
            + sums[base + 2 * ROWS : base + 3 * ROWS]
        )

    for copy in wind:
        copy.wait()
    set_coefs(courants, coefs, range(TOP, TOP + ROWS, 8))
    for copy in large:
        copy.wait()

    @pl.loop(0, GROUPS)
    def _(block):
        for field in range(LOCAL + 2):
            span = slice(field * EDGE, (field + 1) * EDGE)
            if field < LOCAL:
                up[block, span, :] = old[field, block + 1, TOP : TOP + EDGE, :]
                down[block, span, :] = old[field, block + 1, TOP + ROWS - EDGE : TOP + ROWS, :]
            else:
                kind = field - LOCAL
                up[block, span, :] = courants[kind, block, TOP : TOP + EDGE, :]
                down[block, span, :] = courants[kind, block, TOP + ROWS - EDGE : TOP + ROWS, :]

    base = (LOCAL + 2) * EDGE
    for row in range(REACH):
        for kind in range(2):
            up[row, base + kind : base + kind + 1, :] = fields[kind, row : row + 1, :]
            down[row, base + kind : base + kind + 1, :] = fields[
                kind, ROWS - REACH + row : ROWS - REACH + row + 1, :
            ]
        up[row, base + 2 : HALO, :] = jnp.zeros((HALO - base - 2, LANES), F32)
        down[row, base + 2 : HALO, :] = jnp.zeros((HALO - base - 2, LANES), F32)

    advance(old, new, coefs, range(TOP, TOP + ROWS, 8))
    advance(new, old, coefs, range(TOP, TOP + ROWS, 8))
    skip = (ROWS - MID) // 2
    advance(old, new, coefs, range(TOP + skip, TOP + skip + MID, 8))
    for member in range(LOCAL):
        for block in range(GROUPS):
            out[member, block] = new[member, block + 1, TOP + skip : TOP + skip + MID, :]
    middle = [fields[kind, skip : skip + MID, :] for kind in range(2)]
    pack(new, ((TOP + skip, 0, MID),), middle, rolled, send)


LOW = 8


def outer_kernel(
    members, courant_x, courant_y, above, below, fields,
    out, send, fields_tall,
    old, new, courants, coefs, rolled, rims, member_sems, sems,
):
    top, end = slice(TOP, TOP + 8), slice(ROWS - 8 + LOW, ROWS + LOW)
    copies = []
    for block in range(GROUPS):
        lanes = slice(block * LANES, (block + 1) * LANES)
        for part, span in enumerate((top, end)):
            rows = slice(0, 8) if part == 0 else slice(ROWS - 8, ROWS)
            copies.append(
                pltpu.make_async_copy(
                    members.at[:, rows, lanes], old.at[:, block + 1, span, :],
                    member_sems.at[part, block],
                )
            )
            for kind, source in enumerate((courant_x, courant_y)):
                copies.append(
                    pltpu.make_async_copy(
                        source.at[rows, lanes], courants.at[kind, block, span, :],
                        sems.at[kind, part, block],
                    )
                )
    for copy in copies:
        copy.start()
    clear_sides((old, new, rolled))
    base = (LOCAL + 2) * EDGE

    @pl.loop(0, GROUPS)
    def _(block):
        for field in range(LOCAL + 2):
            span = slice(field * EDGE, (field + 1) * EDGE)
            before, after = above[block, span, :], below[block, span, :]
            if field < LOCAL:
                old[field, block + 1, TOP - EDGE : TOP, :] = before
                old[field, block + 1, ROWS + LOW : ROWS + LOW + EDGE, :] = after
            else:
                courants[field - LOCAL, block, TOP - EDGE : TOP, :] = before
                courants[field - LOCAL, block, ROWS + LOW : ROWS + LOW + EDGE, :] = after

    for kind in range(2):
        for row in range(REACH):
            fields_tall[kind, row : row + 1, :] = above[row, base + kind : base + kind + 1, :]
            fields_tall[kind, REACH + ROWS + row : REACH + ROWS + row + 1, :] = below[
                row, base + kind : base + kind + 1, :
            ]
        fields_tall[kind, REACH : REACH + ROWS, :] = fields[kind]
        rims[kind, 0:RIM, :] = fields_tall[kind, 0:RIM, :]
        rims[kind, RIM:MID, :] = fields_tall[kind, TALL - RIM : TALL, :]
    for copy in copies:
        copy.wait()
    set_coefs(courants, coefs, range(0, HEIGHT, 8))
    for step in range(3):
        high, low = TOP - EDGE + 1 + step, ROWS - 6 + step + LOW
        pair = (old, new) if step % 2 == 0 else (new, old)
        advance(*pair, coefs, (high, high + 8, low, low + 8))
    keep = (ROWS - MID) // 2
    low = ROWS - keep + LOW
    for member in range(LOCAL):
        for block in range(GROUPS):
            out[member, block, 0:keep, :] = new[member, block + 1, TOP : TOP + keep, :]
            out[member, block, keep : 2 * keep, :] = new[member, block + 1, low : low + keep, :]
    pack(new, ((TOP - REACH, 0, RIM), (low, RIM, RIM)), rims, rolled, send)


DEEP = 56
MID_ROWS = ((RIM, 0, MID),)
RIM_ROWS = ((0, 0, RIM), (TALL - RIM, RIM, RIM))


def member_place(member):
    return member * WIDE // LANES, member * WIDE % LANES


def folded(slots, lane):
    near, far = None, None
    for member in range(LOCAL):
        base, shift = member_place(member)
        here, there = slots(base), slots(base + 1)
        if shift:
            here = pltpu.roll(jnp.where(lane >= shift, here, there), LANES - shift, 1)
            there = pltpu.roll(there, LANES - shift, 1)
        near = here if near is None else near + here
        far = there if far is None else far + there
    return near, far


def spread_out(near, far, lane, store):
    slots = [None] * SLOTS
    for member in range(LOCAL):
        base, shift = member_place(member)
        moved = pltpu.roll(near, shift, 1) if shift else near
        tail = pltpu.roll(far, shift, 1) if shift else far
        slots[base] = moved if slots[base] is None else jnp.where(lane >= shift, moved, slots[base])
        slots[base + 1] = jnp.where(
            lane < shift, moved, jnp.where(lane < shift + 2 * REACH, tail, 0.0)
        )
    for slot in range(SLOTS):
        store(slot, slots[slot])


def shifted_copies(copies, slots, low, rows):
    lane = lane_ids(rows)

    for slot in range(slots):
        mid = copies[RADIUS, slot, low : low + rows, :]
        after = copies[RADIUS, min(slot + 1, SLOTS - 1), low : low + rows, :]
        before = copies[RADIUS, max(slot - 1, 0), low : low + rows, :]
        for shift in (1, 2):
            copies[RADIUS + shift, slot, low : low + rows, :] = pltpu.roll(
                jnp.where(lane < shift, after, mid), LANES - shift, 1
            )
            copies[RADIUS - shift, slot, low : low + rows, :] = pltpu.roll(
                jnp.where(lane >= LANES - shift, before, mid), shift, 1
            )


def analysis_kernel(
    place, offsets, weights, got_mid, got_rim, fields, increment, spread_copies,
    spread, averages, gains, inside, products, localized, total, plane, ends,
):
    tile, block = place[0], place[1]
    lane = lane_ids(TALL)
    entries = offsets.shape[0]
    tap_row = [offsets[entry, 0] for entry in range(entries)]
    tap_col = [offsets[entry, 1] for entry in range(entries)]
    tap = [weights[entry] for entry in range(entries)]
    weight_sum = tap[0]
    for entry in range(1, entries):
        weight_sum = weight_sum + tap[entry]
    scale = 1.0 / jnp.full((1, LANES), weight_sum, F32)
    scale = scale * scale

    @pl.loop(0, SLOTS)
    def _(slot):
        for got, parts in ((got_mid, MID_ROWS), (got_rim, RIM_ROWS)):
            value = got[0, slot]
            for source in range(1, GROUPS):
                value = value + got[source, slot]
            for here, there, count in parts:
                averages[slot, here : here + count, :] = value[there : there + count]

    near, far = folded(lambda slot: averages[slot], lane)
    count = GROUPS * LOCAL

    def store_average(slot, value):
        averages[slot] = value

    spread_out(near / count, far / count, lane, store_average)
    deviation = 1.0 / math.sqrt(count - 1)

    @pl.loop(0, SLOTS)
    def _(slot):
        for got, parts in ((got_mid, MID_ROWS), (got_rim, RIM_ROWS)):
            for here, there, count in parts:
                average = averages[slot, here : here + count, :]
                for source in range(GROUPS):
                    value = got[source, slot, there : there + count, :]
                    spread[source, slot, here : here + count, :] = (value - average) * deviation

    row = lax.broadcasted_iota(jnp.int32, (TALL, LANES), 0) + (tile * ROWS - REACH)
    col = lane + (block * LANES - REACH)
    row_ok = (row >= 0) & (row < ROWS * 32)
    near_ok = row_ok & (col >= 0) & (col < COLS)
    far_ok = row_ok & (col + LANES < COLS)

    def store_inside(slot, value):
        inside[slot, 0:TALL, :] = value
        inside[slot, TALL:DEEP, :] = jnp.zeros((DEEP - TALL, LANES), F32)

    spread_out(near_ok.astype(F32), far_ok.astype(F32), lane, store_inside)

    for got, parts in ((got_mid, MID_ROWS), (got_rim, RIM_ROWS)):
        for here, there, count in parts:
            rows = slice(there, there + count)
            ends[0, here : here + count, :] = got[jnp.maximum(block - 1, 0), SLOTS - 1, rows, :]
            ends[1, here : here + count, :] = got[
                jnp.minimum(block + 1, GROUPS - 1), SLOTS - 1, rows, :
            ]
    left_ends = jnp.where(block > 0, ends[0], 0.0)
    right_ends = jnp.where(block < GROUPS - 1, ends[1], 0.0)
    planes = []
    for kind in range(2):
        back = LANES - SPARE - 2 * REACH * kind
        own = pltpu.roll(fields[kind], REACH, 1)
        near = jnp.where(lane < REACH, pltpu.roll(left_ends, back, 1), own)
        far = jnp.where(lane < REACH, own, pltpu.roll(right_ends, back, 1))
        far = jnp.where(lane < 2 * REACH, far, 0.0)
        planes.append((near, far))

    def store_gain(slot, value):
        gains[slot] = value

    def sweep(slots, multiplier, y_rows, z_low, z_rows, x_low, x_rows, finish):
        @pl.loop(0, slots)
        def _(slot):
            products[RADIUS, slot, 0:TALL, :] = multiplier(slot)

        shifted_copies(products, slots, z_low - RADIUS, y_rows)

        @pl.loop(0, slots)
        def _(slot):
            value = None
            for entry in range(entries):
                term = tap[entry] * products[
                    RADIUS - tap_col[entry], slot, pl.ds(z_low - tap_row[entry], z_rows), :
                ]
                value = term if value is None else value + term
            rows = slice(z_low, z_low + z_rows)
            localized[RADIUS, slot, rows, :] = value * inside[slot, rows, :]

        shifted_copies(localized, slots, z_low, z_rows)

        @pl.loop(0, slots)
        def _(slot):
            value = None
            for entry in range(entries):
                term = tap[entry] * localized[
                    RADIUS + tap_col[entry], slot, pl.ds(x_low + tap_row[entry], x_rows), :
                ]
                value = term if value is None else value + term
            finish(slot, value)

    def apply(near, far, y_rows, z_low, z_rows, x_low, x_rows):
        spread_out(near, far, lane, store_gain)
        ones = []

        def finish_ones(slot, value):
            plane[slot, 0:x_rows, :] = value

        sweep(2, lambda slot: gains[slot], y_rows, z_low, z_rows, x_low, x_rows, finish_ones)

        @pl.loop(0, SLOTS)
        def _(slot):
            total[slot, 0:x_rows, :] = jnp.zeros((x_rows, LANES), F32)

        @pl.loop(0, GROUPS)
        def _(source):
            def finish(slot, value):
                total[slot, 0:x_rows, :] += value * spread[source, slot, x_low : x_low + x_rows, :]

            sweep(
                SLOTS, lambda slot: gains[slot] * spread[source, slot],
                y_rows, z_low, z_rows, x_low, x_rows, finish,
            )

        near, far = folded(lambda slot: total[slot, 0:x_rows, :], lane_ids(x_rows))
        return (near + plane[0, 0:x_rows, :]) * scale, (far + plane[1, 0:x_rows, :]) * scale

    for slot in range(SLOTS):
        for kind in range(2 * RADIUS + 1):
            products[kind, slot, TALL:DEEP, :] = jnp.zeros((DEEP - TALL, LANES), F32)
        localized[RADIUS, slot] = jnp.zeros((DEEP, LANES), F32)

    (near_v, far_v), (near_w, far_w) = planes
    near, far = apply(near_v, far_v, 48, 2, 48, 4, 40)
    for part, value in enumerate((near, far)):
        plane[2 + part, 0:TALL, :] = jnp.zeros((TALL, LANES), F32)
        plane[2 + part, 4:44, :] = value
    near = (STEP_SIZE * near_w) * plane[2, 0:TALL, :] - (2.0 - STEP_SIZE) * near_v
    far = (STEP_SIZE * far_w) * plane[3, 0:TALL, :] - (2.0 - STEP_SIZE) * far_v
    far = jnp.where(lane < 2 * REACH, far, 0.0)
    near, far = apply(near, far, 40, 6, 40, 8, 32)
    short_lane = lane_ids(ROWS)
    result = pltpu.roll(jnp.where(short_lane < REACH, far, near), LANES - REACH, 1) * -STEP_SIZE
    increment[...] = result
    for target in range(GROUPS):
        spread_copies[target] = result


def recentre_kernel(middle, rim, increments, out):
    keep = (ROWS - MID) // 2
    for block in range(GROUPS):
        lanes = slice(block * LANES, (block + 1) * LANES)
        for member in range(LOCAL):
            out[member, 0:keep, lanes] = rim[member, block, 0:keep, :] + increments[block, 0:keep, :]
            out[member, keep : keep + MID, lanes] = (
                middle[member, block] + increments[block, keep : keep + MID, :]
            )
            out[member, keep + MID : ROWS, lanes] = (
                rim[member, block, keep : 2 * keep, :] + increments[block, keep + MID : ROWS, :]
            )


def on_vmem(count):
    return [pl.BlockSpec(memory_space=pltpu.VMEM)] * count


def in_hbm(count):
    return [pl.BlockSpec(memory_space=pltpu.HBM)] * count


def array(*shape):
    return jax.ShapeDtypeStruct(shape, F32)


def on_device(
    members, courant_x, courant_y, obs_cell, innovation, obs_weight, stencil_offsets, stencil_weights
):
    both = ("member", "grp")
    params = pltpu.CompilerParams(vmem_limit_bytes=VMEM)
    tiles = lax.axis_size("tile")
    keep = (ROWS - MID) // 2
    buffers = [
        pltpu.VMEM((LOCAL, GROUPS + 2, HEIGHT, LANES), F32),
        pltpu.VMEM((LOCAL, GROUPS + 2, HEIGHT, LANES), F32),
        pltpu.VMEM((2, GROUPS, HEIGHT, LANES), F32),
        pltpu.VMEM((5, GROUPS, HEIGHT, LANES), F32),
        pltpu.VMEM((LOCAL, GROUPS + 2, MID, LANES), F32),
    ]
    up, down, fields, middle, send_mid = pl.pallas_call(
        inner_kernel,
        out_shape=[
            array(GROUPS, HALO, LANES),
            array(GROUPS, HALO, LANES),
            array(2, ROWS, LANES),
            array(LOCAL, GROUPS, MID, LANES),
            array(GROUPS, SLOTS, MID, LANES),
        ],
        in_specs=in_hbm(6),
        out_specs=on_vmem(5),
        scratch_shapes=buffers
        + [
            pltpu.VMEM((1, 1, 1024), jnp.int32),
            pltpu.VMEM((2, 1, 1, 1024), F32),
            pltpu.SemaphoreType.DMA((GROUPS,)),
            pltpu.SemaphoreType.DMA((3 + 2 * GROUPS,)),
        ],
        compiler_params=params,
        name="inner",
    )(members, courant_x, courant_y, obs_cell, innovation, obs_weight)
    got_mid = exchanged(send_mid, both)
    above = lax.ppermute(down, "tile", [(i, i + 1) for i in range(tiles - 1)])
    below = lax.ppermute(up, "tile", [(i + 1, i) for i in range(tiles - 1)])
    rim, send_rim, fields_tall = pl.pallas_call(
        outer_kernel,
        out_shape=[
            array(LOCAL, GROUPS, 2 * keep, LANES),
            array(GROUPS, SLOTS, MID, LANES),
            array(2, TALL, LANES),
        ],
        in_specs=in_hbm(3) + on_vmem(3),
        out_specs=on_vmem(3),
        scratch_shapes=buffers
        + [
            pltpu.VMEM((2, MID, LANES), F32),
            pltpu.SemaphoreType.DMA((2, GROUPS)),
            pltpu.SemaphoreType.DMA((2, 2, GROUPS)),
        ],
        compiler_params=params,
        name="outer",
    )(members, courant_x, courant_y, above, below, fields)
    got_rim = exchanged(send_rim, both)
    place = jnp.stack([lax.axis_index("tile"), lax.axis_index(both)]).astype(jnp.int32)
    increment, copies = pl.pallas_call(
        analysis_kernel,
        out_shape=[array(ROWS, LANES), array(GROUPS, ROWS, LANES)],
        in_specs=[pl.BlockSpec(memory_space=pltpu.SMEM)] * 3 + on_vmem(3),
        out_specs=on_vmem(2),
        scratch_shapes=[
            pltpu.VMEM((GROUPS, SLOTS, TALL, LANES), F32),
            pltpu.VMEM((SLOTS, TALL, LANES), F32),
            pltpu.VMEM((SLOTS, TALL, LANES), F32),
            pltpu.VMEM((SLOTS, DEEP, LANES), F32),
            pltpu.VMEM((2 * RADIUS + 1, SLOTS, DEEP, LANES), F32),
            pltpu.VMEM((2 * RADIUS + 1, SLOTS, DEEP, LANES), F32),
            pltpu.VMEM((SLOTS, TALL, LANES), F32),
            pltpu.VMEM((4, TALL, LANES), F32),
            pltpu.VMEM((2, TALL, LANES), F32),
        ],
        compiler_params=params,
        name="analysis",
    )(place, stencil_offsets, stencil_weights, got_mid, got_rim, fields_tall)
    increments = lax.all_to_all(copies, both, 0, 0, tiled=True)
    analysis = pl.pallas_call(
        recentre_kernel,
        out_shape=array(*members.shape),
        in_specs=on_vmem(3),
        out_specs=pl.BlockSpec(memory_space=pltpu.VMEM),
        compiler_params=params,
        name="recentre",
    )(middle, rim, increments)
    return analysis, increment


def exchanged(blocks, axes):
    flat = blocks.reshape(GROUPS, -1, LANES)
    return lax.all_to_all(flat, axes, 0, 0, tiled=True).reshape(blocks.shape)


def solution(mesh):
    both = ("member", "grp")
    placed = (
        P(both, "tile", None),
        P("tile", None),
        P("tile", None),
        P("tile", both, None),
        P("tile", both, None),
        P("tile", both, None),
        P(),
        P(),
    )
    return jax.shard_map(
        on_device,
        mesh=mesh,
        in_specs=placed,
        out_specs=(P(both, "tile", None), P("tile", both)),
        check_vma=False,
    )
```

```python
import math

import jax
import jax.numpy as jnp
from jax import lax
from jax.experimental import pallas as pl
from jax.experimental.pallas import tpu as pltpu
from jax.sharding import PartitionSpec as P

F32 = jnp.float32
BF16 = jnp.bfloat16
RADIUS = 2
STEP_SIZE = 0.25
GROUPS = 8
LOCAL = 10
ROWS = 32
LANES = 128
COLS = 1024
REACH = 4 * RADIUS
EDGE = REACH + 3
TALL = ROWS + 2 * REACH
WIDE = LANES + 2 * REACH
SLOTS = 12
SPARE = LOCAL * WIDE - (SLOTS - 1) * LANES
HALO = 136
MID = 24
RIM = (TALL - MID) // 2
VMEM = 48 * 1024 * 1024
ALL_VMEM = 60 * 1024 * 1024


def lane_ids(rows):
    return lax.broadcasted_iota(jnp.int32, (rows, LANES), 1)


def pieces(value, count):
    found = []
    for _ in range(count):
        part = value.astype(BF16)
        found.append(part)
        value = value - part.astype(F32)
    return found


def set_coefs(courants, coefs, rows):
    @pl.loop(0, GROUPS)
    def _(block):
        for low in rows:
            span = slice(low, low + 8)
            cx = courants[0, block, span, :]
            cy = courants[1, block, span, :]
            x_plus, x_minus = jnp.maximum(cx, 0.0), jnp.minimum(cx, 0.0)
            y_plus, y_minus = jnp.maximum(cy, 0.0), jnp.minimum(cy, 0.0)
            coefs[0, block, span, :] = 1.0 - x_plus + x_minus - y_plus + y_minus
            coefs[1, block, span, :] = x_plus
            coefs[2, block, span, :] = -x_minus
            coefs[3, block, span, :] = y_plus
            coefs[4, block, span, :] = -y_minus


def clear_sides(buffers):
    for buffer in buffers:
        nothing = jnp.zeros(buffer.shape[2:], F32)
        for member in range(LOCAL):
            for side in (0, GROUPS + 1):
                buffer[member, side] = nothing


def advance(source, target, coefs, starts, homes=None):
    homes = starts if homes is None else homes
    lane = lane_ids(8)
    first, last = lane == 0, lane == LANES - 1

    @pl.loop(0, GROUPS)
    def _(block):
        for low, home in zip(starts, homes):
            rows = slice(low, low + 8)
            k_mid, k_up, k_down, k_left, k_right = (coefs[kind, block, rows, :] for kind in range(5))
            for member in range(LOCAL):
                mid = source[member, block + 1, rows, :]
                before = source[member, block, rows, :]
                after = source[member, block + 2, rows, :]
                target[member, block + 1, home : home + 8, :] = (
                    k_mid * mid
                    + k_up * source[member, block + 1, low - 1 : low + 7, :]
                    + k_down * source[member, block + 1, low + 1 : low + 9, :]
                    + k_left * pltpu.roll(jnp.where(last, before, mid), 1, 1)
                    + k_right * pltpu.roll(jnp.where(first, after, mid), LANES - 1, 1)
                )


def send_plan():
    plan = [[] for _ in range(SLOTS)]
    for member in range(LOCAL):
        start = member * WIDE
        spans = (
            (start, start + REACH, -1),
            (start + REACH, start + REACH + LANES, 0),
            (start + REACH + LANES, start + WIDE, 1),
        )
        for low, high, offset in spans:
            while low < high:
                slot = low // LANES
                stop = min(high, (slot + 1) * LANES)
                plan[slot].append((member, offset, low - slot * LANES, stop - slot * LANES))
                low = stop
    return plan


def pack(final, fields, rolled, blocks, send, sems):
    @pl.loop(0, GROUPS)
    def _(block):
        for member in range(LOCAL):
            shift = (member * WIDE + REACH) % LANES
            value = final[member, block + 1, 0:MID, :]
            rolled[member, block + 1] = pltpu.roll(value, shift, 1) if shift else value

    lane = lane_ids(MID)
    ends = jnp.where(
        lane < SPARE + 2 * REACH,
        pltpu.roll(fields[0], SPARE + REACH, 1),
        pltpu.roll(fields[1], SPARE + 3 * REACH, 1),
    )
    plan = send_plan()

    @pl.loop(0, GROUPS)
    def _(block):
        for slot in range(SLOTS):
            value = ends if slot == SLOTS - 1 else None
            for member, offset, low, high in plan[slot]:
                part = rolled[member, block + 1 + offset]
                if value is None:
                    value = part
                else:
                    value = jnp.where((lane >= low) & (lane < high), part, value)
            blocks[block, slot] = value
        pltpu.make_async_copy(blocks.at[block], send.at[block], sems.at[block]).start()


def finish_pack(blocks, send, sems):
    for block in range(GROUPS):
        pltpu.make_async_copy(blocks.at[block], send.at[block], sems.at[block]).wait()


def message_kernel(
    members, courant_x, courant_y, cell, innov, weight,
    up, down, fields, own, courants, cells, values, member_sems, sems,
):
    small = [
        pltpu.make_async_copy(cell, cells, sems.at[0]),
        pltpu.make_async_copy(innov, values.at[0], sems.at[1]),
        pltpu.make_async_copy(weight, values.at[1], sems.at[2]),
    ]
    large = [
        pltpu.make_async_copy(members, own, member_sems.at[0]),
        pltpu.make_async_copy(courant_x, courants.at[0], member_sems.at[1]),
        pltpu.make_async_copy(courant_y, courants.at[1], member_sems.at[2]),
    ]
    for copy in small + large:
        copy.start()
    for copy in small:
        copy.wait()

    row_hit = lax.broadcasted_iota(jnp.int32, (ROWS, 1024), 0) == lax.shift_right_logical(cells[0], 7)
    col_hit = lax.broadcasted_iota(jnp.int32, (LANES, 1024), 0) == lax.bitwise_and(
        cells[0], LANES - 1
    )
    parts = pieces(values[1, 0] * values[0, 0], 3) + pieces(values[1, 0], 3)
    hits = row_hit.astype(F32)
    left = jnp.concatenate([(hits * part.astype(F32)).astype(BF16) for part in parts], axis=0)
    sums = lax.dot_general(
        left, col_hit.astype(F32).astype(BF16), (((1,), (1,)), ((), ())), preferred_element_type=F32
    )
    for kind in range(2):
        base = 3 * ROWS * kind
        fields[kind] = (
            sums[base : base + ROWS]
            + sums[base + ROWS : base + 2 * ROWS]
            + sums[base + 2 * ROWS : base + 3 * ROWS]
        )
    base = (LOCAL + 2) * EDGE
    for row in range(REACH):
        for kind in range(2):
            up[row, base + kind : base + kind + 1, :] = fields[kind, row : row + 1, :]
            down[row, base + kind : base + kind + 1, :] = fields[
                kind, ROWS - REACH + row : ROWS - REACH + row + 1, :
            ]
        up[row, base + 2 : HALO, :] = jnp.zeros((HALO - base - 2, LANES), F32)
        down[row, base + 2 : HALO, :] = jnp.zeros((HALO - base - 2, LANES), F32)
    for copy in large:
        copy.wait()
    for field in range(LOCAL + 2):
        span = slice(field * EDGE, (field + 1) * EDGE)
        source = own.at[field] if field < LOCAL else courants.at[field - LOCAL]
        first, last = source[0:EDGE, :], source[ROWS - EDGE : ROWS, :]
        for block in range(GROUPS):
            lanes = slice(block * LANES, (block + 1) * LANES)
            up[block, span, :] = first[:, lanes]
            down[block, span, :] = last[:, lanes]


TOP = 16
HEIGHT = 56


def inner_kernel(
    members, courant_x, courant_y, fields, out, send,
    old, new, courants, coefs, rolled, final, blocks, member_sems, wind_sems, sems,
):
    own = slice(TOP, TOP + ROWS)
    large, wind = [], []
    for block in range(GROUPS):
        lanes = slice(block * LANES, (block + 1) * LANES)
        for kind, source in enumerate((courant_x, courant_y)):
            wind.append(
                pltpu.make_async_copy(
                    source.at[:, lanes], courants.at[kind, block, own, :], wind_sems.at[kind, block]
                )
            )
        large.append(
            pltpu.make_async_copy(
                members.at[:, :, lanes], old.at[:, block + 1, own, :], member_sems.at[block]
            )
        )
    for copy in wind + large:
        copy.start()
    clear_sides((old, new, rolled))
    for copy in wind:
        copy.wait()
    set_coefs(courants, coefs, range(TOP, TOP + ROWS, 8))
    for copy in large:
        copy.wait()
    advance(old, new, coefs, range(TOP, TOP + ROWS, 8))
    advance(new, old, coefs, range(TOP, TOP + ROWS, 8))
    skip = (ROWS - MID) // 2
    advance(old, final, coefs, range(TOP + skip, TOP + skip + MID, 8), range(0, MID, 8))
    whole = pltpu.make_async_copy(final.at[:, pl.ds(1, GROUPS), pl.ds(0, MID), :], out, sems.at[GROUPS])
    whole.start()
    middle = [fields[kind, skip : skip + MID, :] for kind in range(2)]
    pack(final, middle, rolled, blocks, send, sems)
    finish_pack(blocks, send, sems)
    whole.wait()


LOW = 8


def outer_kernel(
    members, courant_x, courant_y, above, below, fields,
    out, send, fields_tall,
    old, new, courants, coefs, rolled, final, blocks, rims, member_sems, wind_sems, sems,
):
    top, end = slice(TOP, TOP + 8), slice(ROWS - 8 + LOW, ROWS + LOW)
    copies = []
    for block in range(GROUPS):
        lanes = slice(block * LANES, (block + 1) * LANES)
        for part, span in enumerate((top, end)):
            rows = slice(0, 8) if part == 0 else slice(ROWS - 8, ROWS)
            copies.append(
                pltpu.make_async_copy(
                    members.at[:, rows, lanes], old.at[:, block + 1, span, :],
                    member_sems.at[part, block],
                )
            )
            for kind, source in enumerate((courant_x, courant_y)):
                copies.append(
                    pltpu.make_async_copy(
                        source.at[rows, lanes], courants.at[kind, block, span, :],
                        wind_sems.at[kind, part, block],
                    )
                )
    for copy in copies:
        copy.start()
    clear_sides((old, new, rolled))
    base = (LOCAL + 2) * EDGE

    @pl.loop(0, GROUPS)
    def _(block):
        for field in range(LOCAL + 2):
            span = slice(field * EDGE, (field + 1) * EDGE)
            before, after = above[block, span, :], below[block, span, :]
            if field < LOCAL:
                old[field, block + 1, TOP - EDGE : TOP, :] = before
                old[field, block + 1, ROWS + LOW : ROWS + LOW + EDGE, :] = after
            else:
                courants[field - LOCAL, block, TOP - EDGE : TOP, :] = before
                courants[field - LOCAL, block, ROWS + LOW : ROWS + LOW + EDGE, :] = after

    for kind in range(2):
        for row in range(REACH):
            fields_tall[kind, row : row + 1, :] = above[row, base + kind : base + kind + 1, :]
            fields_tall[kind, REACH + ROWS + row : REACH + ROWS + row + 1, :] = below[
                row, base + kind : base + kind + 1, :
            ]
        fields_tall[kind, REACH : REACH + ROWS, :] = fields[kind]
        rims[kind, 0:RIM, :] = fields_tall[kind, 0:RIM, :]
        rims[kind, RIM:MID, :] = fields_tall[kind, TALL - RIM : TALL, :]
    for copy in copies:
        copy.wait()
    set_coefs(courants, coefs, range(0, HEIGHT, 8))
    for step in range(3):
        high, low = TOP - EDGE + 1 + step, ROWS - 6 + step + LOW
        starts = (high, high + 8, low, low + 8)
        if step < 2:
            pair = (old, new) if step == 0 else (new, old)
            advance(*pair, coefs, starts)
        else:
            advance(old, final, coefs, starts, (0, 8, RIM, RIM + 8))
    whole = pltpu.make_async_copy(
        final.at[:, pl.ds(1, GROUPS), pl.ds(REACH, 8), :], out, sems.at[GROUPS]
    )
    whole.start()
    pack(final, rims, rolled, blocks, send, sems)
    finish_pack(blocks, send, sems)
    whole.wait()


COPIES = 4
DEEP = 56
MID_ROWS = ((RIM, 0, MID),)
RIM_ROWS = ((0, 0, RIM), (TALL - RIM, RIM, RIM))


def member_place(member):
    return member * WIDE // LANES, member * WIDE % LANES


def folded(slots, lane):
    near, far = None, None
    for member in range(LOCAL):
        base, shift = member_place(member)
        here, there = slots(base), slots(base + 1)
        if shift:
            here = pltpu.roll(jnp.where(lane >= shift, here, there), LANES - shift, 1)
            there = pltpu.roll(there, LANES - shift, 1)
        near = here if near is None else near + here
        far = there if far is None else far + there
    return near, far


def spread_out(near, far, lane, store):
    slots = [None] * SLOTS
    for member in range(LOCAL):
        base, shift = member_place(member)
        moved = pltpu.roll(near, shift, 1) if shift else near
        tail = pltpu.roll(far, shift, 1) if shift else far
        slots[base] = moved if slots[base] is None else jnp.where(lane >= shift, moved, slots[base])
        slots[base + 1] = jnp.where(
            lane < shift, moved, jnp.where(lane < shift + 2 * REACH, tail, 0.0)
        )
    for slot in range(SLOTS):
        store(slot, slots[slot])


def shifted(before, mid, after, lane):
    found = {0: mid}
    for shift in (1, 2):
        found[shift] = pltpu.roll(jnp.where(lane < shift, after, mid), LANES - shift, 1)
        found[-shift] = pltpu.roll(jnp.where(lane >= LANES - shift, before, mid), shift, 1)
    return found


def put(target, span, found):
    for shift, value in found.items():
        target[RADIUS + shift, span, :] = value


def analysis_kernel(
    place, offsets, weights, got_mid, got_rim, fields, increment, spread_copies,
    spread, averages, gains, inside, total, plane, ends, *copies,
):
    first_copies, second_copies = copies[: len(copies) // 2], copies[len(copies) // 2 :]
    tile, block = place[0], place[1]
    lane = lane_ids(TALL)
    entries = offsets.shape[0]
    tap_row = [offsets[entry, 0] for entry in range(entries)]
    tap_col = [offsets[entry, 1] for entry in range(entries)]
    tap = [weights[entry] for entry in range(entries)]
    weight_sum = tap[0]
    for entry in range(1, entries):
        weight_sum = weight_sum + tap[entry]
    scale = 1.0 / jnp.full((1, LANES), weight_sum, F32)
    scale = scale * scale

    @pl.loop(0, SLOTS)
    def _(slot):
        for got, parts in ((got_mid, MID_ROWS), (got_rim, RIM_ROWS)):
            value = got[0, slot]
            for source in range(1, GROUPS):
                value = value + got[source, slot]
            for here, there, count in parts:
                averages[slot, here : here + count, :] = value[there : there + count]

    near, far = folded(lambda slot: averages[slot], lane)
    count = GROUPS * LOCAL

    def store_average(slot, value):
        averages[slot] = value

    spread_out(near / count, far / count, lane, store_average)
    deviation = 1.0 / math.sqrt(count - 1)

    @pl.loop(0, SLOTS)
    def _(slot):
        for got, parts in ((got_mid, MID_ROWS), (got_rim, RIM_ROWS)):
            for here, there, count in parts:
                average = averages[slot, here : here + count, :]
                for source in range(GROUPS):
                    value = got[source, slot, there : there + count, :]
                    spread[source, slot, here : here + count, :] = (value - average) * deviation

    row = lax.broadcasted_iota(jnp.int32, (TALL, LANES), 0) + (tile * ROWS - REACH)
    col = lane + (block * LANES - REACH)
    row_ok = (row >= 0) & (row < ROWS * 32)
    near_ok = row_ok & (col >= 0) & (col < COLS)
    far_ok = row_ok & (col + LANES < COLS)

    def store_inside(slot, value):
        inside[slot, 0:TALL, :] = value
        inside[slot, TALL:DEEP, :] = jnp.zeros((DEEP - TALL, LANES), F32)

    spread_out(near_ok.astype(F32), far_ok.astype(F32), lane, store_inside)

    for got, parts in ((got_mid, MID_ROWS), (got_rim, RIM_ROWS)):
        for here, there, count in parts:
            rows = slice(there, there + count)
            ends[0, here : here + count, :] = got[jnp.maximum(block - 1, 0), SLOTS - 1, rows, :]
            ends[1, here : here + count, :] = got[
                jnp.minimum(block + 1, GROUPS - 1), SLOTS - 1, rows, :
            ]
    left_ends = jnp.where(block > 0, ends[0], 0.0)
    right_ends = jnp.where(block < GROUPS - 1, ends[1], 0.0)
    planes = []
    for kind in range(2):
        back = LANES - SPARE - 2 * REACH * kind
        own = pltpu.roll(fields[kind], REACH, 1)
        near = jnp.where(lane < REACH, pltpu.roll(left_ends, back, 1), own)
        far = jnp.where(lane < REACH, own, pltpu.roll(right_ends, back, 1))
        far = jnp.where(lane < 2 * REACH, far, 0.0)
        planes.append((near, far))

    def store_gain(slot, value):
        gains[slot] = value

    def taps(source, sign, low, rows):
        value = None
        for entry in range(entries):
            term = tap[entry] * source[
                RADIUS + sign * tap_col[entry], pl.ds(low + sign * tap_row[entry], rows), :
            ]
            value = term if value is None else value + term
        return value

    def sweep(slots, multiplier, y_rows, z_low, z_rows, x_low, x_rows, finish):
        y_span = slice(z_low - RADIUS, z_low - RADIUS + y_rows)
        z_span = slice(z_low, z_low + z_rows)
        y_lane, z_lane = lane_ids(y_rows), lane_ids(z_rows)
        products, localized = {}, {}

        def copies_of(held, slot, lane_here):
            mid = held[slot]
            return shifted(held.get(slot - 1, mid), mid, held.get(slot + 1, mid), lane_here)

        products[0], products[1] = multiplier(0, y_span), multiplier(1, y_span)
        put(first_copies[0], y_span, copies_of(products, 0, y_lane))
        for slot in range(slots + 3):
            if slot + 1 < slots:
                if slot + 2 < slots:
                    products[slot + 2] = multiplier(slot + 2, y_span)
                ahead = copies_of(products, slot + 1, y_lane)
            if slot < slots:
                value = taps(first_copies[slot % COPIES], -1, z_low, z_rows)
                localized[slot] = value * inside[slot, z_span, :]
            if slot + 1 < slots:
                put(first_copies[(slot + 1) % COPIES], y_span, ahead)
            if 1 < slot < slots + 2:
                behind = copies_of(localized, slot - 2, z_lane)
            if slot > 2:
                finish(slot - 3, taps(second_copies[(slot - 3) % COPIES], 1, x_low, x_rows))
            if 1 < slot < slots + 2:
                put(second_copies[(slot - 2) % COPIES], z_span, behind)

    def apply(near, far, y_rows, z_low, z_rows, x_low, x_rows):
        spread_out(near, far, lane, store_gain)
        ones = []

        def finish_ones(slot, value):
            plane[slot, 0:x_rows, :] = value

        sweep(2, lambda slot, rows: gains[slot, rows, :], y_rows, z_low, z_rows, x_low, x_rows, finish_ones)

        @pl.loop(0, SLOTS)
        def _(slot):
            total[slot, 0:x_rows, :] = jnp.zeros((x_rows, LANES), F32)

        @pl.loop(0, GROUPS)
        def _(source):
            def finish(slot, value):
                total[slot, 0:x_rows, :] += value * spread[source, slot, x_low : x_low + x_rows, :]

            sweep(
                SLOTS, lambda slot, rows: gains[slot, rows, :] * spread[source, slot, rows, :],
                y_rows, z_low, z_rows, x_low, x_rows, finish,
            )

        near, far = folded(lambda slot: total[slot, 0:x_rows, :], lane_ids(x_rows))
        return (near + plane[0, 0:x_rows, :]) * scale, (far + plane[1, 0:x_rows, :]) * scale

    (near_v, far_v), (near_w, far_w) = planes
    near, far = apply(near_v, far_v, 48, 2, 48, 4, 40)
    for part, value in enumerate((near, far)):
        plane[2 + part, 0:TALL, :] = jnp.zeros((TALL, LANES), F32)
        plane[2 + part, 4:44, :] = value
    near = (STEP_SIZE * near_w) * plane[2, 0:TALL, :] - (2.0 - STEP_SIZE) * near_v
    far = (STEP_SIZE * far_w) * plane[3, 0:TALL, :] - (2.0 - STEP_SIZE) * far_v
    far = jnp.where(lane < 2 * REACH, far, 0.0)
    near, far = apply(near, far, 40, 6, 40, 8, 32)
    short_lane = lane_ids(ROWS)
    result = pltpu.roll(jnp.where(short_lane < REACH, far, near), LANES - REACH, 1) * -STEP_SIZE
    increment[...] = result
    for target in range(GROUPS):
        spread_copies[target] = result


def recentre_kernel(middle, rim, increments, out):
    keep = (ROWS - MID) // 2
    for block in range(GROUPS):
        lanes = slice(block * LANES, (block + 1) * LANES)
        for member in range(LOCAL):
            out[member, 0:keep, lanes] = rim[member, block, 0:keep, :] + increments[block, 0:keep, :]
            out[member, keep : keep + MID, lanes] = (
                middle[member, block] + increments[block, keep : keep + MID, :]
            )
            out[member, keep + MID : ROWS, lanes] = (
                rim[member, block, keep : 2 * keep, :] + increments[block, keep + MID : ROWS, :]
            )


def on_vmem(count):
    return [pl.BlockSpec(memory_space=pltpu.VMEM)] * count


def in_hbm(count):
    return [pl.BlockSpec(memory_space=pltpu.HBM)] * count


def array(*shape):
    return jax.ShapeDtypeStruct(shape, F32)


def on_device(
    members, courant_x, courant_y, obs_cell, innovation, obs_weight, stencil_offsets, stencil_weights
):
    both = ("member", "grp")
    params = pltpu.CompilerParams(vmem_limit_bytes=VMEM)
    crowded = pltpu.CompilerParams(vmem_limit_bytes=ALL_VMEM)
    cost = pl.CostEstimate(flops=10_000_000, bytes_accessed=60_000_000, transcendentals=0)
    tiles = lax.axis_size("tile")
    keep = (ROWS - MID) // 2
    sems = pltpu.SemaphoreType.DMA
    buffers = [
        pltpu.VMEM((LOCAL, GROUPS + 2, HEIGHT, LANES), F32),
        pltpu.VMEM((LOCAL, GROUPS + 2, HEIGHT, LANES), F32),
        pltpu.VMEM((2, GROUPS, HEIGHT, LANES), F32),
        pltpu.VMEM((5, GROUPS, HEIGHT, LANES), F32),
        pltpu.VMEM((LOCAL, GROUPS + 2, MID, LANES), F32),
        pltpu.VMEM((LOCAL, GROUPS + 2, MID + 8, LANES), F32),
        pltpu.VMEM((GROUPS, SLOTS, MID, LANES), F32),
    ]
    up, down, fields = pl.pallas_call(
        message_kernel,
        out_shape=[array(GROUPS, HALO, LANES), array(GROUPS, HALO, LANES), array(2, ROWS, LANES)],
        in_specs=in_hbm(6),
        out_specs=on_vmem(3),
        scratch_shapes=[
            pltpu.VMEM(members.shape, F32),
            pltpu.VMEM((2, ROWS, COLS), F32),
            pltpu.VMEM((1, 1, 1024), jnp.int32),
            pltpu.VMEM((2, 1, 1, 1024), F32),
            sems((3,)),
            sems((3,)),
        ],
        compiler_params=crowded,
        name="messages",
    )(members, courant_x, courant_y, obs_cell, innovation, obs_weight)
    above = lax.ppermute(down, "tile", [(i, i + 1) for i in range(tiles - 1)])
    below = lax.ppermute(up, "tile", [(i + 1, i) for i in range(tiles - 1)])
    middle, send_mid = pl.pallas_call(
        inner_kernel,
        out_shape=[array(LOCAL, GROUPS, MID, LANES), array(GROUPS, SLOTS, MID, LANES)],
        in_specs=in_hbm(3) + on_vmem(1),
        out_specs=in_hbm(2),
        scratch_shapes=buffers + [sems((GROUPS,)), sems((2, GROUPS)), sems((GROUPS + 1,))],
        compiler_params=crowded,
        cost_estimate=cost,
        name="inner",
    )(members, courant_x, courant_y, fields)
    send_mid, above, below = lax.optimization_barrier((send_mid, above, below))
    got_mid = exchanged(send_mid, both)
    rim, send_rim, fields_tall = pl.pallas_call(
        outer_kernel,
        out_shape=[
            array(LOCAL, GROUPS, 2 * keep, LANES),
            array(GROUPS, SLOTS, MID, LANES),
            array(2, TALL, LANES),
        ],
        in_specs=in_hbm(3) + on_vmem(3),
        out_specs=in_hbm(2) + on_vmem(1),
        scratch_shapes=buffers
        + [
            pltpu.VMEM((2, MID, LANES), F32),
            sems((2, GROUPS)),
            sems((2, 2, GROUPS)),
            sems((GROUPS + 1,)),
        ],
        compiler_params=crowded,
        cost_estimate=cost,
        name="outer",
    )(members, courant_x, courant_y, above, below, fields)
    send_rim, got_mid = lax.optimization_barrier((send_rim, got_mid))
    got_rim = exchanged(send_rim, both)
    place = jnp.stack([lax.axis_index("tile"), lax.axis_index(both)]).astype(jnp.int32)
    increment, copies = pl.pallas_call(
        analysis_kernel,
        out_shape=[array(ROWS, LANES), array(GROUPS, ROWS, LANES)],
        in_specs=[pl.BlockSpec(memory_space=pltpu.SMEM)] * 3 + on_vmem(3),
        out_specs=on_vmem(2),
        scratch_shapes=[
            pltpu.VMEM((GROUPS, SLOTS, TALL, LANES), F32),
            pltpu.VMEM((SLOTS, TALL, LANES), F32),
            pltpu.VMEM((SLOTS, TALL, LANES), F32),
            pltpu.VMEM((SLOTS, DEEP, LANES), F32),
            pltpu.VMEM((SLOTS, TALL, LANES), F32),
            pltpu.VMEM((4, TALL, LANES), F32),
            pltpu.VMEM((2, TALL, LANES), F32),
        ]
        + [pltpu.VMEM((2 * RADIUS + 1, DEEP, LANES), F32)] * (2 * COPIES),
        compiler_params=params,
        name="analysis",
    )(place, stencil_offsets, stencil_weights, got_mid, got_rim, fields_tall)
    increments = lax.all_to_all(copies, both, 0, 0, tiled=True)
    analysis = pl.pallas_call(
        recentre_kernel,
        out_shape=array(*members.shape),
        in_specs=on_vmem(3),
        out_specs=pl.BlockSpec(memory_space=pltpu.VMEM),
        compiler_params=params,
        name="recentre",
    )(middle, rim, increments)
    return analysis, increment


def exchanged(blocks, axes):
    flat = blocks.reshape(GROUPS, -1, LANES)
    return lax.all_to_all(flat, axes, 0, 0, tiled=True).reshape(blocks.shape)


def solution(mesh):
    both = ("member", "grp")
    placed = (
        P(both, "tile", None),
        P("tile", None),
        P("tile", None),
        P("tile", both, None),
        P("tile", both, None),
        P("tile", both, None),
        P(),
        P(),
    )
    return jax.shard_map(
        on_device,
        mesh=mesh,
        in_specs=placed,
        out_specs=(P(both, "tile", None), P("tile", both)),
        check_vma=False,
    )
```

```python
import math

import jax
import jax.numpy as jnp
from jax import lax
from jax.experimental import pallas as pl
from jax.experimental.pallas import tpu as pltpu
from jax.sharding import PartitionSpec as P

F32 = jnp.float32
BF16 = jnp.bfloat16
RADIUS = 2
STEP_SIZE = 0.25
GROUPS = 8
LOCAL = 10
ROWS = 32
LANES = 128
COLS = 1024
REACH = 4 * RADIUS
EDGE = REACH + 3
TALL = ROWS + 2 * REACH
WIDE = LANES + 2 * REACH
SLOTS = 12
SPARE = LOCAL * WIDE - (SLOTS - 1) * LANES
HALO = 136
MID = 24
RIM = (TALL - MID) // 2
VMEM = 16 * 1024 * 1024
ALL_VMEM = 60 * 1024 * 1024


def lane_ids(rows):
    return lax.broadcasted_iota(jnp.int32, (rows, LANES), 1)


def pieces(value, count):
    found = []
    for _ in range(count):
        part = value.astype(BF16)
        found.append(part)
        value = value - part.astype(F32)
    return found


def set_coefs(courants, coefs, rows):
    @pl.loop(0, GROUPS)
    def _(block):
        for low in rows:
            span = slice(low, low + 8)
            cx = courants[0, block, span, :]
            cy = courants[1, block, span, :]
            x_plus, x_minus = jnp.maximum(cx, 0.0), jnp.minimum(cx, 0.0)
            y_plus, y_minus = jnp.maximum(cy, 0.0), jnp.minimum(cy, 0.0)
            coefs[0, block, span, :] = 1.0 - x_plus + x_minus - y_plus + y_minus
            coefs[1, block, span, :] = x_plus
            coefs[2, block, span, :] = -x_minus
            coefs[3, block, span, :] = y_plus
            coefs[4, block, span, :] = -y_minus


def clear_sides(buffers):
    for buffer in buffers:
        nothing = jnp.zeros(buffer.shape[2:], F32)
        for member in range(LOCAL):
            for side in (0, GROUPS + 1):
                buffer[member, side] = nothing


def advance(source, target, coefs, starts, homes=None):
    homes = starts if homes is None else homes
    lane = lane_ids(8)
    first, last = lane == 0, lane == LANES - 1

    @pl.loop(0, GROUPS, unroll=4)
    def _(block):
        for low, home in zip(starts, homes):
            rows = slice(low, low + 8)
            k_mid, k_up, k_down, k_left, k_right = (coefs[kind, block, rows, :] for kind in range(5))
            for member in range(LOCAL):
                mid = source[member, block + 1, rows, :]
                before = source[member, block, rows, :]
                after = source[member, block + 2, rows, :]
                target[member, block + 1, home : home + 8, :] = (
                    k_mid * mid
                    + k_up * source[member, block + 1, low - 1 : low + 7, :]
                    + k_down * source[member, block + 1, low + 1 : low + 9, :]
                    + k_left * pltpu.roll(jnp.where(last, before, mid), 1, 1)
                    + k_right * pltpu.roll(jnp.where(first, after, mid), LANES - 1, 1)
                )


def send_plan():
    plan = [[] for _ in range(SLOTS)]
    for member in range(LOCAL):
        start = member * WIDE
        spans = (
            (start, start + REACH, -1),
            (start + REACH, start + REACH + LANES, 0),
            (start + REACH + LANES, start + WIDE, 1),
        )
        for low, high, offset in spans:
            while low < high:
                slot = low // LANES
                stop = min(high, (slot + 1) * LANES)
                plan[slot].append((member, offset, low - slot * LANES, stop - slot * LANES))
                low = stop
    return plan


def pack(final, fields, rolled, blocks, send, sems):
    @pl.loop(0, GROUPS, unroll=8)
    def _(block):
        for member in range(LOCAL):
            shift = (member * WIDE + REACH) % LANES
            value = final[member, block + 1, 0:MID, :]
            rolled[member, block + 1] = pltpu.roll(value, shift, 1) if shift else value

    lane = lane_ids(MID)
    ends = jnp.where(
        lane < SPARE + 2 * REACH,
        pltpu.roll(fields[0], SPARE + REACH, 1),
        pltpu.roll(fields[1], SPARE + 3 * REACH, 1),
    )
    plan = send_plan()

    @pl.loop(0, GROUPS)
    def _(block):
        for slot in range(SLOTS):
            value = ends if slot == SLOTS - 1 else None
            for member, offset, low, high in plan[slot]:
                part = rolled[member, block + 1 + offset]
                if value is None:
                    value = part
                else:
                    value = jnp.where((lane >= low) & (lane < high), part, value)
            blocks[block, slot] = value
        pltpu.make_async_copy(blocks.at[block], send.at[block], sems.at[block]).start()


def finish_pack(blocks, send, sems):
    for block in range(GROUPS):
        pltpu.make_async_copy(blocks.at[block], send.at[block], sems.at[block]).wait()


def message_kernel(
    members, courant_x, courant_y, cell, innov, weight,
    up, down, fields, own, courants, cells, values, member_sems, sems,
):
    small = [
        pltpu.make_async_copy(cell, cells, sems.at[0]),
        pltpu.make_async_copy(innov, values.at[0], sems.at[1]),
        pltpu.make_async_copy(weight, values.at[1], sems.at[2]),
    ]
    large = [
        pltpu.make_async_copy(members, own, member_sems.at[0]),
        pltpu.make_async_copy(courant_x, courants.at[0], member_sems.at[1]),
        pltpu.make_async_copy(courant_y, courants.at[1], member_sems.at[2]),
    ]
    for copy in small + large:
        copy.start()
    for copy in small:
        copy.wait()

    row_hit = lax.broadcasted_iota(jnp.int32, (ROWS, 1024), 0) == lax.shift_right_logical(cells[0], 7)
    col_hit = lax.broadcasted_iota(jnp.int32, (LANES, 1024), 0) == lax.bitwise_and(
        cells[0], LANES - 1
    )
    parts = pieces(values[1, 0] * values[0, 0], 3) + pieces(values[1, 0], 3)
    hits = row_hit.astype(F32)
    left = jnp.concatenate([(hits * part.astype(F32)).astype(BF16) for part in parts], axis=0)
    sums = lax.dot_general(
        left, col_hit.astype(F32).astype(BF16), (((1,), (1,)), ((), ())), preferred_element_type=F32
    )
    for kind in range(2):
        base = 3 * ROWS * kind
        fields[kind] = (
            sums[base : base + ROWS]
            + sums[base + ROWS : base + 2 * ROWS]
            + sums[base + 2 * ROWS : base + 3 * ROWS]
        )
    base = (LOCAL + 2) * EDGE
    for row in range(REACH):
        for kind in range(2):
            up[row, base + kind : base + kind + 1, :] = fields[kind, row : row + 1, :]
            down[row, base + kind : base + kind + 1, :] = fields[
                kind, ROWS - REACH + row : ROWS - REACH + row + 1, :
            ]
        up[row, base + 2 : HALO, :] = jnp.zeros((HALO - base - 2, LANES), F32)
        down[row, base + 2 : HALO, :] = jnp.zeros((HALO - base - 2, LANES), F32)
    for copy in large:
        copy.wait()
    for field in range(LOCAL + 2):
        span = slice(field * EDGE, (field + 1) * EDGE)
        source = own.at[field] if field < LOCAL else courants.at[field - LOCAL]
        first, last = source[0:EDGE, :], source[ROWS - EDGE : ROWS, :]
        for block in range(GROUPS):
            lanes = slice(block * LANES, (block + 1) * LANES)
            up[block, span, :] = first[:, lanes]
            down[block, span, :] = last[:, lanes]


TOP = 16
HEIGHT = 56


def inner_kernel(
    members, courant_x, courant_y, fields, out, send,
    old, new, courants, coefs, rolled, final, blocks, member_sems, wind_sems, sems,
):
    own = slice(TOP, TOP + ROWS)
    large, wind = [], []
    for block in range(GROUPS):
        lanes = slice(block * LANES, (block + 1) * LANES)
        for kind, source in enumerate((courant_x, courant_y)):
            wind.append(
                pltpu.make_async_copy(
                    source.at[:, lanes], courants.at[kind, block, own, :], wind_sems.at[kind, block]
                )
            )
        large.append(
            pltpu.make_async_copy(
                members.at[:, :, lanes], old.at[:, block + 1, own, :], member_sems.at[block]
            )
        )
    for copy in wind + large:
        copy.start()
    clear_sides((old, new, rolled))
    for copy in wind:
        copy.wait()
    set_coefs(courants, coefs, range(TOP, TOP + ROWS, 8))
    for copy in large:
        copy.wait()
    advance(old, new, coefs, range(TOP, TOP + ROWS, 8))
    advance(new, old, coefs, range(TOP, TOP + ROWS, 8))
    skip = (ROWS - MID) // 2
    advance(old, final, coefs, range(TOP + skip, TOP + skip + MID, 8), range(0, MID, 8))
    whole = pltpu.make_async_copy(final.at[:, pl.ds(1, GROUPS), pl.ds(0, MID), :], out, sems.at[GROUPS])
    whole.start()
    middle = [fields[kind, skip : skip + MID, :] for kind in range(2)]
    pack(final, middle, rolled, blocks, send, sems)
    finish_pack(blocks, send, sems)
    whole.wait()


LOW = 8


def outer_kernel(
    members, courant_x, courant_y, above, below, fields,
    out, send, fields_tall,
    old, new, courants, coefs, rolled, final, blocks, rims, member_sems, wind_sems, sems,
):
    top, end = slice(TOP, TOP + 8), slice(ROWS - 8 + LOW, ROWS + LOW)
    copies = []
    for block in range(GROUPS):
        lanes = slice(block * LANES, (block + 1) * LANES)
        for part, span in enumerate((top, end)):
            rows = slice(0, 8) if part == 0 else slice(ROWS - 8, ROWS)
            copies.append(
                pltpu.make_async_copy(
                    members.at[:, rows, lanes], old.at[:, block + 1, span, :],
                    member_sems.at[part, block],
                )
            )
            for kind, source in enumerate((courant_x, courant_y)):
                copies.append(
                    pltpu.make_async_copy(
                        source.at[rows, lanes], courants.at[kind, block, span, :],
                        wind_sems.at[kind, part, block],
                    )
                )
    for copy in copies:
        copy.start()
    clear_sides((old, new, rolled))
    base = (LOCAL + 2) * EDGE

    @pl.loop(0, GROUPS)
    def _(block):
        for field in range(LOCAL + 2):
            span = slice(field * EDGE, (field + 1) * EDGE)
            before, after = above[block, span, :], below[block, span, :]
            if field < LOCAL:
                old[field, block + 1, TOP - EDGE : TOP, :] = before
                old[field, block + 1, ROWS + LOW : ROWS + LOW + EDGE, :] = after
            else:
                courants[field - LOCAL, block, TOP - EDGE : TOP, :] = before
                courants[field - LOCAL, block, ROWS + LOW : ROWS + LOW + EDGE, :] = after

    for kind in range(2):
        for row in range(REACH):
            fields_tall[kind, row : row + 1, :] = above[row, base + kind : base + kind + 1, :]
            fields_tall[kind, REACH + ROWS + row : REACH + ROWS + row + 1, :] = below[
                row, base + kind : base + kind + 1, :
            ]
        fields_tall[kind, REACH : REACH + ROWS, :] = fields[kind]
        rims[kind, 0:RIM, :] = fields_tall[kind, 0:RIM, :]
        rims[kind, RIM:MID, :] = fields_tall[kind, TALL - RIM : TALL, :]
    for copy in copies:
        copy.wait()
    set_coefs(courants, coefs, range(0, HEIGHT, 8))
    for step in range(3):
        high, low = TOP - EDGE + 1 + step, ROWS - 6 + step + LOW
        starts = (high, high + 8, low, low + 8)
        if step < 2:
            pair = (old, new) if step == 0 else (new, old)
            advance(*pair, coefs, starts)
        else:
            advance(old, final, coefs, starts, (0, 8, RIM, RIM + 8))
    whole = pltpu.make_async_copy(
        final.at[:, pl.ds(1, GROUPS), pl.ds(REACH, 8), :], out, sems.at[GROUPS]
    )
    whole.start()
    pack(final, rims, rolled, blocks, send, sems)
    finish_pack(blocks, send, sems)
    whole.wait()


COPIES = 4
DEEP = 56


def member_place(member):
    return member * WIDE // LANES, member * WIDE % LANES


def folded(slots, lane):
    near, far = None, None
    for member in range(LOCAL):
        base, shift = member_place(member)
        here, there = slots(base), slots(base + 1)
        if shift:
            here = pltpu.roll(jnp.where(lane >= shift, here, there), LANES - shift, 1)
            there = pltpu.roll(there, LANES - shift, 1)
        near = here if near is None else near + here
        far = there if far is None else far + there
    return near, far


def spread_out(near, far, lane, store):
    slots = [None] * SLOTS
    for member in range(LOCAL):
        base, shift = member_place(member)
        moved = pltpu.roll(near, shift, 1) if shift else near
        tail = pltpu.roll(far, shift, 1) if shift else far
        slots[base] = moved if slots[base] is None else jnp.where(lane >= shift, moved, slots[base])
        slots[base + 1] = jnp.where(
            lane < shift, moved, jnp.where(lane < shift + 2 * REACH, tail, 0.0)
        )
    for slot in range(SLOTS):
        store(slot, slots[slot])


def shifted(before, mid, after, lane):
    found = {0: mid}
    for shift in (1, 2):
        found[shift] = pltpu.roll(jnp.where(lane < shift, after, mid), LANES - shift, 1)
        found[-shift] = pltpu.roll(jnp.where(lane >= LANES - shift, before, mid), shift, 1)
    return found


def put(target, span, found):
    for shift, value in found.items():
        target[RADIUS + shift, span, :] = value


def localizer(offsets, weights, inside, copies):
    entries = offsets.shape[0]
    tap_row = [offsets[entry, 0] for entry in range(entries)]
    tap_col = [offsets[entry, 1] for entry in range(entries)]
    tap = [weights[entry] for entry in range(entries)]
    weight_sum = tap[0]
    for entry in range(1, entries):
        weight_sum = weight_sum + tap[entry]
    scale = 1.0 / jnp.full((1, LANES), weight_sum, F32)
    first_copies, second_copies = copies[: len(copies) // 2], copies[len(copies) // 2 :]

    def taps(source, sign, low, rows):
        value = None
        for entry in range(entries):
            term = tap[entry] * source[
                RADIUS + sign * tap_col[entry], pl.ds(low + sign * tap_row[entry], rows), :
            ]
            value = term if value is None else value + term
        return value

    def sweep(slots, multiplier, bands, finish):
        def copies_of(held, slot):
            found = []
            for at, mid in enumerate(held[slot]):
                before = held.get(slot - 1, held[slot])[at]
                after = held.get(slot + 1, held[slot])[at]
                found.append(shifted(before, mid, after, lane_ids(mid.shape[0])))
            return found

        def put_all(target, found, kind):
            for band, values in zip(bands, found):
                low, rows = band[kind]
                put(target, slice(low, low + rows), values)

        def entering(slot):
            return [multiplier(slot, slice(band[0][0], sum(band[0]))) for band in bands]

        products, localized = {0: entering(0), 1: entering(1)}, {}
        put_all(first_copies[0], copies_of(products, 0), 0)
        for slot in range(slots + 3):
            if slot + 1 < slots:
                if slot + 2 < slots:
                    products[slot + 2] = entering(slot + 2)
                ahead = copies_of(products, slot + 1)
            if slot < slots:
                localized[slot] = [
                    taps(first_copies[slot % COPIES], -1, *band[1])
                    * inside[slot, band[1][0] : sum(band[1]), :]
                    for band in bands
                ]
            if slot + 1 < slots:
                put_all(first_copies[(slot + 1) % COPIES], ahead, 0)
            if 1 < slot < slots + 2:
                behind = copies_of(localized, slot - 2)
            if slot > 2:
                done = slot - 3
                finish(done, [taps(second_copies[done % COPIES], 1, *band[2]) for band in bands])
            if 1 < slot < slots + 2:
                put_all(second_copies[(slot - 2) % COPIES], behind, 1)

    return sweep, scale * scale


def applied(sweep, scale, near, far, bands, spread, gains, total, plane):
    spots, rows = [], 0
    for band in bands:
        spots.append((slice(rows, rows + band[2][1]), slice(band[2][0], sum(band[2]))))
        rows += band[2][1]

    def store_gain(slot, value):
        gains[slot] = value

    spread_out(near, far, lane_ids(near.shape[0]), store_gain)

    def finish_ones(slot, values):
        for (here, _), value in zip(spots, values):
            plane[slot, here, :] = value

    sweep(2, lambda slot, span: gains[slot, span, :], bands, finish_ones)

    @pl.loop(0, SLOTS)
    def _(slot):
        total[slot, 0:rows, :] = jnp.zeros((rows, LANES), F32)

    @pl.loop(0, GROUPS)
    def _(source):
        def finish(slot, values):
            for (here, there), value in zip(spots, values):
                total[slot, here, :] += value * spread(source, slot, there)

        sweep(
            SLOTS, lambda slot, span: gains[slot, span, :] * spread(source, slot, span),
            bands, finish,
        )

    near, far = folded(lambda slot: total[slot, 0:rows, :], lane_ids(rows))
    return (near + plane[0, 0:rows, :]) * scale, (far + plane[1, 0:rows, :]) * scale


def set_spread(got, parts, averages, spread):
    count = GROUPS * LOCAL
    deviation = 1.0 / math.sqrt(count - 1)
    rows = parts[0][2] * len(parts)

    @pl.loop(0, SLOTS)
    def _(slot):
        value = got[0, slot]
        for source in range(1, GROUPS):
            value = value + got[source, slot]
        averages[slot, 0:rows, :] = value

    lane = lane_ids(rows)
    near, far = folded(lambda slot: averages[slot, 0:rows, :], lane)

    def store_average(slot, value):
        averages[slot, 0:rows, :] = value

    spread_out(near / count, far / count, lane, store_average)

    @pl.loop(0, SLOTS)
    def _(slot):
        average = averages[slot, 0:rows, :]
        for source in range(GROUPS):
            value = (got[source, slot] - average) * deviation
            for here, there, number in parts:
                spread[source, slot, here : here + number, :] = value[there : there + number]


def block_ends(got, parts, block, ends):
    for here, there, count in parts:
        rows = slice(there, there + count)
        ends[0, here : here + count, :] = got[jnp.maximum(block - 1, 0), SLOTS - 1, rows, :]
        ends[1, here : here + count, :] = got[
            jnp.minimum(block + 1, GROUPS - 1), SLOTS - 1, rows, :
        ]


def with_margins(own, kind, block, ends, rows):
    lane = lane_ids(rows.stop - rows.start)
    back = LANES - SPARE - 2 * REACH * kind
    left_ends = jnp.where(block > 0, ends[0, rows, :], 0.0)
    right_ends = jnp.where(block < GROUPS - 1, ends[1, rows, :], 0.0)
    own = pltpu.roll(own, REACH, 1)
    near = jnp.where(lane < REACH, pltpu.roll(left_ends, back, 1), own)
    far = jnp.where(lane < REACH, own, pltpu.roll(right_ends, back, 1))
    return near, jnp.where(lane < 2 * REACH, far, 0.0)


EARLY = 16
EARLY_BAND = ((RIM, MID), (RIM + RADIUS, MID), (RIM + 2 * RADIUS, EARLY))


SPREAD_ROWS = GROUPS * SLOTS * MID
SHARED = SLOTS + 5


def handed_on(rows):
    spread = rows.at[pl.ds(0, SPREAD_ROWS)].reshape(GROUPS, SLOTS, MID, LANES)
    return spread, rows.at[pl.ds(SPREAD_ROWS, SHARED * TALL)].reshape(SHARED, TALL, LANES)


def early_kernel(
    place, offsets, weights, got, fields, handed,
    averages, gains, total, plane, ends, *copies,
):
    spread, shared = handed_on(handed)
    tile, block = place[0], place[1]
    lane = lane_ids(TALL)
    set_spread(got, ((0, 0, MID),), averages, spread)

    row = lax.broadcasted_iota(jnp.int32, (TALL, LANES), 0) + (tile * ROWS - REACH)
    col = lane + (block * LANES - REACH)
    row_ok = (row >= 0) & (row < ROWS * 32)
    near_ok = row_ok & (col >= 0) & (col < COLS)
    far_ok = row_ok & (col + LANES < COLS)

    def store_inside(slot, value):
        shared[slot] = value

    spread_out(near_ok.astype(F32), far_ok.astype(F32), lane, store_inside)
    sweep, scale = localizer(offsets, weights, shared, copies)
    ends[...] = jnp.zeros(ends.shape, F32)
    block_ends(got, ((RIM, 0, MID),), block, ends)
    near, far = with_margins(fields[0], 0, block, ends, slice(0, TALL))

    def at(source, slot, rows):
        return spread[source, slot, rows.start - RIM : rows.stop - RIM, :]

    near, far = applied(sweep, scale, near, far, (EARLY_BAND,), at, gains, total, plane)
    for part, value in enumerate((near, far)):
        shared[SLOTS, part * EARLY : (part + 1) * EARLY, :] = value
    shared[SLOTS, 2 * EARLY : TALL, :] = jnp.zeros((TALL - 2 * EARLY, LANES), F32)
    for kind in range(2):
        shared[SLOTS + 1 + kind] = ends[kind]
        shared[SLOTS + 3 + kind] = fields[kind]


RIM_BANDS = (
    ((0, MID), (RADIUS, EARLY), (2 * RADIUS, EARLY)),
    ((MID, MID), (TALL - RADIUS - EARLY, EARLY), (TALL - 2 * RADIUS - EARLY, EARLY)),
)
LAST_BAND = ((2 * RADIUS, 40), (3 * RADIUS, 40), (REACH, ROWS))


def analysis_kernel(
    place, offsets, weights, got, handed, increment, spread_copies,
    spread, averages, gains, total, plane, ends, *copies,
):
    spread_mid, shared = handed_on(handed)
    block = place[1]
    set_spread(got, ((0, 0, RIM), (TALL - RIM, RIM, RIM)), averages, spread)

    @pl.loop(0, SLOTS)
    def _(slot):
        for source in range(GROUPS):
            spread[source, slot, RIM : RIM + MID, :] = spread_mid[source, slot]

    def at(source, slot, rows):
        return spread[source, slot, rows, :]

    sweep, scale = localizer(offsets, weights, shared, copies)
    for kind in range(2):
        ends[kind] = shared[SLOTS + 1 + kind]
    block_ends(got, ((0, 0, RIM), (TALL - RIM, RIM, RIM)), block, ends)
    rows = slice(0, TALL)
    near_v, far_v = with_margins(shared[SLOTS + 3], 0, block, ends, rows)
    near_w, far_w = with_margins(shared[SLOTS + 4], 1, block, ends, rows)

    values = applied(sweep, scale, near_v, far_v, RIM_BANDS, at, gains, total, plane)
    for part in range(2):
        plane[2 + part] = jnp.zeros((TALL, LANES), F32)
        low = 2 * RADIUS
        plane[2 + part, low : low + EARLY, :] = values[part][0:EARLY]
        plane[2 + part, TALL - low - EARLY : TALL - low, :] = values[part][EARLY : 2 * EARLY]
        plane[2 + part, RIM + low : RIM + low + EARLY, :] = shared[
            SLOTS, part * EARLY : (part + 1) * EARLY, :
        ]
    near = (STEP_SIZE * near_w) * plane[2] - (2.0 - STEP_SIZE) * near_v
    far = (STEP_SIZE * far_w) * plane[3] - (2.0 - STEP_SIZE) * far_v
    far = jnp.where(lane_ids(TALL) < 2 * REACH, far, 0.0)
    near, far = applied(sweep, scale, near, far, (LAST_BAND,), at, gains, total, plane)
    lane = lane_ids(ROWS)
    result = pltpu.roll(jnp.where(lane < REACH, far, near), LANES - REACH, 1) * -STEP_SIZE
    increment[...] = result
    for target in range(GROUPS):
        spread_copies[target] = result


def recentre_kernel(middle, rim, increments, out):
    keep = (ROWS - MID) // 2
    for block in range(GROUPS):
        lanes = slice(block * LANES, (block + 1) * LANES)
        for member in range(LOCAL):
            out[member, 0:keep, lanes] = rim[member, block, 0:keep, :] + increments[block, 0:keep, :]
            out[member, keep : keep + MID, lanes] = (
                middle[member, block] + increments[block, keep : keep + MID, :]
            )
            out[member, keep + MID : ROWS, lanes] = (
                rim[member, block, keep : 2 * keep, :] + increments[block, keep + MID : ROWS, :]
            )


def on_vmem(count):
    return [pl.BlockSpec(memory_space=pltpu.VMEM)] * count


def in_hbm(count):
    return [pl.BlockSpec(memory_space=pltpu.HBM)] * count


def array(*shape):
    return jax.ShapeDtypeStruct(shape, F32)


def on_device(
    members, courant_x, courant_y, obs_cell, innovation, obs_weight, stencil_offsets, stencil_weights
):
    both = ("member", "grp")
    params = pltpu.CompilerParams(vmem_limit_bytes=VMEM)
    crowded = pltpu.CompilerParams(vmem_limit_bytes=ALL_VMEM)
    cost = pl.CostEstimate(flops=10_000_000, bytes_accessed=60_000_000, transcendentals=0)
    tiles = lax.axis_size("tile")
    keep = (ROWS - MID) // 2
    sems = pltpu.SemaphoreType.DMA
    buffers = [
        pltpu.VMEM((LOCAL, GROUPS + 2, HEIGHT, LANES), F32),
        pltpu.VMEM((LOCAL, GROUPS + 2, HEIGHT, LANES), F32),
        pltpu.VMEM((2, GROUPS, HEIGHT, LANES), F32),
        pltpu.VMEM((5, GROUPS, HEIGHT, LANES), F32),
        pltpu.VMEM((LOCAL, GROUPS + 2, MID, LANES), F32),
        pltpu.VMEM((LOCAL, GROUPS + 2, MID + 8, LANES), F32),
        pltpu.VMEM((GROUPS, SLOTS, MID, LANES), F32),
    ]
    up, down, fields = pl.pallas_call(
        message_kernel,
        out_shape=[array(GROUPS, HALO, LANES), array(GROUPS, HALO, LANES), array(2, ROWS, LANES)],
        in_specs=in_hbm(6),
        out_specs=on_vmem(3),
        scratch_shapes=[
            pltpu.VMEM(members.shape, F32),
            pltpu.VMEM((2, ROWS, COLS), F32),
            pltpu.VMEM((1, 1, 1024), jnp.int32),
            pltpu.VMEM((2, 1, 1, 1024), F32),
            sems((3,)),
            sems((3,)),
        ],
        compiler_params=crowded,
        name="messages",
    )(members, courant_x, courant_y, obs_cell, innovation, obs_weight)
    above = lax.ppermute(down, "tile", [(i, i + 1) for i in range(tiles - 1)])
    below = lax.ppermute(up, "tile", [(i + 1, i) for i in range(tiles - 1)])
    middle, send_mid = pl.pallas_call(
        inner_kernel,
        out_shape=[array(LOCAL, GROUPS, MID, LANES), array(GROUPS, SLOTS, MID, LANES)],
        in_specs=in_hbm(3) + on_vmem(1),
        out_specs=in_hbm(2),
        scratch_shapes=buffers + [sems((GROUPS,)), sems((2, GROUPS)), sems((GROUPS + 1,))],
        compiler_params=crowded,
        cost_estimate=cost,
        name="inner",
    )(members, courant_x, courant_y, fields)
    send_mid, above, below = lax.optimization_barrier((send_mid, above, below))
    got_mid = exchanged(send_mid, both)
    rim, send_rim, fields_tall = pl.pallas_call(
        outer_kernel,
        out_shape=[
            array(LOCAL, GROUPS, 2 * keep, LANES),
            array(GROUPS, SLOTS, MID, LANES),
            array(2, TALL, LANES),
        ],
        in_specs=in_hbm(3) + on_vmem(3),
        out_specs=in_hbm(2) + on_vmem(1),
        scratch_shapes=buffers
        + [
            pltpu.VMEM((2, MID, LANES), F32),
            sems((2, GROUPS)),
            sems((2, 2, GROUPS)),
            sems((GROUPS + 1,)),
        ],
        compiler_params=crowded,
        cost_estimate=cost,
        name="outer",
    )(members, courant_x, courant_y, above, below, fields)
    send_rim, got_mid = lax.optimization_barrier((send_rim, got_mid))
    got_rim = exchanged(send_rim, both)
    place = jnp.stack([lax.axis_index("tile"), lax.axis_index(both)]).astype(jnp.int32)
    tables = [pl.BlockSpec(memory_space=pltpu.SMEM)] * 3
    held = pltpu.VMEM((SLOTS, TALL, LANES), F32)
    work = [
        held, held, held, pltpu.VMEM((4, TALL, LANES), F32), pltpu.VMEM((2, TALL, LANES), F32)
    ]
    shifts = [pltpu.VMEM((2 * RADIUS + 1, DEEP, LANES), F32)] * (2 * COPIES)
    handed = pl.pallas_call(
        early_kernel,
        out_shape=array(SPREAD_ROWS + SHARED * TALL, LANES),
        in_specs=tables + on_vmem(2),
        out_specs=pl.BlockSpec(memory_space=pltpu.VMEM),
        scratch_shapes=work + shifts,
        compiler_params=params,
        cost_estimate=cost,
        name="early",
    )(place, stencil_offsets, stencil_weights, got_mid, fields_tall)
    increment, copies = pl.pallas_call(
        analysis_kernel,
        out_shape=[array(ROWS, LANES), array(GROUPS, ROWS, LANES)],
        in_specs=tables + on_vmem(2),
        out_specs=on_vmem(2),
        scratch_shapes=[pltpu.VMEM((GROUPS, SLOTS, TALL, LANES), F32)] + work + shifts,
        compiler_params=params,
        name="analysis",
    )(place, stencil_offsets, stencil_weights, got_rim, handed)
    increments = lax.all_to_all(copies, both, 0, 0, tiled=True)
    analysis = pl.pallas_call(
        recentre_kernel,
        out_shape=array(*members.shape),
        in_specs=on_vmem(3),
        out_specs=pl.BlockSpec(memory_space=pltpu.VMEM),
        compiler_params=params,
        name="recentre",
    )(middle, rim, increments)
    return analysis, increment


def exchanged(blocks, axes):
    flat = blocks.reshape(GROUPS, -1, LANES)
    return lax.all_to_all(flat, axes, 0, 0, tiled=True).reshape(blocks.shape)


def solution(mesh):
    both = ("member", "grp")
    placed = (
        P(both, "tile", None),
        P("tile", None),
        P("tile", None),
        P("tile", both, None),
        P("tile", both, None),
        P("tile", both, None),
        P(),
        P(),
    )
    return jax.shard_map(
        on_device,
        mesh=mesh,
        in_specs=placed,
        out_specs=(P(both, "tile", None), P("tile", both)),
        check_vma=False,
    )
```

```python
import math

import jax
import jax.numpy as jnp
from jax import lax
from jax.experimental import pallas as pl
from jax.experimental.pallas import tpu as pltpu
from jax.sharding import PartitionSpec as P

F32 = jnp.float32
BF16 = jnp.bfloat16
RADIUS = 2
STEP_SIZE = 0.25
GROUPS = 8
LOCAL = 10
ROWS = 32
LANES = 128
COLS = 1024
REACH = 4 * RADIUS
EDGE = REACH + 3
TALL = ROWS + 2 * REACH
WIDE = LANES + 2 * REACH
SLOTS = 12
SPARE = LOCAL * WIDE - (SLOTS - 1) * LANES
HALO = 136
MID = 24
RIM = (TALL - MID) // 2
VMEM = 16 * 1024 * 1024
ALL_VMEM = 60 * 1024 * 1024


def lane_ids(rows):
    return lax.broadcasted_iota(jnp.int32, (rows, LANES), 1)


def pieces(value, count):
    found = []
    for _ in range(count):
        part = value.astype(BF16)
        found.append(part)
        value = value - part.astype(F32)
    return found


def set_coefs(courants, coefs, rows):
    @pl.loop(0, GROUPS)
    def _(block):
        for low in rows:
            span = slice(low, low + 8)
            cx = courants[0, block, span, :]
            cy = courants[1, block, span, :]
            x_plus, x_minus = jnp.maximum(cx, 0.0), jnp.minimum(cx, 0.0)
            y_plus, y_minus = jnp.maximum(cy, 0.0), jnp.minimum(cy, 0.0)
            coefs[0, block, span, :] = 1.0 - x_plus + x_minus - y_plus + y_minus
            coefs[1, block, span, :] = x_plus
            coefs[2, block, span, :] = -x_minus
            coefs[3, block, span, :] = y_plus
            coefs[4, block, span, :] = -y_minus


def clear_sides(buffers):
    for buffer in buffers:
        nothing = jnp.zeros(buffer.shape[2:], F32)
        for member in range(LOCAL):
            for side in (0, GROUPS + 1):
                buffer[member, side] = nothing


def advance(source, target, coefs, starts, homes=None):
    homes = starts if homes is None else homes
    lane = lane_ids(8)
    first, last = lane == 0, lane == LANES - 1

    @pl.loop(0, GROUPS, unroll=4)
    def _(block):
        for low, home in zip(starts, homes):
            rows = slice(low, low + 8)
            k_mid, k_up, k_down, k_left, k_right = (coefs[kind, block, rows, :] for kind in range(5))
            for member in range(LOCAL):
                mid = source[member, block + 1, rows, :]
                before = source[member, block, rows, :]
                after = source[member, block + 2, rows, :]
                target[member, block + 1, home : home + 8, :] = (
                    k_mid * mid
                    + k_up * source[member, block + 1, low - 1 : low + 7, :]
                    + k_down * source[member, block + 1, low + 1 : low + 9, :]
                    + k_left * pltpu.roll(jnp.where(last, before, mid), 1, 1)
                    + k_right * pltpu.roll(jnp.where(first, after, mid), LANES - 1, 1)
                )


def send_plan():
    plan = [[] for _ in range(SLOTS)]
    for member in range(LOCAL):
        start = member * WIDE
        spans = (
            (start, start + REACH, -1),
            (start + REACH, start + REACH + LANES, 0),
            (start + REACH + LANES, start + WIDE, 1),
        )
        for low, high, offset in spans:
            while low < high:
                slot = low // LANES
                stop = min(high, (slot + 1) * LANES)
                plan[slot].append((member, offset, low - slot * LANES, stop - slot * LANES))
                low = stop
    return plan


def pack(final, fields, rolled, blocks, send, sems):
    @pl.loop(0, GROUPS, unroll=8)
    def _(block):
        for member in range(LOCAL):
            shift = (member * WIDE + REACH) % LANES
            value = final[member, block + 1, 0:MID, :]
            rolled[member, block + 1] = pltpu.roll(value, shift, 1) if shift else value

    lane = lane_ids(MID)
    ends = jnp.where(
        lane < SPARE + 2 * REACH,
        pltpu.roll(fields[0], SPARE + REACH, 1),
        pltpu.roll(fields[1], SPARE + 3 * REACH, 1),
    )
    plan = send_plan()

    @pl.loop(0, GROUPS)
    def _(block):
        for slot in range(SLOTS):
            value = ends if slot == SLOTS - 1 else None
            for member, offset, low, high in plan[slot]:
                part = rolled[member, block + 1 + offset]
                if value is None:
                    value = part
                else:
                    value = jnp.where((lane >= low) & (lane < high), part, value)
            blocks[block, slot] = value
        pltpu.make_async_copy(blocks.at[block], send.at[block], sems.at[block]).start()


def finish_pack(blocks, send, sems):
    for block in range(GROUPS):
        pltpu.make_async_copy(blocks.at[block], send.at[block], sems.at[block]).wait()


def message_kernel(
    members, courant_x, courant_y, cell, innov, weight,
    up, down, fields, own, courants, cells, values, member_sems, sems,
):
    small = [
        pltpu.make_async_copy(cell, cells, sems.at[0]),
        pltpu.make_async_copy(innov, values.at[0], sems.at[1]),
        pltpu.make_async_copy(weight, values.at[1], sems.at[2]),
    ]
    large = [
        pltpu.make_async_copy(members, own, member_sems.at[0]),
        pltpu.make_async_copy(courant_x, courants.at[0], member_sems.at[1]),
        pltpu.make_async_copy(courant_y, courants.at[1], member_sems.at[2]),
    ]
    for copy in small + large:
        copy.start()
    for copy in small:
        copy.wait()

    row_hit = lax.broadcasted_iota(jnp.int32, (ROWS, 1024), 0) == lax.shift_right_logical(cells[0], 7)
    col_hit = lax.broadcasted_iota(jnp.int32, (LANES, 1024), 0) == lax.bitwise_and(
        cells[0], LANES - 1
    )
    parts = pieces(values[1, 0] * values[0, 0], 3) + pieces(values[1, 0], 3)
    hits = row_hit.astype(F32)
    left = jnp.concatenate([(hits * part.astype(F32)).astype(BF16) for part in parts], axis=0)
    sums = lax.dot_general(
        left, col_hit.astype(F32).astype(BF16), (((1,), (1,)), ((), ())), preferred_element_type=F32
    )
    for kind in range(2):
        base = 3 * ROWS * kind
        fields[kind] = (
            sums[base : base + ROWS]
            + sums[base + ROWS : base + 2 * ROWS]
            + sums[base + 2 * ROWS : base + 3 * ROWS]
        )
    base = (LOCAL + 2) * EDGE
    for row in range(REACH):
        for kind in range(2):
            up[row, base + kind : base + kind + 1, :] = fields[kind, row : row + 1, :]
            down[row, base + kind : base + kind + 1, :] = fields[
                kind, ROWS - REACH + row : ROWS - REACH + row + 1, :
            ]
        up[row, base + 2 : HALO, :] = jnp.zeros((HALO - base - 2, LANES), F32)
        down[row, base + 2 : HALO, :] = jnp.zeros((HALO - base - 2, LANES), F32)
    for copy in large:
        copy.wait()
    for field in range(LOCAL + 2):
        span = slice(field * EDGE, (field + 1) * EDGE)
        source = own.at[field] if field < LOCAL else courants.at[field - LOCAL]
        first, last = source[0:EDGE, :], source[ROWS - EDGE : ROWS, :]
        for block in range(GROUPS):
            lanes = slice(block * LANES, (block + 1) * LANES)
            up[block, span, :] = first[:, lanes]
            down[block, span, :] = last[:, lanes]


TOP = 16
HEIGHT = 56


def inner_kernel(
    members, courant_x, courant_y, fields, out, send,
    old, new, courants, coefs, rolled, final, blocks, member_sems, wind_sems, sems,
):
    own = slice(TOP, TOP + ROWS)
    large, wind = [], []
    for block in range(GROUPS):
        lanes = slice(block * LANES, (block + 1) * LANES)
        for kind, source in enumerate((courant_x, courant_y)):
            wind.append(
                pltpu.make_async_copy(
                    source.at[:, lanes], courants.at[kind, block, own, :], wind_sems.at[kind, block]
                )
            )
        large.append(
            pltpu.make_async_copy(
                members.at[:, :, lanes], old.at[:, block + 1, own, :], member_sems.at[block]
            )
        )
    for copy in wind + large:
        copy.start()
    clear_sides((old, new, rolled))
    for copy in wind:
        copy.wait()
    set_coefs(courants, coefs, range(TOP, TOP + ROWS, 8))
    for copy in large:
        copy.wait()
    advance(old, new, coefs, range(TOP, TOP + ROWS, 8))
    advance(new, old, coefs, range(TOP, TOP + ROWS, 8))
    skip = (ROWS - MID) // 2
    advance(old, final, coefs, range(TOP + skip, TOP + skip + MID, 8), range(0, MID, 8))
    whole = pltpu.make_async_copy(final.at[:, pl.ds(1, GROUPS), pl.ds(0, MID), :], out, sems.at[GROUPS])
    whole.start()
    middle = [fields[kind, skip : skip + MID, :] for kind in range(2)]
    pack(final, middle, rolled, blocks, send, sems)
    finish_pack(blocks, send, sems)
    whole.wait()


LOW = 8


def outer_kernel(
    members, courant_x, courant_y, above, below, fields,
    out, send, fields_tall,
    old, new, courants, coefs, rolled, final, blocks, rims, member_sems, wind_sems, sems,
):
    top, end = slice(TOP, TOP + 8), slice(ROWS - 8 + LOW, ROWS + LOW)
    copies = []
    for block in range(GROUPS):
        lanes = slice(block * LANES, (block + 1) * LANES)
        for part, span in enumerate((top, end)):
            rows = slice(0, 8) if part == 0 else slice(ROWS - 8, ROWS)
            copies.append(
                pltpu.make_async_copy(
                    members.at[:, rows, lanes], old.at[:, block + 1, span, :],
                    member_sems.at[part, block],
                )
            )
            for kind, source in enumerate((courant_x, courant_y)):
                copies.append(
                    pltpu.make_async_copy(
                        source.at[rows, lanes], courants.at[kind, block, span, :],
                        wind_sems.at[kind, part, block],
                    )
                )
    for copy in copies:
        copy.start()
    clear_sides((old, new, rolled))
    base = (LOCAL + 2) * EDGE

    @pl.loop(0, GROUPS)
    def _(block):
        for field in range(LOCAL + 2):
            span = slice(field * EDGE, (field + 1) * EDGE)
            before, after = above[block, span, :], below[block, span, :]
            if field < LOCAL:
                old[field, block + 1, TOP - EDGE : TOP, :] = before
                old[field, block + 1, ROWS + LOW : ROWS + LOW + EDGE, :] = after
            else:
                courants[field - LOCAL, block, TOP - EDGE : TOP, :] = before
                courants[field - LOCAL, block, ROWS + LOW : ROWS + LOW + EDGE, :] = after

    for kind in range(2):
        for row in range(REACH):
            fields_tall[kind, row : row + 1, :] = above[row, base + kind : base + kind + 1, :]
            fields_tall[kind, REACH + ROWS + row : REACH + ROWS + row + 1, :] = below[
                row, base + kind : base + kind + 1, :
            ]
        fields_tall[kind, REACH : REACH + ROWS, :] = fields[kind]
        rims[kind, 0:RIM, :] = fields_tall[kind, 0:RIM, :]
        rims[kind, RIM:MID, :] = fields_tall[kind, TALL - RIM : TALL, :]
    for copy in copies:
        copy.wait()
    set_coefs(courants, coefs, range(0, HEIGHT, 8))
    for step in range(3):
        high, low = TOP - EDGE + 1 + step, ROWS - 6 + step + LOW
        starts = (high, high + 8, low, low + 8)
        if step < 2:
            pair = (old, new) if step == 0 else (new, old)
            advance(*pair, coefs, starts)
        else:
            advance(old, final, coefs, starts, (0, 8, RIM, RIM + 8))
    whole = pltpu.make_async_copy(
        final.at[:, pl.ds(1, GROUPS), pl.ds(REACH, 8), :], out, sems.at[GROUPS]
    )
    whole.start()
    pack(final, rims, rolled, blocks, send, sems)
    finish_pack(blocks, send, sems)
    whole.wait()


COPIES = 4
DEEP = 56


def member_place(member):
    return member * WIDE // LANES, member * WIDE % LANES


def folded(slots, lane):
    near, far = None, None
    for member in range(LOCAL):
        base, shift = member_place(member)
        here, there = slots(base), slots(base + 1)
        if shift:
            here = pltpu.roll(jnp.where(lane >= shift, here, there), LANES - shift, 1)
            there = pltpu.roll(there, LANES - shift, 1)
        near = here if near is None else near + here
        far = there if far is None else far + there
    return near, far


def spread_out(near, far, lane, store):
    slots = [None] * SLOTS
    for member in range(LOCAL):
        base, shift = member_place(member)
        moved = pltpu.roll(near, shift, 1) if shift else near
        tail = pltpu.roll(far, shift, 1) if shift else far
        slots[base] = moved if slots[base] is None else jnp.where(lane >= shift, moved, slots[base])
        slots[base + 1] = jnp.where(
            lane < shift, moved, jnp.where(lane < shift + 2 * REACH, tail, 0.0)
        )
    for slot in range(SLOTS):
        store(slot, slots[slot])


def shifted(before, mid, after, lane):
    found = {0: mid}
    for shift in (1, 2):
        found[shift] = pltpu.roll(jnp.where(lane < shift, after, mid), LANES - shift, 1)
        found[-shift] = pltpu.roll(jnp.where(lane >= LANES - shift, before, mid), shift, 1)
    return found


def put(target, span, found):
    for shift, value in found.items():
        target[RADIUS + shift, span, :] = value


def localizer(offsets, weights, inside, copies):
    entries = offsets.shape[0]
    tap_row = [offsets[entry, 0] for entry in range(entries)]
    tap_col = [offsets[entry, 1] for entry in range(entries)]
    tap = [weights[entry] for entry in range(entries)]
    weight_sum = tap[0]
    for entry in range(1, entries):
        weight_sum = weight_sum + tap[entry]
    scale = 1.0 / jnp.full((1, LANES), weight_sum, F32)
    first_copies, second_copies = copies[: len(copies) // 2], copies[len(copies) // 2 :]

    def taps(source, sign, low, rows):
        value = None
        for entry in range(entries):
            term = tap[entry] * source[
                RADIUS + sign * tap_col[entry], pl.ds(low + sign * tap_row[entry], rows), :
            ]
            value = term if value is None else value + term
        return value

    def sweep(slots, multiplier, bands, finish):
        def copies_of(held, slot):
            found = []
            for at, mid in enumerate(held[slot]):
                before = held.get(slot - 1, held[slot])[at]
                after = held.get(slot + 1, held[slot])[at]
                found.append(shifted(before, mid, after, lane_ids(mid.shape[0])))
            return found

        def put_all(target, found, kind):
            for band, values in zip(bands, found):
                low, rows = band[kind]
                put(target, slice(low, low + rows), values)

        def entering(slot):
            return [multiplier(slot, slice(band[0][0], sum(band[0]))) for band in bands]

        products, localized = {0: entering(0), 1: entering(1)}, {}
        put_all(first_copies[0], copies_of(products, 0), 0)
        for slot in range(slots + 3):
            if slot + 1 < slots:
                if slot + 2 < slots:
                    products[slot + 2] = entering(slot + 2)
                ahead = copies_of(products, slot + 1)
            if slot < slots:
                localized[slot] = [
                    taps(first_copies[slot % COPIES], -1, *band[1])
                    * inside[slot, band[1][0] : sum(band[1]), :]
                    for band in bands
                ]
            if slot + 1 < slots:
                put_all(first_copies[(slot + 1) % COPIES], ahead, 0)
            if 1 < slot < slots + 2:
                behind = copies_of(localized, slot - 2)
            if slot > 2:
                done = slot - 3
                finish(done, [taps(second_copies[done % COPIES], 1, *band[2]) for band in bands])
            if 1 < slot < slots + 2:
                put_all(second_copies[(slot - 2) % COPIES], behind, 1)

    return sweep, scale * scale


def applied(sweep, scale, near, far, bands, spread, gains, total, plane):
    spots, rows = [], 0
    for band in bands:
        spots.append((slice(rows, rows + band[2][1]), slice(band[2][0], sum(band[2]))))
        rows += band[2][1]

    def store_gain(slot, value):
        gains[slot] = value

    spread_out(near, far, lane_ids(near.shape[0]), store_gain)

    def finish_ones(slot, values):
        for (here, _), value in zip(spots, values):
            plane[slot, here, :] = value

    sweep(2, lambda slot, span: gains[slot, span, :], bands, finish_ones)

    @pl.loop(0, SLOTS)
    def _(slot):
        total[slot, 0:rows, :] = jnp.zeros((rows, LANES), F32)

    @pl.loop(0, GROUPS)
    def _(source):
        def finish(slot, values):
            for (here, there), value in zip(spots, values):
                total[slot, here, :] += value * spread(source, slot, there)

        sweep(
            SLOTS, lambda slot, span: gains[slot, span, :] * spread(source, slot, span),
            bands, finish,
        )

    near, far = folded(lambda slot: total[slot, 0:rows, :], lane_ids(rows))
    return (near + plane[0, 0:rows, :]) * scale, (far + plane[1, 0:rows, :]) * scale


def set_spread(got, parts, averages, spread):
    count = GROUPS * LOCAL
    deviation = 1.0 / math.sqrt(count - 1)
    rows = parts[0][2] * len(parts)

    @pl.loop(0, SLOTS)
    def _(slot):
        value = got[0, slot]
        for source in range(1, GROUPS):
            value = value + got[source, slot]
        averages[slot, 0:rows, :] = value

    lane = lane_ids(rows)
    near, far = folded(lambda slot: averages[slot, 0:rows, :], lane)

    def store_average(slot, value):
        averages[slot, 0:rows, :] = value

    spread_out(near / count, far / count, lane, store_average)

    @pl.loop(0, SLOTS)
    def _(slot):
        average = averages[slot, 0:rows, :]
        for source in range(GROUPS):
            value = (got[source, slot] - average) * deviation
            for here, there, number in parts:
                spread[source, slot, here : here + number, :] = value[there : there + number]


def block_ends(got, parts, block, ends):
    for here, there, count in parts:
        rows = slice(there, there + count)
        ends[0, here : here + count, :] = got[jnp.maximum(block - 1, 0), SLOTS - 1, rows, :]
        ends[1, here : here + count, :] = got[
            jnp.minimum(block + 1, GROUPS - 1), SLOTS - 1, rows, :
        ]


def with_margins(own, kind, block, ends, rows):
    lane = lane_ids(rows.stop - rows.start)
    back = LANES - SPARE - 2 * REACH * kind
    left_ends = jnp.where(block > 0, ends[0, rows, :], 0.0)
    right_ends = jnp.where(block < GROUPS - 1, ends[1, rows, :], 0.0)
    own = pltpu.roll(own, REACH, 1)
    near = jnp.where(lane < REACH, pltpu.roll(left_ends, back, 1), own)
    far = jnp.where(lane < REACH, own, pltpu.roll(right_ends, back, 1))
    return near, jnp.where(lane < 2 * REACH, far, 0.0)


EARLY = 16
EARLY_BAND = ((RIM, MID), (RIM + RADIUS, MID), (RIM + 2 * RADIUS, EARLY))


SPREAD_ROWS = GROUPS * SLOTS * MID
SHARED = SLOTS + 5


def handed_on(rows):
    spread = rows.at[pl.ds(0, SPREAD_ROWS)].reshape(GROUPS, SLOTS, MID, LANES)
    return spread, rows.at[pl.ds(SPREAD_ROWS, SHARED * TALL)].reshape(SHARED, TALL, LANES)


def early_kernel(
    place, offsets, weights, got, fields, handed,
    averages, gains, total, plane, ends, *copies,
):
    spread, shared = handed_on(handed)
    tile, block = place[0], place[1]
    lane = lane_ids(TALL)
    set_spread(got, ((0, 0, MID),), averages, spread)

    row = lax.broadcasted_iota(jnp.int32, (TALL, LANES), 0) + (tile * ROWS - REACH)
    col = lane + (block * LANES - REACH)
    row_ok = (row >= 0) & (row < ROWS * 32)
    near_ok = row_ok & (col >= 0) & (col < COLS)
    far_ok = row_ok & (col + LANES < COLS)

    def store_inside(slot, value):
        shared[slot] = value

    spread_out(near_ok.astype(F32), far_ok.astype(F32), lane, store_inside)
    sweep, scale = localizer(offsets, weights, shared, copies)
    ends[...] = jnp.zeros(ends.shape, F32)
    block_ends(got, ((RIM, 0, MID),), block, ends)
    near, far = with_margins(fields[0], 0, block, ends, slice(0, TALL))

    def at(source, slot, rows):
        return spread[source, slot, rows.start - RIM : rows.stop - RIM, :]

    near, far = applied(sweep, scale, near, far, (EARLY_BAND,), at, gains, total, plane)
    for part, value in enumerate((near, far)):
        shared[SLOTS, part * EARLY : (part + 1) * EARLY, :] = value
    shared[SLOTS, 2 * EARLY : TALL, :] = jnp.zeros((TALL - 2 * EARLY, LANES), F32)
    for kind in range(2):
        shared[SLOTS + 1 + kind] = ends[kind]
        shared[SLOTS + 3 + kind] = fields[kind]


RIM_BANDS = (
    ((0, MID), (RADIUS, EARLY), (2 * RADIUS, EARLY)),
    ((MID, MID), (TALL - RADIUS - EARLY, EARLY), (TALL - 2 * RADIUS - EARLY, EARLY)),
)
LAST_BAND = ((2 * RADIUS, 40), (3 * RADIUS, 40), (REACH, ROWS))


def analysis_kernel(
    place, offsets, weights, got, handed, increment, spread_copies,
    spread, averages, gains, total, plane, ends, *copies,
):
    spread_mid, shared = handed_on(handed)
    block = place[1]
    set_spread(got, ((0, 0, RIM), (TALL - RIM, RIM, RIM)), averages, spread)

    @pl.loop(0, SLOTS)
    def _(slot):
        for source in range(GROUPS):
            spread[source, slot, RIM : RIM + MID, :] = spread_mid[source, slot]

    def at(source, slot, rows):
        return spread[source, slot, rows, :]

    sweep, scale = localizer(offsets, weights, shared, copies)
    for kind in range(2):
        ends[kind] = shared[SLOTS + 1 + kind]
    block_ends(got, ((0, 0, RIM), (TALL - RIM, RIM, RIM)), block, ends)
    rows = slice(0, TALL)
    near_v, far_v = with_margins(shared[SLOTS + 3], 0, block, ends, rows)
    near_w, far_w = with_margins(shared[SLOTS + 4], 1, block, ends, rows)

    values = applied(sweep, scale, near_v, far_v, RIM_BANDS, at, gains, total, plane)
    for part in range(2):
        plane[2 + part] = jnp.zeros((TALL, LANES), F32)
        low = 2 * RADIUS
        plane[2 + part, low : low + EARLY, :] = values[part][0:EARLY]
        plane[2 + part, TALL - low - EARLY : TALL - low, :] = values[part][EARLY : 2 * EARLY]
        plane[2 + part, RIM + low : RIM + low + EARLY, :] = shared[
            SLOTS, part * EARLY : (part + 1) * EARLY, :
        ]
    near = (STEP_SIZE * near_w) * plane[2] - (2.0 - STEP_SIZE) * near_v
    far = (STEP_SIZE * far_w) * plane[3] - (2.0 - STEP_SIZE) * far_v
    far = jnp.where(lane_ids(TALL) < 2 * REACH, far, 0.0)
    near, far = applied(sweep, scale, near, far, (LAST_BAND,), at, gains, total, plane)
    lane = lane_ids(ROWS)
    result = pltpu.roll(jnp.where(lane < REACH, far, near), LANES - REACH, 1) * -STEP_SIZE
    increment[...] = result
    for target in range(GROUPS):
        spread_copies[target] = result


def recentre_kernel(middle, rim, increments, out):
    keep = (ROWS - MID) // 2
    for block in range(GROUPS):
        lanes = slice(block * LANES, (block + 1) * LANES)
        for member in range(LOCAL):
            out[member, 0:keep, lanes] = rim[member, block, 0:keep, :] + increments[block, 0:keep, :]
            out[member, keep : keep + MID, lanes] = (
                middle[member, block] + increments[block, keep : keep + MID, :]
            )
            out[member, keep + MID : ROWS, lanes] = (
                rim[member, block, keep : 2 * keep, :] + increments[block, keep + MID : ROWS, :]
            )


def on_vmem(count):
    return [pl.BlockSpec(memory_space=pltpu.VMEM)] * count


def in_hbm(count):
    return [pl.BlockSpec(memory_space=pltpu.HBM)] * count


def array(*shape):
    return jax.ShapeDtypeStruct(shape, F32)


def on_device(
    members, courant_x, courant_y, obs_cell, innovation, obs_weight, stencil_offsets, stencil_weights
):
    both = ("member", "grp")
    params = pltpu.CompilerParams(vmem_limit_bytes=VMEM)
    crowded = pltpu.CompilerParams(vmem_limit_bytes=ALL_VMEM)
    cost = pl.CostEstimate(flops=10_000_000, bytes_accessed=60_000_000, transcendentals=0)
    tiles = lax.axis_size("tile")
    keep = (ROWS - MID) // 2
    sems = pltpu.SemaphoreType.DMA
    buffers = [
        pltpu.VMEM((LOCAL, GROUPS + 2, HEIGHT, LANES), F32),
        pltpu.VMEM((LOCAL, GROUPS + 2, HEIGHT, LANES), F32),
        pltpu.VMEM((2, GROUPS, HEIGHT, LANES), F32),
        pltpu.VMEM((5, GROUPS, HEIGHT, LANES), F32),
        pltpu.VMEM((LOCAL, GROUPS + 2, MID, LANES), F32),
        pltpu.VMEM((LOCAL, GROUPS + 2, MID + 8, LANES), F32),
        pltpu.VMEM((GROUPS, SLOTS, MID, LANES), F32),
    ]
    up, down, fields = pl.pallas_call(
        message_kernel,
        out_shape=[array(GROUPS, HALO, LANES), array(GROUPS, HALO, LANES), array(2, ROWS, LANES)],
        in_specs=in_hbm(6),
        out_specs=on_vmem(3),
        scratch_shapes=[
            pltpu.VMEM(members.shape, F32),
            pltpu.VMEM((2, ROWS, COLS), F32),
            pltpu.VMEM((1, 1, 1024), jnp.int32),
            pltpu.VMEM((2, 1, 1, 1024), F32),
            sems((3,)),
            sems((3,)),
        ],
        compiler_params=crowded,
        name="messages",
    )(members, courant_x, courant_y, obs_cell, innovation, obs_weight)
    above = lax.ppermute(down, "tile", [(i, i + 1) for i in range(tiles - 1)])
    below = lax.ppermute(up, "tile", [(i + 1, i) for i in range(tiles - 1)])
    middle, send_mid = pl.pallas_call(
        inner_kernel,
        out_shape=[array(LOCAL, GROUPS, MID, LANES), array(GROUPS, SLOTS, MID, LANES)],
        in_specs=in_hbm(3) + on_vmem(1),
        out_specs=in_hbm(2),
        scratch_shapes=buffers + [sems((GROUPS,)), sems((2, GROUPS)), sems((GROUPS + 1,))],
        compiler_params=crowded,
        cost_estimate=cost,
        name="inner",
    )(members, courant_x, courant_y, fields)
    send_mid, _ = lax.optimization_barrier((send_mid, above))
    got_mid = exchanged(send_mid, both)
    rim, send_rim, fields_tall = pl.pallas_call(
        outer_kernel,
        out_shape=[
            array(LOCAL, GROUPS, 2 * keep, LANES),
            array(GROUPS, SLOTS, MID, LANES),
            array(2, TALL, LANES),
        ],
        in_specs=in_hbm(3) + on_vmem(3),
        out_specs=in_hbm(2) + on_vmem(1),
        scratch_shapes=buffers
        + [
            pltpu.VMEM((2, MID, LANES), F32),
            sems((2, GROUPS)),
            sems((2, 2, GROUPS)),
            sems((GROUPS + 1,)),
        ],
        compiler_params=crowded,
        cost_estimate=cost,
        name="outer",
    )(members, courant_x, courant_y, above, below, fields)
    send_rim, got_mid = lax.optimization_barrier((send_rim, got_mid))
    got_rim = exchanged(send_rim, both)
    place = jnp.stack([lax.axis_index("tile"), lax.axis_index(both)]).astype(jnp.int32)
    tables = [pl.BlockSpec(memory_space=pltpu.SMEM)] * 3
    held = pltpu.VMEM((SLOTS, TALL, LANES), F32)
    work = [
        held, held, held, pltpu.VMEM((4, TALL, LANES), F32), pltpu.VMEM((2, TALL, LANES), F32)
    ]
    shifts = [pltpu.VMEM((2 * RADIUS + 1, DEEP, LANES), F32)] * (2 * COPIES)
    handed = pl.pallas_call(
        early_kernel,
        out_shape=array(SPREAD_ROWS + SHARED * TALL, LANES),
        in_specs=tables + on_vmem(2),
        out_specs=pl.BlockSpec(memory_space=pltpu.VMEM),
        scratch_shapes=work + shifts,
        compiler_params=params,
        cost_estimate=cost,
        name="early",
    )(place, stencil_offsets, stencil_weights, got_mid, fields_tall)
    increment, copies = pl.pallas_call(
        analysis_kernel,
        out_shape=[array(ROWS, LANES), array(GROUPS, ROWS, LANES)],
        in_specs=tables + on_vmem(2),
        out_specs=on_vmem(2),
        scratch_shapes=[pltpu.VMEM((GROUPS, SLOTS, TALL, LANES), F32)] + work + shifts,
        compiler_params=params,
        name="analysis",
    )(place, stencil_offsets, stencil_weights, got_rim, handed)
    increments = lax.all_to_all(copies, both, 0, 0, tiled=True)
    analysis = pl.pallas_call(
        recentre_kernel,
        out_shape=array(*members.shape),
        in_specs=on_vmem(3),
        out_specs=pl.BlockSpec(memory_space=pltpu.VMEM),
        compiler_params=params,
        name="recentre",
    )(middle, rim, increments)
    return analysis, increment


def exchanged(blocks, axes):
    flat = blocks.reshape(GROUPS, -1, LANES)
    return lax.all_to_all(flat, axes, 0, 0, tiled=True).reshape(blocks.shape)


def solution(mesh):
    both = ("member", "grp")
    placed = (
        P(both, "tile", None),
        P("tile", None),
        P("tile", None),
        P("tile", both, None),
        P("tile", both, None),
        P("tile", both, None),
        P(),
        P(),
    )
    return jax.shard_map(
        on_device,
        mesh=mesh,
        in_specs=placed,
        out_specs=(P(both, "tile", None), P("tile", both)),
        check_vma=False,
    )
```

```python
import math

import jax
import jax.numpy as jnp
from jax import lax
from jax.experimental import pallas as pl
from jax.experimental.pallas import tpu as pltpu
from jax.sharding import PartitionSpec as P

F32 = jnp.float32
BF16 = jnp.bfloat16
RADIUS = 2
STEP_SIZE = 0.25
GROUPS = 8
LOCAL = 10
ROWS = 32
LANES = 128
COLS = 1024
REACH = 4 * RADIUS
EDGE = REACH + 3
TALL = ROWS + 2 * REACH
WIDE = LANES + 2 * REACH
SLOTS = 12
SPARE = LOCAL * WIDE - (SLOTS - 1) * LANES
HALO = 136
MID = 24
RIM = (TALL - MID) // 2
VMEM = 16 * 1024 * 1024
ALL_VMEM = 60 * 1024 * 1024


def lane_ids(rows):
    return lax.broadcasted_iota(jnp.int32, (rows, LANES), 1)


def pieces(value, count):
    found = []
    for _ in range(count):
        part = value.astype(BF16)
        found.append(part)
        value = value - part.astype(F32)
    return found


def set_coefs(courants, coefs, rows):
    @pl.loop(0, GROUPS)
    def _(block):
        for low in rows:
            span = slice(low, low + 8)
            cx = courants[0, block, span, :]
            cy = courants[1, block, span, :]
            x_plus, x_minus = jnp.maximum(cx, 0.0), jnp.minimum(cx, 0.0)
            y_plus, y_minus = jnp.maximum(cy, 0.0), jnp.minimum(cy, 0.0)
            coefs[0, block, span, :] = 1.0 - x_plus + x_minus - y_plus + y_minus
            coefs[1, block, span, :] = x_plus
            coefs[2, block, span, :] = -x_minus
            coefs[3, block, span, :] = y_plus
            coefs[4, block, span, :] = -y_minus


def clear_sides(buffers):
    for buffer in buffers:
        nothing = jnp.zeros(buffer.shape[2:], F32)
        for member in range(LOCAL):
            for side in (0, GROUPS + 1):
                buffer[member, side] = nothing


def advance(source, target, coefs, starts, homes=None):
    homes = starts if homes is None else homes
    lane = lane_ids(8)
    first, last = lane == 0, lane == LANES - 1

    @pl.loop(0, GROUPS, unroll=4)
    def _(block):
        for low, home in zip(starts, homes):
            rows = slice(low, low + 8)
            k_mid, k_up, k_down, k_left, k_right = (coefs[kind, block, rows, :] for kind in range(5))
            for member in range(LOCAL):
                mid = source[member, block + 1, rows, :]
                before = source[member, block, rows, :]
                after = source[member, block + 2, rows, :]
                target[member, block + 1, home : home + 8, :] = (
                    k_mid * mid
                    + k_up * source[member, block + 1, low - 1 : low + 7, :]
                    + k_down * source[member, block + 1, low + 1 : low + 9, :]
                    + k_left * pltpu.roll(jnp.where(last, before, mid), 1, 1)
                    + k_right * pltpu.roll(jnp.where(first, after, mid), LANES - 1, 1)
                )


def send_plan():
    plan = [[] for _ in range(SLOTS)]
    for member in range(LOCAL):
        start = member * WIDE
        spans = (
            (start, start + REACH, -1),
            (start + REACH, start + REACH + LANES, 0),
            (start + REACH + LANES, start + WIDE, 1),
        )
        for low, high, offset in spans:
            while low < high:
                slot = low // LANES
                stop = min(high, (slot + 1) * LANES)
                plan[slot].append((member, offset, low - slot * LANES, stop - slot * LANES))
                low = stop
    return plan


def pack(final, fields, rows, rolled, blocks, send, sems):
    @pl.loop(0, GROUPS, unroll=8)
    def _(block):
        for member in range(LOCAL):
            shift = (member * WIDE + REACH) % LANES
            value = final[member, block + 1, 0:rows, :]
            rolled[member, block + 1] = pltpu.roll(value, shift, 1) if shift else value

    lane = lane_ids(rows)
    ends = jnp.where(
        lane < SPARE + 2 * REACH,
        pltpu.roll(fields[0], SPARE + REACH, 1),
        pltpu.roll(fields[1], SPARE + 3 * REACH, 1),
    )
    plan = send_plan()

    @pl.loop(0, GROUPS)
    def _(block):
        for slot in range(SLOTS):
            value = ends if slot == SLOTS - 1 else None
            for member, offset, low, high in plan[slot]:
                part = rolled[member, block + 1 + offset]
                if value is None:
                    value = part
                else:
                    value = jnp.where((lane >= low) & (lane < high), part, value)
            blocks[block, slot * rows : (slot + 1) * rows, :] = value
        pltpu.make_async_copy(blocks.at[block], send(block), sems.at[block]).start()


def finish_pack(blocks, send, sems):
    for block in range(GROUPS):
        pltpu.make_async_copy(blocks.at[block], send(block), sems.at[block]).wait()


def observed(cells, values, fields):
    row_hit = lax.broadcasted_iota(jnp.int32, (ROWS, 1024), 0) == lax.shift_right_logical(cells[0], 7)
    col_hit = lax.broadcasted_iota(jnp.int32, (LANES, 1024), 0) == lax.bitwise_and(
        cells[0], LANES - 1
    )
    parts = pieces(values[1, 0] * values[0, 0], 3) + pieces(values[1, 0], 3)
    hits = row_hit.astype(F32)
    left = jnp.concatenate([(hits * part.astype(F32)).astype(BF16) for part in parts], axis=0)
    sums = lax.dot_general(
        left, col_hit.astype(F32).astype(BF16), (((1,), (1,)), ((), ())), preferred_element_type=F32
    )
    for kind in range(2):
        base = 3 * ROWS * kind
        fields[kind] = (
            sums[base : base + ROWS]
            + sums[base + ROWS : base + 2 * ROWS]
            + sums[base + 2 * ROWS : base + 3 * ROWS]
        )


def set_messages(members, courants, fields, up, down):
    @pl.loop(0, GROUPS)
    def _(block):
        for field in range(LOCAL + 2):
            span = slice(field * EDGE, (field + 1) * EDGE)
            for target, low in ((up, TOP), (down, TOP + ROWS - EDGE)):
                rows = slice(low, low + EDGE)
                if field < LOCAL:
                    target[block, span, :] = members[field, block + 1, rows, :]
                else:
                    target[block, span, :] = courants[field - LOCAL, block, rows, :]

    base = (LOCAL + 2) * EDGE
    for row in range(REACH):
        for kind in range(2):
            up[row, base + kind : base + kind + 1, :] = fields[kind, row : row + 1, :]
            down[row, base + kind : base + kind + 1, :] = fields[
                kind, ROWS - REACH + row : ROWS - REACH + row + 1, :
            ]
        up[row, base + 2 : HALO, :] = jnp.zeros((HALO - base - 2, LANES), F32)
        down[row, base + 2 : HALO, :] = jnp.zeros((HALO - base - 2, LANES), F32)


TOP = 16
HEIGHT = 56


def inner_kernel(
    members, courant_x, courant_y, cell, innov, weight, up_out, down_out, out, send, fields,
    old, new, courants, coefs, rolled, final, blocks, cells, values, up, down,
    member_sems, wind_sems, sems, small_sems,
):
    own = slice(TOP, TOP + ROWS)
    large, wind = [], []
    for block in range(GROUPS):
        lanes = slice(block * LANES, (block + 1) * LANES)
        for kind, source in enumerate((courant_x, courant_y)):
            wind.append(
                pltpu.make_async_copy(
                    source.at[:, lanes], courants.at[kind, block, own, :], wind_sems.at[kind, block]
                )
            )
        large.append(
            pltpu.make_async_copy(
                members.at[:, :, lanes], old.at[:, block + 1, own, :], member_sems.at[block]
            )
        )
    small = [
        pltpu.make_async_copy(cell, cells, small_sems.at[0]),
        pltpu.make_async_copy(innov, values.at[0], small_sems.at[1]),
        pltpu.make_async_copy(weight, values.at[1], small_sems.at[2]),
    ]
    for copy in small + wind + large:
        copy.start()
    clear_sides((old, new, rolled))
    for copy in small:
        copy.wait()
    observed(cells, values, fields)
    for copy in wind:
        copy.wait()
    set_coefs(courants, coefs, range(TOP, TOP + ROWS, 8))
    for copy in large:
        copy.wait()
    set_messages(old, courants, fields, up, down)
    messages = [
        pltpu.make_async_copy(up, up_out, small_sems.at[0]),
        pltpu.make_async_copy(down, down_out, small_sems.at[1]),
    ]
    for copy in messages:
        copy.start()
    advance(old, new, coefs, range(TOP, TOP + ROWS, 8))
    advance(new, old, coefs, range(TOP, TOP + ROWS, 8))
    skip = (ROWS - MID) // 2
    advance(old, final, coefs, range(TOP + skip, TOP + skip + MID, 8), range(0, MID, 8))
    whole = pltpu.make_async_copy(final.at[:, pl.ds(1, GROUPS), pl.ds(0, MID), :], out, sems.at[GROUPS])
    whole.start()
    middle = [fields[kind, skip : skip + MID, :] for kind in range(2)]
    pack(final, middle, MID, rolled, blocks, lambda block: send.at[block], sems)
    finish_pack(blocks, lambda block: send.at[block], sems)
    for copy in messages + [whole]:
        copy.wait()


SIDE = SLOTS * RIM
SHORT = 32


def rim_rows(
    lower, members, courant_x, courant_y, message, fields, out, send,
    old, new, courants, coefs, rolled, final, blocks, rim, member_sems, wind_sems, sems,
):
    own = slice(0, 8) if lower else slice(TOP, TOP + 8)
    rows = slice(ROWS - 8, ROWS) if lower else slice(0, 8)
    beside = 8 if lower else TOP - EDGE
    copies = []
    for block in range(GROUPS):
        lanes = slice(block * LANES, (block + 1) * LANES)
        copies.append(
            pltpu.make_async_copy(
                members.at[:, rows, lanes], old.at[:, block + 1, own, :], member_sems.at[block]
            )
        )
        for kind, source in enumerate((courant_x, courant_y)):
            copies.append(
                pltpu.make_async_copy(
                    source.at[rows, lanes], courants.at[kind, block, own, :],
                    wind_sems.at[kind, block],
                )
            )
    for copy in copies:
        copy.start()
    clear_sides((old, new, rolled))

    @pl.loop(0, GROUPS)
    def _(block):
        for field in range(LOCAL + 2):
            value = message[block, field * EDGE : (field + 1) * EDGE, :]
            if field < LOCAL:
                old[field, block + 1, beside : beside + EDGE, :] = value
            else:
                courants[field - LOCAL, block, beside : beside + EDGE, :] = value

    base, keep = (LOCAL + 2) * EDGE, RIM - REACH
    for kind in range(2):
        for row in range(REACH):
            at = row + (keep if lower else 0)
            rim[kind, at : at + 1, :] = message[row, base + kind : base + kind + 1, :]
        if lower:
            rim[kind, 0:keep, :] = fields[kind, ROWS - keep : ROWS, :]
        else:
            rim[kind, REACH:RIM, :] = fields[kind, 0:keep, :]
    for copy in copies:
        copy.wait()
    set_coefs(courants, coefs, range(0, SHORT, 8))
    first = 2 if lower else TOP - EDGE + 1
    advance(old, new, coefs, (first, first + 8))
    advance(new, old, coefs, (first + 1, first + 9))
    advance(old, final, coefs, (first + 2, first + 10), (0, 8))
    low = 0 if lower else REACH
    whole = pltpu.make_async_copy(
        final.at[:, pl.ds(1, GROUPS), pl.ds(low, 8), :], out, sems.at[GROUPS]
    )
    whole.start()

    def place(block):
        return send.at[block, pl.ds(SIDE if lower else 0, SIDE), :]

    pack(final, rim, RIM, rolled, blocks, place, sems)
    finish_pack(blocks, place, sems)
    whole.wait()


def upper_kernel(members, courant_x, courant_y, above, fields, out, send, rim, *rest):
    work, sems = rest[:-3], rest[-3:]
    rim_rows(
        False, members, courant_x, courant_y, above, fields, out, send, *work, rim, *sems
    )


def lower_kernel(
    members, courant_x, courant_y, below, fields, upper, sent, out, send, fields_tall, *rest
):
    del sent
    work, rim, sems = rest[:-4], rest[-4], rest[-3:]
    rim_rows(
        True, members, courant_x, courant_y, below, fields, out, send, *work, rim, *sems
    )
    for kind in range(2):
        fields_tall[kind, 0:RIM, :] = upper[kind]
        fields_tall[kind, REACH : REACH + ROWS, :] = fields[kind]
        fields_tall[kind, TALL - RIM : TALL, :] = rim[kind]


COPIES = 4
DEEP = 56


def member_place(member):
    return member * WIDE // LANES, member * WIDE % LANES


def folded(slots, lane):
    near, far = None, None
    for member in range(LOCAL):
        base, shift = member_place(member)
        here, there = slots(base), slots(base + 1)
        if shift:
            here = pltpu.roll(jnp.where(lane >= shift, here, there), LANES - shift, 1)
            there = pltpu.roll(there, LANES - shift, 1)
        near = here if near is None else near + here
        far = there if far is None else far + there
    return near, far


def spread_out(near, far, lane, store):
    slots = [None] * SLOTS
    for member in range(LOCAL):
        base, shift = member_place(member)
        moved = pltpu.roll(near, shift, 1) if shift else near
        tail = pltpu.roll(far, shift, 1) if shift else far
        slots[base] = moved if slots[base] is None else jnp.where(lane >= shift, moved, slots[base])
        slots[base + 1] = jnp.where(
            lane < shift, moved, jnp.where(lane < shift + 2 * REACH, tail, 0.0)
        )
    for slot in range(SLOTS):
        store(slot, slots[slot])


def shifted(before, mid, after, lane):
    found = {0: mid}
    for shift in (1, 2):
        found[shift] = pltpu.roll(jnp.where(lane < shift, after, mid), LANES - shift, 1)
        found[-shift] = pltpu.roll(jnp.where(lane >= LANES - shift, before, mid), shift, 1)
    return found


def put(target, span, found):
    for shift, value in found.items():
        target[RADIUS + shift, span, :] = value


def localizer(offsets, weights, inside, copies):
    entries = offsets.shape[0]
    tap_row = [offsets[entry, 0] for entry in range(entries)]
    tap_col = [offsets[entry, 1] for entry in range(entries)]
    tap = [weights[entry] for entry in range(entries)]
    weight_sum = tap[0]
    for entry in range(1, entries):
        weight_sum = weight_sum + tap[entry]
    scale = 1.0 / jnp.full((1, LANES), weight_sum, F32)
    first_copies, second_copies = copies[: len(copies) // 2], copies[len(copies) // 2 :]

    def taps(source, sign, low, rows):
        value = None
        for entry in range(entries):
            term = tap[entry] * source[
                RADIUS + sign * tap_col[entry], pl.ds(low + sign * tap_row[entry], rows), :
            ]
            value = term if value is None else value + term
        return value

    def sweep(slots, multiplier, bands, finish):
        def copies_of(held, slot):
            found = []
            for at, mid in enumerate(held[slot]):
                before = held.get(slot - 1, held[slot])[at]
                after = held.get(slot + 1, held[slot])[at]
                found.append(shifted(before, mid, after, lane_ids(mid.shape[0])))
            return found

        def put_all(target, found, kind):
            for band, values in zip(bands, found):
                low, rows = band[kind]
                put(target, slice(low, low + rows), values)

        def entering(slot):
            return [multiplier(slot, slice(band[0][0], sum(band[0]))) for band in bands]

        products, localized = {0: entering(0), 1: entering(1)}, {}
        put_all(first_copies[0], copies_of(products, 0), 0)
        for slot in range(slots + 3):
            if slot + 1 < slots:
                if slot + 2 < slots:
                    products[slot + 2] = entering(slot + 2)
                ahead = copies_of(products, slot + 1)
            if slot < slots:
                localized[slot] = [
                    taps(first_copies[slot % COPIES], -1, *band[1])
                    * inside[slot, band[1][0] : sum(band[1]), :]
                    for band in bands
                ]
            if slot + 1 < slots:
                put_all(first_copies[(slot + 1) % COPIES], ahead, 0)
            if 1 < slot < slots + 2:
                behind = copies_of(localized, slot - 2)
            if slot > 2:
                done = slot - 3
                finish(done, [taps(second_copies[done % COPIES], 1, *band[2]) for band in bands])
            if 1 < slot < slots + 2:
                put_all(second_copies[(slot - 2) % COPIES], behind, 1)

    return sweep, scale * scale


def applied(sweep, scale, near, far, bands, spread, gains, total, plane):
    spots, rows = [], 0
    for band in bands:
        spots.append((slice(rows, rows + band[2][1]), slice(band[2][0], sum(band[2]))))
        rows += band[2][1]

    def store_gain(slot, value):
        gains[slot] = value

    spread_out(near, far, lane_ids(near.shape[0]), store_gain)

    def finish_ones(slot, values):
        for (here, _), value in zip(spots, values):
            plane[slot, here, :] = value

    sweep(2, lambda slot, span: gains[slot, span, :], bands, finish_ones)

    @pl.loop(0, SLOTS)
    def _(slot):
        total[slot, 0:rows, :] = jnp.zeros((rows, LANES), F32)

    @pl.loop(0, GROUPS)
    def _(source):
        def finish(slot, values):
            for (here, there), value in zip(spots, values):
                total[slot, here, :] += value * spread(source, slot, there)

        sweep(
            SLOTS, lambda slot, span: gains[slot, span, :] * spread(source, slot, span),
            bands, finish,
        )

    near, far = folded(lambda slot: total[slot, 0:rows, :], lane_ids(rows))
    return (near + plane[0, 0:rows, :]) * scale, (far + plane[1, 0:rows, :]) * scale


def set_spread(loads, starts, rows, averages, spread):
    count = GROUPS * LOCAL
    deviation = 1.0 / math.sqrt(count - 1)
    lane = lane_ids(rows)
    for load, start in zip(loads, starts):
        span = slice(start, start + rows)

        @pl.loop(0, SLOTS)
        def _(slot):
            value = load(0, slot)
            for source in range(1, GROUPS):
                value = value + load(source, slot)
            averages[slot, span, :] = value

        near, far = folded(lambda slot: averages[slot, span, :], lane)

        def store_average(slot, value):
            averages[slot, span, :] = value

        spread_out(near / count, far / count, lane, store_average)

        @pl.loop(0, SLOTS)
        def _(slot):
            average = averages[slot, span, :]
            for source in range(GROUPS):
                spread[source, slot, span, :] = (load(source, slot) - average) * deviation


def block_ends(loads, starts, rows, block, ends):
    for load, start in zip(loads, starts):
        span = slice(start, start + rows)
        ends[0, span, :] = load(jnp.maximum(block - 1, 0), SLOTS - 1)
        ends[1, span, :] = load(jnp.minimum(block + 1, GROUPS - 1), SLOTS - 1)


def loads_of(got, rows, sides):
    def load_from(side):
        base = side * SLOTS * rows

        def load(source, slot):
            return got[source, pl.ds(base + slot * rows, rows), :]

        return load

    return [load_from(side) for side in range(sides)]


def with_margins(own, kind, block, ends, rows):
    lane = lane_ids(rows.stop - rows.start)
    back = LANES - SPARE - 2 * REACH * kind
    left_ends = jnp.where(block > 0, ends[0, rows, :], 0.0)
    right_ends = jnp.where(block < GROUPS - 1, ends[1, rows, :], 0.0)
    own = pltpu.roll(own, REACH, 1)
    near = jnp.where(lane < REACH, pltpu.roll(left_ends, back, 1), own)
    far = jnp.where(lane < REACH, own, pltpu.roll(right_ends, back, 1))
    return near, jnp.where(lane < 2 * REACH, far, 0.0)


EARLY = 16
EARLY_BAND = ((RIM, MID), (RIM + RADIUS, MID), (RIM + 2 * RADIUS, EARLY))


SPREAD_ROWS = GROUPS * SLOTS * MID
SHARED = SLOTS + 5


def handed_on(rows):
    spread = rows.at[pl.ds(0, SPREAD_ROWS)].reshape(GROUPS, SLOTS, MID, LANES)
    return spread, rows.at[pl.ds(SPREAD_ROWS, SHARED * TALL)].reshape(SHARED, TALL, LANES)


def early_kernel(
    place, offsets, weights, got, fields, handed,
    averages, gains, total, plane, ends, *copies,
):
    spread, shared = handed_on(handed)
    tile, block = place[0], place[1]
    lane = lane_ids(TALL)
    loads = loads_of(got, MID, 1)
    set_spread(loads, (0,), MID, averages, spread)

    row = lax.broadcasted_iota(jnp.int32, (TALL, LANES), 0) + (tile * ROWS - REACH)
    col = lane + (block * LANES - REACH)
    row_ok = (row >= 0) & (row < ROWS * 32)
    near_ok = row_ok & (col >= 0) & (col < COLS)
    far_ok = row_ok & (col + LANES < COLS)

    def store_inside(slot, value):
        shared[slot] = value

    spread_out(near_ok.astype(F32), far_ok.astype(F32), lane, store_inside)
    sweep, scale = localizer(offsets, weights, shared, copies)
    ends[...] = jnp.zeros(ends.shape, F32)
    block_ends(loads, (RIM,), MID, block, ends)
    near, far = with_margins(fields[0], 0, block, ends, slice(0, TALL))

    def at(source, slot, rows):
        return spread[source, slot, rows.start - RIM : rows.stop - RIM, :]

    near, far = applied(sweep, scale, near, far, (EARLY_BAND,), at, gains, total, plane)
    for part, value in enumerate((near, far)):
        shared[SLOTS, part * EARLY : (part + 1) * EARLY, :] = value
    shared[SLOTS, 2 * EARLY : TALL, :] = jnp.zeros((TALL - 2 * EARLY, LANES), F32)
    for kind in range(2):
        shared[SLOTS + 1 + kind] = ends[kind]
        shared[SLOTS + 3 + kind] = fields[kind]


RIM_BANDS = (
    ((0, MID), (RADIUS, EARLY), (2 * RADIUS, EARLY)),
    ((MID, MID), (TALL - RADIUS - EARLY, EARLY), (TALL - 2 * RADIUS - EARLY, EARLY)),
)
LAST_BAND = ((2 * RADIUS, 40), (3 * RADIUS, 40), (REACH, ROWS))


def analysis_kernel(
    place, offsets, weights, got, handed, increment, spread_copies,
    spread, averages, gains, total, plane, ends, *copies,
):
    spread_mid, shared = handed_on(handed)
    block = place[1]
    loads, starts = loads_of(got, RIM, 2), (0, TALL - RIM)
    set_spread(loads, starts, RIM, averages, spread)

    @pl.loop(0, SLOTS)
    def _(slot):
        for source in range(GROUPS):
            spread[source, slot, RIM : RIM + MID, :] = spread_mid[source, slot]

    def at(source, slot, rows):
        return spread[source, slot, rows, :]

    sweep, scale = localizer(offsets, weights, shared, copies)
    for kind in range(2):
        ends[kind] = shared[SLOTS + 1 + kind]
    block_ends(loads, starts, RIM, block, ends)
    rows = slice(0, TALL)
    near_v, far_v = with_margins(shared[SLOTS + 3], 0, block, ends, rows)
    near_w, far_w = with_margins(shared[SLOTS + 4], 1, block, ends, rows)

    values = applied(sweep, scale, near_v, far_v, RIM_BANDS, at, gains, total, plane)
    for part in range(2):
        plane[2 + part] = jnp.zeros((TALL, LANES), F32)
        low = 2 * RADIUS
        plane[2 + part, low : low + EARLY, :] = values[part][0:EARLY]
        plane[2 + part, TALL - low - EARLY : TALL - low, :] = values[part][EARLY : 2 * EARLY]
        plane[2 + part, RIM + low : RIM + low + EARLY, :] = shared[
            SLOTS, part * EARLY : (part + 1) * EARLY, :
        ]
    near = (STEP_SIZE * near_w) * plane[2] - (2.0 - STEP_SIZE) * near_v
    far = (STEP_SIZE * far_w) * plane[3] - (2.0 - STEP_SIZE) * far_v
    far = jnp.where(lane_ids(TALL) < 2 * REACH, far, 0.0)
    near, far = applied(sweep, scale, near, far, (LAST_BAND,), at, gains, total, plane)
    lane = lane_ids(ROWS)
    result = pltpu.roll(jnp.where(lane < REACH, far, near), LANES - REACH, 1) * -STEP_SIZE
    increment[...] = result
    for target in range(GROUPS):
        spread_copies[target] = result


def recentre_kernel(middle, upper, lower, increments, out):
    keep = (ROWS - MID) // 2
    for block in range(GROUPS):
        lanes = slice(block * LANES, (block + 1) * LANES)
        for member in range(LOCAL):
            out[member, 0:keep, lanes] = upper[member, block, 0:keep, :] + increments[block, 0:keep, :]
            out[member, keep : keep + MID, lanes] = (
                middle[member, block] + increments[block, keep : keep + MID, :]
            )
            out[member, keep + MID : ROWS, lanes] = (
                lower[member, block, 0:keep, :] + increments[block, keep + MID : ROWS, :]
            )


def on_vmem(count):
    return [pl.BlockSpec(memory_space=pltpu.VMEM)] * count


def in_hbm(count):
    return [pl.BlockSpec(memory_space=pltpu.HBM)] * count


def array(*shape):
    return jax.ShapeDtypeStruct(shape, F32)


def on_device(
    members, courant_x, courant_y, obs_cell, innovation, obs_weight, stencil_offsets, stencil_weights
):
    both = ("member", "grp")
    params = pltpu.CompilerParams(vmem_limit_bytes=VMEM)
    crowded = pltpu.CompilerParams(vmem_limit_bytes=ALL_VMEM)
    cost = pl.CostEstimate(flops=10_000_000, bytes_accessed=60_000_000, transcendentals=0)
    tiles = lax.axis_size("tile")
    keep = (ROWS - MID) // 2
    sems = pltpu.SemaphoreType.DMA

    def buffers(height, rows, spare):
        return [
            pltpu.VMEM((LOCAL, GROUPS + 2, height, LANES), F32),
            pltpu.VMEM((LOCAL, GROUPS + 2, height, LANES), F32),
            pltpu.VMEM((2, GROUPS, height, LANES), F32),
            pltpu.VMEM((5, GROUPS, height, LANES), F32),
            pltpu.VMEM((LOCAL, GROUPS + 2, rows, LANES), F32),
            pltpu.VMEM((LOCAL, GROUPS + 2, rows + spare, LANES), F32),
            pltpu.VMEM((GROUPS, SLOTS * rows, LANES), F32),
        ]

    dma = [sems((GROUPS,)), sems((2, GROUPS)), sems((GROUPS + 1,))]
    up, down, middle, send_mid, fields = pl.pallas_call(
        inner_kernel,
        out_shape=[
            array(GROUPS, HALO, LANES),
            array(GROUPS, HALO, LANES),
            array(LOCAL, GROUPS, MID, LANES),
            array(GROUPS, SLOTS * MID, LANES),
            array(2, ROWS, LANES),
        ],
        in_specs=in_hbm(6),
        out_specs=in_hbm(4) + on_vmem(1),
        scratch_shapes=buffers(HEIGHT, MID, 0)
        + [
            pltpu.VMEM((1, 1, 1024), jnp.int32),
            pltpu.VMEM((2, 1, 1, 1024), F32),
            pltpu.VMEM((GROUPS, HALO, LANES), F32),
            pltpu.VMEM((GROUPS, HALO, LANES), F32),
        ]
        + dma
        + [sems((3,))],
        compiler_params=crowded,
        cost_estimate=cost,
        name="inner",
    )(members, courant_x, courant_y, obs_cell, innovation, obs_weight)
    above = lax.ppermute(down, "tile", [(i, i + 1) for i in range(tiles - 1)])
    below = lax.ppermute(up, "tile", [(i + 1, i) for i in range(tiles - 1)])
    got_mid = exchanged(send_mid, both)
    upper, send_upper, rim_fields = pl.pallas_call(
        upper_kernel,
        out_shape=[
            array(LOCAL, GROUPS, 8, LANES),
            array(GROUPS, 2 * SIDE, LANES),
            array(2, RIM, LANES),
        ],
        in_specs=in_hbm(3) + on_vmem(2),
        out_specs=in_hbm(2) + on_vmem(1),
        scratch_shapes=buffers(SHORT, RIM, 4) + dma,
        compiler_params=crowded,
        cost_estimate=cost,
        name="upper",
    )(members, courant_x, courant_y, above, fields)
    lower, send_rim, fields_tall = pl.pallas_call(
        lower_kernel,
        out_shape=[
            array(LOCAL, GROUPS, 8, LANES),
            array(GROUPS, 2 * SIDE, LANES),
            array(2, TALL, LANES),
        ],
        in_specs=in_hbm(3) + on_vmem(3) + in_hbm(1),
        out_specs=in_hbm(2) + on_vmem(1),
        scratch_shapes=buffers(SHORT, RIM, 4) + [pltpu.VMEM((2, RIM, LANES), F32)] + dma,
        input_output_aliases={6: 1},
        compiler_params=crowded,
        cost_estimate=cost,
        name="lower",
    )(members, courant_x, courant_y, below, fields, rim_fields, send_upper)
    send_rim, got_mid = lax.optimization_barrier((send_rim, got_mid))
    got_rim = exchanged(send_rim, both)
    place = jnp.stack([lax.axis_index("tile"), lax.axis_index(both)]).astype(jnp.int32)
    tables = [pl.BlockSpec(memory_space=pltpu.SMEM)] * 3
    held = pltpu.VMEM((SLOTS, TALL, LANES), F32)
    work = [
        held, held, held, pltpu.VMEM((4, TALL, LANES), F32), pltpu.VMEM((2, TALL, LANES), F32)
    ]
    shifts = [pltpu.VMEM((2 * RADIUS + 1, DEEP, LANES), F32)] * (2 * COPIES)
    handed = pl.pallas_call(
        early_kernel,
        out_shape=array(SPREAD_ROWS + SHARED * TALL, LANES),
        in_specs=tables + on_vmem(2),
        out_specs=pl.BlockSpec(memory_space=pltpu.VMEM),
        scratch_shapes=work + shifts,
        compiler_params=params,
        cost_estimate=cost,
        name="early",
    )(place, stencil_offsets, stencil_weights, got_mid, fields_tall)
    increment, copies = pl.pallas_call(
        analysis_kernel,
        out_shape=[array(ROWS, LANES), array(GROUPS, ROWS, LANES)],
        in_specs=tables + on_vmem(2),
        out_specs=on_vmem(2),
        scratch_shapes=[pltpu.VMEM((GROUPS, SLOTS, TALL, LANES), F32)] + work + shifts,
        compiler_params=params,
        name="analysis",
    )(place, stencil_offsets, stencil_weights, got_rim, handed)
    increments = lax.all_to_all(copies, both, 0, 0, tiled=True)
    analysis = pl.pallas_call(
        recentre_kernel,
        out_shape=array(*members.shape),
        in_specs=on_vmem(4),
        out_specs=pl.BlockSpec(memory_space=pltpu.VMEM),
        compiler_params=params,
        name="recentre",
    )(middle, upper, lower, increments)
    return analysis, increment


def exchanged(blocks, axes):
    return lax.all_to_all(blocks, axes, 0, 0, tiled=True)


def solution(mesh):
    both = ("member", "grp")
    placed = (
        P(both, "tile", None),
        P("tile", None),
        P("tile", None),
        P("tile", both, None),
        P("tile", both, None),
        P("tile", both, None),
        P(),
        P(),
    )
    return jax.shard_map(
        on_device,
        mesh=mesh,
        in_specs=placed,
        out_specs=(P(both, "tile", None), P("tile", both)),
        check_vma=False,
    )
```

```python
import math

import jax
import jax.numpy as jnp
from jax import lax
from jax.experimental import pallas as pl
from jax.experimental.pallas import tpu as pltpu
from jax.sharding import PartitionSpec as P

F32 = jnp.float32
BF16 = jnp.bfloat16
RADIUS = 2
STEP_SIZE = 0.25
GROUPS = 8
LOCAL = 10
ROWS = 32
LANES = 128
COLS = 1024
REACH = 4 * RADIUS
EDGE = REACH + 3
TALL = ROWS + 2 * REACH
WIDE = LANES + 2 * REACH
SLOTS = 12
SPARE = LOCAL * WIDE - (SLOTS - 1) * LANES
HALO = 136
MID = 24
RIM = (TALL - MID) // 2
VMEM = 16 * 1024 * 1024
ALL_VMEM = 60 * 1024 * 1024


def lane_ids(rows):
    return lax.broadcasted_iota(jnp.int32, (rows, LANES), 1)


def pieces(value, count):
    found = []
    for _ in range(count):
        part = value.astype(BF16)
        found.append(part)
        value = value - part.astype(F32)
    return found


def set_coefs(courants, coefs, rows):
    @pl.loop(0, GROUPS)
    def _(block):
        for low in rows:
            span = slice(low, low + 8)
            cx = courants[0, block, span, :]
            cy = courants[1, block, span, :]
            x_plus, x_minus = jnp.maximum(cx, 0.0), jnp.minimum(cx, 0.0)
            y_plus, y_minus = jnp.maximum(cy, 0.0), jnp.minimum(cy, 0.0)
            coefs[0, block, span, :] = 1.0 - x_plus + x_minus - y_plus + y_minus
            coefs[1, block, span, :] = x_plus
            coefs[2, block, span, :] = -x_minus
            coefs[3, block, span, :] = y_plus
            coefs[4, block, span, :] = -y_minus


def clear_sides(buffers):
    for buffer in buffers:
        nothing = jnp.zeros(buffer.shape[2:], F32)
        for member in range(LOCAL):
            for side in (0, GROUPS + 1):
                buffer[member, side] = nothing


def advance(source, target, coefs, starts, homes=None):
    homes = starts if homes is None else homes
    lane = lane_ids(8)
    first, last = lane == 0, lane == LANES - 1

    @pl.loop(0, GROUPS, unroll=8)
    def _(block):
        for low, home in zip(starts, homes):
            rows = slice(low, low + 8)
            k_mid, k_up, k_down, k_left, k_right = (coefs[kind, block, rows, :] for kind in range(5))
            for member in range(LOCAL):
                mid = source[member, block + 1, rows, :]
                before = source[member, block, rows, :]
                after = source[member, block + 2, rows, :]
                target[member, block + 1, home : home + 8, :] = (
                    k_mid * mid
                    + k_up * source[member, block + 1, low - 1 : low + 7, :]
                    + k_down * source[member, block + 1, low + 1 : low + 9, :]
                    + k_left * pltpu.roll(jnp.where(last, before, mid), 1, 1)
                    + k_right * pltpu.roll(jnp.where(first, after, mid), LANES - 1, 1)
                )


def send_plan():
    plan = [[] for _ in range(SLOTS)]
    for member in range(LOCAL):
        start = member * WIDE
        spans = (
            (start, start + REACH, -1),
            (start + REACH, start + REACH + LANES, 0),
            (start + REACH + LANES, start + WIDE, 1),
        )
        for low, high, offset in spans:
            while low < high:
                slot = low // LANES
                stop = min(high, (slot + 1) * LANES)
                plan[slot].append((member, offset, low - slot * LANES, stop - slot * LANES))
                low = stop
    return plan


def pack(final, fields, rows, rolled, blocks, send, sems):
    @pl.loop(0, GROUPS, unroll=8)
    def _(block):
        for member in range(LOCAL):
            shift = (member * WIDE + REACH) % LANES
            value = final[member, block + 1, 0:rows, :]
            rolled[member, block + 1] = pltpu.roll(value, shift, 1) if shift else value

    lane = lane_ids(rows)
    ends = jnp.where(
        lane < SPARE + 2 * REACH,
        pltpu.roll(fields[0], SPARE + REACH, 1),
        pltpu.roll(fields[1], SPARE + 3 * REACH, 1),
    )
    plan = send_plan()

    @pl.loop(0, GROUPS)
    def _(block):
        for slot in range(SLOTS):
            value = ends if slot == SLOTS - 1 else None
            for member, offset, low, high in plan[slot]:
                part = rolled[member, block + 1 + offset]
                if value is None:
                    value = part
                else:
                    value = jnp.where((lane >= low) & (lane < high), part, value)
            blocks[block, slot * rows : (slot + 1) * rows, :] = value
        pltpu.make_async_copy(blocks.at[block], send(block), sems.at[block]).start()


def finish_pack(blocks, send, sems):
    for block in range(GROUPS):
        pltpu.make_async_copy(blocks.at[block], send(block), sems.at[block]).wait()


def observed(cells, values, fields):
    row_hit = lax.broadcasted_iota(jnp.int32, (ROWS, 1024), 0) == lax.shift_right_logical(cells[0], 7)
    col_hit = lax.broadcasted_iota(jnp.int32, (LANES, 1024), 0) == lax.bitwise_and(
        cells[0], LANES - 1
    )
    parts = pieces(values[1, 0] * values[0, 0], 3) + pieces(values[1, 0], 3)
    hits = row_hit.astype(F32)
    left = jnp.concatenate([(hits * part.astype(F32)).astype(BF16) for part in parts], axis=0)
    sums = lax.dot_general(
        left, col_hit.astype(F32).astype(BF16), (((1,), (1,)), ((), ())), preferred_element_type=F32
    )
    for kind in range(2):
        base = 3 * ROWS * kind
        fields[kind] = (
            sums[base : base + ROWS]
            + sums[base + ROWS : base + 2 * ROWS]
            + sums[base + 2 * ROWS : base + 3 * ROWS]
        )


def set_messages(members, courants, fields, up, down):
    @pl.loop(0, GROUPS)
    def _(block):
        for field in range(LOCAL + 2):
            span = slice(field * EDGE, (field + 1) * EDGE)
            for target, low in ((up, TOP), (down, TOP + ROWS - EDGE)):
                rows = slice(low, low + EDGE)
                if field < LOCAL:
                    target[block, span, :] = members[field, block + 1, rows, :]
                else:
                    target[block, span, :] = courants[field - LOCAL, block, rows, :]

    base = (LOCAL + 2) * EDGE
    for row in range(REACH):
        for kind in range(2):
            up[row, base + kind : base + kind + 1, :] = fields[kind, row : row + 1, :]
            down[row, base + kind : base + kind + 1, :] = fields[
                kind, ROWS - REACH + row : ROWS - REACH + row + 1, :
            ]
        up[row, base + 2 : HALO, :] = jnp.zeros((HALO - base - 2, LANES), F32)
        down[row, base + 2 : HALO, :] = jnp.zeros((HALO - base - 2, LANES), F32)


TOP = 16
HEIGHT = 56


def inner_kernel(
    members, courant_x, courant_y, cell, innov, weight, up_out, down_out, out, send, fields,
    old, new, courants, coefs, rolled, final, blocks, cells, values, up, down,
    member_sems, wind_sems, sems, small_sems,
):
    own = slice(TOP, TOP + ROWS)
    large, wind = [], []
    for block in range(GROUPS):
        lanes = slice(block * LANES, (block + 1) * LANES)
        for kind, source in enumerate((courant_x, courant_y)):
            wind.append(
                pltpu.make_async_copy(
                    source.at[:, lanes], courants.at[kind, block, own, :], wind_sems.at[kind, block]
                )
            )
        large.append(
            pltpu.make_async_copy(
                members.at[:, :, lanes], old.at[:, block + 1, own, :], member_sems.at[block]
            )
        )
    small = [
        pltpu.make_async_copy(cell, cells, small_sems.at[0]),
        pltpu.make_async_copy(innov, values.at[0], small_sems.at[1]),
        pltpu.make_async_copy(weight, values.at[1], small_sems.at[2]),
    ]
    for copy in small + wind + large:
        copy.start()
    clear_sides((old, new, rolled))
    for copy in small:
        copy.wait()
    observed(cells, values, fields)
    for copy in wind:
        copy.wait()
    set_coefs(courants, coefs, range(TOP, TOP + ROWS, 8))
    for copy in large:
        copy.wait()
    set_messages(old, courants, fields, up, down)
    messages = [
        pltpu.make_async_copy(up, up_out, small_sems.at[0]),
        pltpu.make_async_copy(down, down_out, small_sems.at[1]),
    ]
    for copy in messages:
        copy.start()
    advance(old, new, coefs, range(TOP, TOP + ROWS, 8))
    advance(new, old, coefs, range(TOP, TOP + ROWS, 8))
    skip = (ROWS - MID) // 2
    advance(old, final, coefs, range(TOP + skip, TOP + skip + MID, 8), range(0, MID, 8))
    whole = pltpu.make_async_copy(final.at[:, pl.ds(1, GROUPS), pl.ds(0, MID), :], out, sems.at[GROUPS])
    whole.start()
    middle = [fields[kind, skip : skip + MID, :] for kind in range(2)]
    pack(final, middle, MID, rolled, blocks, lambda block: send.at[block], sems)
    finish_pack(blocks, lambda block: send.at[block], sems)
    for copy in messages + [whole]:
        copy.wait()


SIDE = SLOTS * RIM
SHORT = 32


def rim_rows(
    lower, members, courant_x, courant_y, message, fields, out, send,
    old, new, courants, coefs, rolled, final, blocks, rim, member_sems, wind_sems, sems,
):
    own = slice(0, 8) if lower else slice(TOP, TOP + 8)
    rows = slice(ROWS - 8, ROWS) if lower else slice(0, 8)
    beside = 8 if lower else TOP - EDGE
    copies = []
    for block in range(GROUPS):
        lanes = slice(block * LANES, (block + 1) * LANES)
        copies.append(
            pltpu.make_async_copy(
                members.at[:, rows, lanes], old.at[:, block + 1, own, :], member_sems.at[block]
            )
        )
        for kind, source in enumerate((courant_x, courant_y)):
            copies.append(
                pltpu.make_async_copy(
                    source.at[rows, lanes], courants.at[kind, block, own, :],
                    wind_sems.at[kind, block],
                )
            )
    for copy in copies:
        copy.start()
    clear_sides((old, new, rolled))

    @pl.loop(0, GROUPS)
    def _(block):
        for field in range(LOCAL + 2):
            value = message[block, field * EDGE : (field + 1) * EDGE, :]
            if field < LOCAL:
                old[field, block + 1, beside : beside + EDGE, :] = value
            else:
                courants[field - LOCAL, block, beside : beside + EDGE, :] = value

    base, keep = (LOCAL + 2) * EDGE, RIM - REACH
    for kind in range(2):
        for row in range(REACH):
            at = row + (keep if lower else 0)
            rim[kind, at : at + 1, :] = message[row, base + kind : base + kind + 1, :]
        if lower:
            rim[kind, 0:keep, :] = fields[kind, ROWS - keep : ROWS, :]
        else:
            rim[kind, REACH:RIM, :] = fields[kind, 0:keep, :]
    for copy in copies:
        copy.wait()
    set_coefs(courants, coefs, range(0, SHORT, 8))
    first = 2 if lower else TOP - EDGE + 1
    advance(old, new, coefs, (first, first + 8))
    advance(new, old, coefs, (first + 1, first + 9))
    advance(old, final, coefs, (first + 2, first + 10), (0, 8))
    low = 0 if lower else REACH
    whole = pltpu.make_async_copy(
        final.at[:, pl.ds(1, GROUPS), pl.ds(low, 8), :], out, sems.at[GROUPS]
    )
    whole.start()

    def place(block):
        return send.at[block, pl.ds(SIDE if lower else 0, SIDE), :]

    pack(final, rim, RIM, rolled, blocks, place, sems)
    finish_pack(blocks, place, sems)
    whole.wait()


def upper_kernel(members, courant_x, courant_y, above, fields, out, send, rim, *rest):
    work, sems = rest[:-3], rest[-3:]
    rim_rows(
        False, members, courant_x, courant_y, above, fields, out, send, *work, rim, *sems
    )


def lower_kernel(
    members, courant_x, courant_y, below, fields, upper, sent, out, send, fields_tall, *rest
):
    del sent
    work, rim, sems = rest[:-4], rest[-4], rest[-3:]
    rim_rows(
        True, members, courant_x, courant_y, below, fields, out, send, *work, rim, *sems
    )
    for kind in range(2):
        fields_tall[kind, 0:RIM, :] = upper[kind]
        fields_tall[kind, REACH : REACH + ROWS, :] = fields[kind]
        fields_tall[kind, TALL - RIM : TALL, :] = rim[kind]


COPIES = 4
DEEP = 56


def member_place(member):
    return member * WIDE // LANES, member * WIDE % LANES


def folded(slots, lane):
    near, far = None, None
    for member in range(LOCAL):
        base, shift = member_place(member)
        here, there = slots(base), slots(base + 1)
        if shift:
            here = pltpu.roll(jnp.where(lane >= shift, here, there), LANES - shift, 1)
            there = pltpu.roll(there, LANES - shift, 1)
        near = here if near is None else near + here
        far = there if far is None else far + there
    return near, far


def spread_out(near, far, lane, store):
    slots = [None] * SLOTS
    for member in range(LOCAL):
        base, shift = member_place(member)
        moved = pltpu.roll(near, shift, 1) if shift else near
        tail = pltpu.roll(far, shift, 1) if shift else far
        slots[base] = moved if slots[base] is None else jnp.where(lane >= shift, moved, slots[base])
        slots[base + 1] = jnp.where(
            lane < shift, moved, jnp.where(lane < shift + 2 * REACH, tail, 0.0)
        )
    for slot in range(SLOTS):
        store(slot, slots[slot])


def shifted(before, mid, after, lane):
    found = {0: mid}
    for shift in (1, 2):
        found[shift] = pltpu.roll(jnp.where(lane < shift, after, mid), LANES - shift, 1)
        found[-shift] = pltpu.roll(jnp.where(lane >= LANES - shift, before, mid), shift, 1)
    return found


def put(target, span, found):
    for shift, value in found.items():
        target[RADIUS + shift, span, :] = value


def localizer(offsets, weights, inside, copies):
    entries = offsets.shape[0]
    tap_row = [offsets[entry, 0] for entry in range(entries)]
    tap_col = [offsets[entry, 1] for entry in range(entries)]
    tap = [weights[entry] for entry in range(entries)]
    weight_sum = tap[0]
    for entry in range(1, entries):
        weight_sum = weight_sum + tap[entry]
    scale = 1.0 / jnp.full((1, LANES), weight_sum, F32)
    first_copies, second_copies = copies[: len(copies) // 2], copies[len(copies) // 2 :]

    def taps(source, sign, low, rows):
        value = None
        for entry in range(entries):
            term = tap[entry] * source[
                RADIUS + sign * tap_col[entry], pl.ds(low + sign * tap_row[entry], rows), :
            ]
            value = term if value is None else value + term
        return value

    def sweep(slots, multiplier, bands, finish):
        def copies_of(held, slot):
            found = []
            for at, mid in enumerate(held[slot]):
                before = held.get(slot - 1, held[slot])[at]
                after = held.get(slot + 1, held[slot])[at]
                found.append(shifted(before, mid, after, lane_ids(mid.shape[0])))
            return found

        def put_all(target, found, kind):
            for band, values in zip(bands, found):
                low, rows = band[kind]
                put(target, slice(low, low + rows), values)

        def entering(slot):
            return [multiplier(slot, slice(band[0][0], sum(band[0]))) for band in bands]

        products, localized = {0: entering(0), 1: entering(1)}, {}
        put_all(first_copies[0], copies_of(products, 0), 0)
        for slot in range(slots + 3):
            if slot + 1 < slots:
                if slot + 2 < slots:
                    products[slot + 2] = entering(slot + 2)
                ahead = copies_of(products, slot + 1)
            if slot < slots:
                localized[slot] = [
                    taps(first_copies[slot % COPIES], -1, *band[1])
                    * inside[slot, band[1][0] : sum(band[1]), :]
                    for band in bands
                ]
            if slot + 1 < slots:
                put_all(first_copies[(slot + 1) % COPIES], ahead, 0)
            if 1 < slot < slots + 2:
                behind = copies_of(localized, slot - 2)
            if slot > 2:
                done = slot - 3
                finish(done, [taps(second_copies[done % COPIES], 1, *band[2]) for band in bands])
            if 1 < slot < slots + 2:
                put_all(second_copies[(slot - 2) % COPIES], behind, 1)

    return sweep, scale * scale


def applied(sweep, scale, near, far, bands, spread, gains, total, plane):
    spots, rows = [], 0
    for band in bands:
        spots.append((slice(rows, rows + band[2][1]), slice(band[2][0], sum(band[2]))))
        rows += band[2][1]

    def store_gain(slot, value):
        gains[slot] = value

    spread_out(near, far, lane_ids(near.shape[0]), store_gain)

    def finish_ones(slot, values):
        for (here, _), value in zip(spots, values):
            plane[slot, here, :] = value

    sweep(2, lambda slot, span: gains[slot, span, :], bands, finish_ones)

    @pl.loop(0, SLOTS)
    def _(slot):
        total[slot, 0:rows, :] = jnp.zeros((rows, LANES), F32)

    @pl.loop(0, GROUPS)
    def _(source):
        def finish(slot, values):
            for (here, there), value in zip(spots, values):
                total[slot, here, :] += value * spread(source, slot, there)

        sweep(
            SLOTS, lambda slot, span: gains[slot, span, :] * spread(source, slot, span),
            bands, finish,
        )

    near, far = folded(lambda slot: total[slot, 0:rows, :], lane_ids(rows))
    return (near + plane[0, 0:rows, :]) * scale, (far + plane[1, 0:rows, :]) * scale


def set_spread(loads, starts, rows, averages, spread):
    count = GROUPS * LOCAL
    deviation = 1.0 / math.sqrt(count - 1)
    lane = lane_ids(rows)
    for load, start in zip(loads, starts):
        span = slice(start, start + rows)

        @pl.loop(0, SLOTS)
        def _(slot):
            value = load(0, slot)
            for source in range(1, GROUPS):
                value = value + load(source, slot)
            averages[slot, span, :] = value

        near, far = folded(lambda slot: averages[slot, span, :], lane)

        def store_average(slot, value):
            averages[slot, span, :] = value

        spread_out(near / count, far / count, lane, store_average)

        @pl.loop(0, SLOTS)
        def _(slot):
            average = averages[slot, span, :]
            for source in range(GROUPS):
                spread[source, slot, span, :] = (load(source, slot) - average) * deviation


def block_ends(loads, starts, rows, block, ends):
    for load, start in zip(loads, starts):
        span = slice(start, start + rows)
        ends[0, span, :] = load(jnp.maximum(block - 1, 0), SLOTS - 1)
        ends[1, span, :] = load(jnp.minimum(block + 1, GROUPS - 1), SLOTS - 1)


def loads_of(got, rows, sides):
    def load_from(side):
        base = side * SLOTS * rows

        def load(source, slot):
            return got[source, pl.ds(base + slot * rows, rows), :]

        return load

    return [load_from(side) for side in range(sides)]


def with_margins(own, kind, block, ends, rows):
    lane = lane_ids(rows.stop - rows.start)
    back = LANES - SPARE - 2 * REACH * kind
    left_ends = jnp.where(block > 0, ends[0, rows, :], 0.0)
    right_ends = jnp.where(block < GROUPS - 1, ends[1, rows, :], 0.0)
    own = pltpu.roll(own, REACH, 1)
    near = jnp.where(lane < REACH, pltpu.roll(left_ends, back, 1), own)
    far = jnp.where(lane < REACH, own, pltpu.roll(right_ends, back, 1))
    return near, jnp.where(lane < 2 * REACH, far, 0.0)


EARLY = 16
EARLY_BAND = ((RIM, MID), (RIM + RADIUS, MID), (RIM + 2 * RADIUS, EARLY))


SPREAD_ROWS = GROUPS * SLOTS * MID
SHARED = SLOTS + 5


def handed_on(rows):
    spread = rows.at[pl.ds(0, SPREAD_ROWS)].reshape(GROUPS, SLOTS, MID, LANES)
    return spread, rows.at[pl.ds(SPREAD_ROWS, SHARED * TALL)].reshape(SHARED, TALL, LANES)


def early_kernel(
    place, offsets, weights, got, fields, handed,
    averages, gains, total, plane, ends, *copies,
):
    spread, shared = handed_on(handed)
    tile, block = place[0], place[1]
    lane = lane_ids(TALL)
    loads = loads_of(got, MID, 1)
    set_spread(loads, (0,), MID, averages, spread)

    row = lax.broadcasted_iota(jnp.int32, (TALL, LANES), 0) + (tile * ROWS - REACH)
    col = lane + (block * LANES - REACH)
    row_ok = (row >= 0) & (row < ROWS * 32)
    near_ok = row_ok & (col >= 0) & (col < COLS)
    far_ok = row_ok & (col + LANES < COLS)

    def store_inside(slot, value):
        shared[slot] = value

    spread_out(near_ok.astype(F32), far_ok.astype(F32), lane, store_inside)
    sweep, scale = localizer(offsets, weights, shared, copies)
    ends[...] = jnp.zeros(ends.shape, F32)
    block_ends(loads, (RIM,), MID, block, ends)
    near, far = with_margins(fields[0], 0, block, ends, slice(0, TALL))

    def at(source, slot, rows):
        return spread[source, slot, rows.start - RIM : rows.stop - RIM, :]

    near, far = applied(sweep, scale, near, far, (EARLY_BAND,), at, gains, total, plane)
    for part, value in enumerate((near, far)):
        shared[SLOTS, part * EARLY : (part + 1) * EARLY, :] = value
    shared[SLOTS, 2 * EARLY : TALL, :] = jnp.zeros((TALL - 2 * EARLY, LANES), F32)
    for kind in range(2):
        shared[SLOTS + 1 + kind] = ends[kind]
        shared[SLOTS + 3 + kind] = fields[kind]


RIM_BANDS = (
    ((0, MID), (RADIUS, EARLY), (2 * RADIUS, EARLY)),
    ((MID, MID), (TALL - RADIUS - EARLY, EARLY), (TALL - 2 * RADIUS - EARLY, EARLY)),
)
LAST_BAND = ((2 * RADIUS, 40), (3 * RADIUS, 40), (REACH, ROWS))


def analysis_kernel(
    place, offsets, weights, got, handed, increment, spread_copies,
    spread, averages, gains, total, plane, ends, *copies,
):
    spread_mid, shared = handed_on(handed)
    block = place[1]
    loads, starts = loads_of(got, RIM, 2), (0, TALL - RIM)
    set_spread(loads, starts, RIM, averages, spread)

    @pl.loop(0, SLOTS)
    def _(slot):
        for source in range(GROUPS):
            spread[source, slot, RIM : RIM + MID, :] = spread_mid[source, slot]

    def at(source, slot, rows):
        return spread[source, slot, rows, :]

    sweep, scale = localizer(offsets, weights, shared, copies)
    for kind in range(2):
        ends[kind] = shared[SLOTS + 1 + kind]
    block_ends(loads, starts, RIM, block, ends)
    rows = slice(0, TALL)
    near_v, far_v = with_margins(shared[SLOTS + 3], 0, block, ends, rows)
    near_w, far_w = with_margins(shared[SLOTS + 4], 1, block, ends, rows)

    values = applied(sweep, scale, near_v, far_v, RIM_BANDS, at, gains, total, plane)
    for part in range(2):
        plane[2 + part] = jnp.zeros((TALL, LANES), F32)
        low = 2 * RADIUS
        plane[2 + part, low : low + EARLY, :] = values[part][0:EARLY]
        plane[2 + part, TALL - low - EARLY : TALL - low, :] = values[part][EARLY : 2 * EARLY]
        plane[2 + part, RIM + low : RIM + low + EARLY, :] = shared[
            SLOTS, part * EARLY : (part + 1) * EARLY, :
        ]
    near = (STEP_SIZE * near_w) * plane[2] - (2.0 - STEP_SIZE) * near_v
    far = (STEP_SIZE * far_w) * plane[3] - (2.0 - STEP_SIZE) * far_v
    far = jnp.where(lane_ids(TALL) < 2 * REACH, far, 0.0)
    near, far = applied(sweep, scale, near, far, (LAST_BAND,), at, gains, total, plane)
    lane = lane_ids(ROWS)
    result = pltpu.roll(jnp.where(lane < REACH, far, near), LANES - REACH, 1) * -STEP_SIZE
    increment[...] = result
    for target in range(GROUPS):
        spread_copies[target] = result


def recentre_kernel(middle, upper, lower, increments, out):
    keep = (ROWS - MID) // 2
    for block in range(GROUPS):
        lanes = slice(block * LANES, (block + 1) * LANES)
        for member in range(LOCAL):
            out[member, 0:keep, lanes] = upper[member, block, 0:keep, :] + increments[block, 0:keep, :]
            out[member, keep : keep + MID, lanes] = (
                middle[member, block] + increments[block, keep : keep + MID, :]
            )
            out[member, keep + MID : ROWS, lanes] = (
                lower[member, block, 0:keep, :] + increments[block, keep + MID : ROWS, :]
            )


def on_vmem(count):
    return [pl.BlockSpec(memory_space=pltpu.VMEM)] * count


def in_hbm(count):
    return [pl.BlockSpec(memory_space=pltpu.HBM)] * count


def array(*shape):
    return jax.ShapeDtypeStruct(shape, F32)


def on_device(
    members, courant_x, courant_y, obs_cell, innovation, obs_weight, stencil_offsets, stencil_weights
):
    both = ("member", "grp")
    params = pltpu.CompilerParams(vmem_limit_bytes=VMEM)
    crowded = pltpu.CompilerParams(vmem_limit_bytes=ALL_VMEM)
    cost = pl.CostEstimate(flops=10_000_000, bytes_accessed=60_000_000, transcendentals=0)
    tiles = lax.axis_size("tile")
    keep = (ROWS - MID) // 2
    sems = pltpu.SemaphoreType.DMA

    def buffers(height, rows, spare):
        return [
            pltpu.VMEM((LOCAL, GROUPS + 2, height, LANES), F32),
            pltpu.VMEM((LOCAL, GROUPS + 2, height, LANES), F32),
            pltpu.VMEM((2, GROUPS, height, LANES), F32),
            pltpu.VMEM((5, GROUPS, height, LANES), F32),
            pltpu.VMEM((LOCAL, GROUPS + 2, rows, LANES), F32),
            pltpu.VMEM((LOCAL, GROUPS + 2, rows + spare, LANES), F32),
            pltpu.VMEM((GROUPS, SLOTS * rows, LANES), F32),
        ]

    dma = [sems((GROUPS,)), sems((2, GROUPS)), sems((GROUPS + 1,))]
    up, down, middle, send_mid, fields = pl.pallas_call(
        inner_kernel,
        out_shape=[
            array(GROUPS, HALO, LANES),
            array(GROUPS, HALO, LANES),
            array(LOCAL, GROUPS, MID, LANES),
            array(GROUPS, SLOTS * MID, LANES),
            array(2, ROWS, LANES),
        ],
        in_specs=in_hbm(6),
        out_specs=in_hbm(4) + on_vmem(1),
        scratch_shapes=buffers(HEIGHT, MID, 0)
        + [
            pltpu.VMEM((1, 1, 1024), jnp.int32),
            pltpu.VMEM((2, 1, 1, 1024), F32),
            pltpu.VMEM((GROUPS, HALO, LANES), F32),
            pltpu.VMEM((GROUPS, HALO, LANES), F32),
        ]
        + dma
        + [sems((3,))],
        compiler_params=crowded,
        cost_estimate=cost,
        name="inner",
    )(members, courant_x, courant_y, obs_cell, innovation, obs_weight)
    above = lax.ppermute(down, "tile", [(i, i + 1) for i in range(tiles - 1)])
    below = lax.ppermute(up, "tile", [(i + 1, i) for i in range(tiles - 1)])
    got_mid = exchanged(send_mid, both)
    upper, send_upper, rim_fields = pl.pallas_call(
        upper_kernel,
        out_shape=[
            array(LOCAL, GROUPS, 8, LANES),
            array(GROUPS, 2 * SIDE, LANES),
            array(2, RIM, LANES),
        ],
        in_specs=in_hbm(3) + on_vmem(2),
        out_specs=in_hbm(2) + on_vmem(1),
        scratch_shapes=buffers(SHORT, RIM, 4) + dma,
        compiler_params=crowded,
        cost_estimate=cost,
        name="upper",
    )(members, courant_x, courant_y, above, fields)
    lower, send_rim, fields_tall = pl.pallas_call(
        lower_kernel,
        out_shape=[
            array(LOCAL, GROUPS, 8, LANES),
            array(GROUPS, 2 * SIDE, LANES),
            array(2, TALL, LANES),
        ],
        in_specs=in_hbm(3) + on_vmem(3) + in_hbm(1),
        out_specs=in_hbm(2) + on_vmem(1),
        scratch_shapes=buffers(SHORT, RIM, 4) + [pltpu.VMEM((2, RIM, LANES), F32)] + dma,
        input_output_aliases={6: 1},
        compiler_params=crowded,
        cost_estimate=cost,
        name="lower",
    )(members, courant_x, courant_y, below, fields, rim_fields, send_upper)
    send_rim, got_mid = lax.optimization_barrier((send_rim, got_mid))
    got_rim = exchanged(send_rim, both)
    place = jnp.stack([lax.axis_index("tile"), lax.axis_index(both)]).astype(jnp.int32)
    tables = [pl.BlockSpec(memory_space=pltpu.SMEM)] * 3
    held = pltpu.VMEM((SLOTS, TALL, LANES), F32)
    work = [
        held, held, held, pltpu.VMEM((4, TALL, LANES), F32), pltpu.VMEM((2, TALL, LANES), F32)
    ]
    shifts = [pltpu.VMEM((2 * RADIUS + 1, DEEP, LANES), F32)] * (2 * COPIES)
    handed = pl.pallas_call(
        early_kernel,
        out_shape=array(SPREAD_ROWS + SHARED * TALL, LANES),
        in_specs=tables + on_vmem(2),
        out_specs=pl.BlockSpec(memory_space=pltpu.VMEM),
        scratch_shapes=work + shifts,
        compiler_params=params,
        cost_estimate=cost,
        name="early",
    )(place, stencil_offsets, stencil_weights, got_mid, fields_tall)
    increment, copies = pl.pallas_call(
        analysis_kernel,
        out_shape=[array(ROWS, LANES), array(GROUPS, ROWS, LANES)],
        in_specs=tables + on_vmem(2),
        out_specs=on_vmem(2),
        scratch_shapes=[pltpu.VMEM((GROUPS, SLOTS, TALL, LANES), F32)] + work + shifts,
        compiler_params=params,
        name="analysis",
    )(place, stencil_offsets, stencil_weights, got_rim, handed)
    increments = lax.all_to_all(copies, both, 0, 0, tiled=True)
    analysis = pl.pallas_call(
        recentre_kernel,
        out_shape=array(*members.shape),
        in_specs=on_vmem(4),
        out_specs=pl.BlockSpec(memory_space=pltpu.VMEM),
        compiler_params=params,
        name="recentre",
    )(middle, upper, lower, increments)
    return analysis, increment


def exchanged(blocks, axes):
    return lax.all_to_all(blocks, axes, 0, 0, tiled=True)


def solution(mesh):
    both = ("member", "grp")
    placed = (
        P(both, "tile", None),
        P("tile", None),
        P("tile", None),
        P("tile", both, None),
        P("tile", both, None),
        P("tile", both, None),
        P(),
        P(),
    )
    return jax.shard_map(
        on_device,
        mesh=mesh,
        in_specs=placed,
        out_specs=(P(both, "tile", None), P("tile", both)),
        check_vma=False,
    )
```
